128 devices in a mesh: head: 4 (over y), seq: 32 (over x, z, core).
Axes of the slice: x: 4, y: 4, z: 4, core: 2. Of those that a mesh axis runs over, the one named last changes fastest.
Arguments:
- prompts: bfloat16 [64, 256, 4096], P('seq'), may hold values from -6 to 6
- prompt_len: int32 [64], replicated, may hold values from 32 to 256, as said below
- admitted: int32 [4], replicated, may hold values from -1 to 63, as said below
- cache_len: int32 [4], replicated, may hold values from 1024 to 16384, as said below
- cache_kv: bfloat16 [4, 4, 16384, 256], P('head', None, 'seq'), may hold values from -12 to 12
- dec_tokens: bfloat16 [4, 4, 4096], replicated, may hold values from -6 to 6
- w_query: bfloat16 [4096, 4096], P(None, 'head'), may hold values from -0.09375 to 0.09375
- w_key: bfloat16 [4096, 512], P(None, 'head'), may hold values from -0.09375 to 0.09375
- w_value: bfloat16 [4096, 512], P(None, 'head'), may hold values from -0.09375 to 0.09375
- w_out: bfloat16 [4096, 4096], P('head'), may hold values from -0.09375 to 0.09375
- q_gain: float32 [128], replicated, may hold values from 0.25 to 16
- k_gain: float32 [128], replicated, may hold values from 0.25 to 16
Outputs:
- prefill_out: bfloat16 [64, 256, 4096], P('seq', None, 'head')
- handed_kv: bfloat16 [4, 64, 256, 256], P('head', None, 'seq')
- decode_out: bfloat16 [4, 4, 4096], P(None, None, 'head')
The draws below stay inside these ranges and needn't reach their ends.
Inputs may be any that keep to these rules, and one draw needn't show every extreme that they name: `prompt_len`: some prompt has exactly 256 live tokens. `admitted`: slots with an entry of 0 or more name distinct prompts; in every draw some slot keeps its cache and some slot takes prompt 64 - 1. `cache_len`: some slot has exactly 16384 live positions.
All inputs are finite; a program needn't handle non-finite values.
Results may differ from the reference program's by a relative error of at most 0.02.
The reference program's roundings to bfloat16 on the way count: a program that leaves them out, or rounds other values in their place, can miss the bound.
Values may be sent and summed in bfloat16 or wider, within the bound.
A program may use at most 128 MiB of HBM per device.

```python
import jax
import jax.numpy as jnp
from jax import lax

D = 4096
HQ = 32
KVH = 4
HD = 128
LP = 256
SLOTS = 4
CACHE_DEV = 512
STEPS = 4
PROMPTS = 64
CACHE_LEN = 16384
N_HEAD = 4
N_SEQ = 32


def draw_prompt_len(key, part):
    key = jax.random.fold_in(key, 11)
    first, second = jax.random.split(key)
    values = jax.random.randint(first, (PROMPTS,), max(1, LP // 8), LP + 1, dtype=jnp.int32)
    where = jax.random.randint(second, (), 0, PROMPTS, dtype=jnp.int32)
    return values.at[where].set(LP)


def draw_admitted(key, part):
    key = jax.random.fold_in(key, 13)
    first, second, third = jax.random.split(key, 3)
    order = jax.random.permutation(first, SLOTS).astype(jnp.int32)
    rank = jnp.argsort(order, stable=True).astype(jnp.int32)
    chosen = jax.random.permutation(second, PROMPTS - 1)[:SLOTS].astype(jnp.int32)
    chosen = jnp.where(rank == 1, PROMPTS - 1, chosen).astype(jnp.int32)
    coin = jax.random.randint(third, (SLOTS,), 0, 2, dtype=jnp.int32)
    taken = jnp.where(rank == 0, 0, jnp.where(rank == 1, 1, coin))
    return jnp.where(taken == 1, chosen, -1).astype(jnp.int32)


def draw_cache_len(key, part):
    key = jax.random.fold_in(key, 17)
    first, second = jax.random.split(key)
    values = jax.random.randint(first, (SLOTS,), max(1, CACHE_LEN // 16), CACHE_LEN + 1, dtype=jnp.int32)
    where = jax.random.randint(second, (), 0, SLOTS, dtype=jnp.int32)
    return values.at[where].set(CACHE_LEN)


def draw_cache_kv(key, part):
    key = jax.random.fold_in(key, 19)
    shape = (KVH, SLOTS, CACHE_LEN, 2 * HD)
    values = jax.random.normal(key, shape, jnp.float32)
    return jnp.clip(values, -12.0, 12.0).astype(jnp.bfloat16)


def draw_q_gain(key, part):
    key = jax.random.fold_in(key, 23)
    values = jax.random.uniform(key, (HD,), jnp.float32, 0.6, 1.6)
    return values


def draw_k_gain(key, part):
    key = jax.random.fold_in(key, 29)
    values = jax.random.uniform(key, (HD,), jnp.float32, 0.6, 1.6)
    return values


def steps_of(stream_key, shape, pieces, least, high):
    def one(dim, parts):
        draws = jax.random.uniform(jax.random.fold_in(jax.random.fold_in(stream_key, 6), dim), (parts,), jnp.float32, least / len(pieces), high / len(pieces))
        return jnp.repeat(jnp.exp(draws), shape[dim] // parts).reshape((-1,) + (1,) * (len(shape) - dim - 1))

    loudness = one(*pieces[0])
    for cut in pieces[1:]:
        loudness = loudness * one(*cut)
    return loudness


def centred(rng, dims, scale, limit, cuts=(), held_as=jnp.bfloat16):
    array = scale * jax.random.normal(rng, dims, jnp.float32)
    if cuts:
        array = array * steps_of(rng, dims, cuts, -0.22, 0.18)
    return jnp.clip(array, -limit, limit).astype(held_as)


def setup_inputs(seed: int = 0) -> dict:
    splits = jax.random.split(jax.random.key(seed), 13)
    return {
        "prompts": centred(splits[0], (PROMPTS, LP, D), 1.0, 6.0, ((0, 32),)),
        "prompt_len": draw_prompt_len(jax.random.fold_in(splits[12], 71), 0),
        "admitted": draw_admitted(jax.random.fold_in(splits[12], 71), 0),
        "cache_len": draw_cache_len(jax.random.fold_in(splits[12], 71), 0),
        "cache_kv": draw_cache_kv(jax.random.fold_in(splits[12], 71), 0),
        "dec_tokens": centred(splits[5], (STEPS, SLOTS, D), 1.0, 6.0),
        "w_query": centred(splits[6], (D, HQ * HD), D ** -0.5, 0.09375, ((1, 4),)),
        "w_key": centred(splits[7], (D, KVH * HD), D ** -0.5, 0.09375, ((1, 4),)),
        "w_value": centred(splits[8], (D, KVH * HD), D ** -0.5, 0.09375, ((1, 4),)),
        "w_out": centred(splits[9], (HQ * HD, D), (HQ * HD) ** -0.5, 0.09375, ((0, 4),)),
        "q_gain": draw_q_gain(jax.random.fold_in(splits[12], 71), 0),
        "k_gain": draw_k_gain(jax.random.fold_in(splits[12], 71), 0),
    }


EPS = 1e-06
THETA = 1000000.0
NEG = -1e+30

def rotate(values, positions):
    half = values.shape[-1] // 2
    freq = THETA ** (-jnp.arange(half, dtype=jnp.float32) / half)
    angle = positions.astype(jnp.float32)[..., None, None] * freq
    cosine = jnp.cos(angle)
    sine = jnp.sin(angle)
    first = values[..., :half]
    second = values[..., half:]
    return jnp.concatenate([first * cosine - second * sine, second * cosine + first * sine], axis=-1)

def normalize(values, gain):
    return values * lax.rsqrt(lax.optimization_barrier(jnp.mean(values * values, axis=-1, keepdims=True)) + EPS) * gain

def reference(prompts, prompt_len, admitted, cache_len, cache_kv, dec_tokens, w_query, w_key, w_value, w_out, q_gain, k_gain):
    group = HQ // KVH
    scale = HD ** (-0.5)
    flat = prompts.reshape(PROMPTS * LP, D)
    spots = jnp.arange(LP, dtype=jnp.int32)
    query = jnp.dot(flat, w_query, preferred_element_type=jnp.float32).reshape(PROMPTS, LP, HQ, HD)
    key = jnp.dot(flat, w_key, preferred_element_type=jnp.float32).reshape(PROMPTS, LP, KVH, HD)
    value = jnp.dot(flat, w_value, preferred_element_type=jnp.float32).reshape(PROMPTS, LP, KVH, HD)
    query = rotate(normalize(query, q_gain), spots).astype(jnp.bfloat16)
    key = rotate(normalize(key, k_gain), spots).astype(jnp.bfloat16)
    value = value.astype(jnp.bfloat16)

    def attend(item):
        q_one, k_one, v_one, length = item
        grouped = q_one.reshape(LP, KVH, group, HD).astype(jnp.float32)
        scores = jnp.einsum('skgd,tkd->kgst', grouped, k_one.astype(jnp.float32)) * scale
        allowed = (spots[None, :] <= spots[:, None]) & (spots[None, :] < length)
        scores = jnp.where(allowed, scores, NEG)
        weights = jax.nn.softmax(scores, axis=-1).astype(jnp.bfloat16)
        mixed = jnp.einsum('kgst,tkd->skgd', weights.astype(jnp.float32), v_one.astype(jnp.float32))
        return mixed.reshape(LP, HQ * HD).astype(jnp.bfloat16)
    attn = lax.map(attend, (query, key, value, prompt_len)).reshape(PROMPTS * LP, HQ * HD)
    width = HQ * HD // N_HEAD
    total = jnp.zeros((PROMPTS * LP, D), jnp.float32)
    for index in range(N_HEAD):
        part = jnp.dot(attn[:, index * width:(index + 1) * width], w_out[index * width:(index + 1) * width], preferred_element_type=jnp.float32)
        rounded = lax.optimization_barrier(part.astype(jnp.bfloat16))
        total = total + rounded.astype(jnp.float32)
    prefill_out = total.astype(jnp.bfloat16).reshape(PROMPTS, LP, D)
    kv_pos = jnp.concatenate([key, value], axis=-1).transpose(2, 0, 1, 3)
    rows_each = LP // N_SEQ
    handed_kv = kv_pos.reshape(KVH, PROMPTS, rows_each, N_SEQ, 2 * HD).transpose(0, 1, 3, 2, 4).reshape(KVH, PROMPTS, LP, 2 * HD)
    is_new = admitted >= 0
    pick = jnp.maximum(admitted, 0).astype(jnp.int32)
    eff_len = jnp.where(is_new, prompt_len[pick], cache_len).astype(jnp.int32)
    cache_pos = cache_kv.reshape(KVH, SLOTS, N_SEQ, CACHE_DEV, 2 * HD).transpose(0, 1, 3, 2, 4).reshape(KVH, SLOTS, CACHE_LEN, 2 * HD)
    replaced = kv_pos[:, pick]
    head_part = jnp.where(is_new[None, :, None, None], replaced, cache_pos[:, :, :LP])
    cache_pos = jnp.concatenate([head_part, cache_pos[:, :, LP:]], axis=2)
    rows = dec_tokens.reshape(STEPS * SLOTS, D)
    order = jnp.arange(STEPS, dtype=jnp.int32)
    places = eff_len[None, :] + order[:, None]
    dq = jnp.dot(rows, w_query, preferred_element_type=jnp.float32).reshape(STEPS, SLOTS, HQ, HD)
    dk = jnp.dot(rows, w_key, preferred_element_type=jnp.float32).reshape(STEPS, SLOTS, KVH, HD)
    dv = jnp.dot(rows, w_value, preferred_element_type=jnp.float32).reshape(STEPS, SLOTS, KVH, HD)
    dq = rotate(normalize(dq, q_gain), places).astype(jnp.bfloat16)
    dk = rotate(normalize(dk, k_gain), places).astype(jnp.bfloat16)
    dv = dv.astype(jnp.bfloat16)
    grouped = dq.reshape(STEPS, SLOTS, KVH, group, HD).astype(jnp.float32)
    stored_keys = cache_pos[..., :HD].astype(jnp.float32)
    stored_values = cache_pos[..., HD:].astype(jnp.float32)
    cache_scores = jnp.einsum('trkgd,krcd->trkgc', grouped, stored_keys) * scale
    live = jnp.arange(CACHE_LEN, dtype=jnp.int32)[None, :] < eff_len[:, None]
    cache_scores = jnp.where(live[None, :, None, None, :], cache_scores, NEG)
    new_scores = jnp.einsum('trkgd,urkd->trkgu', grouped, dk.astype(jnp.float32)) * scale
    causal = order[None, :] <= order[:, None]
    new_scores = jnp.where(causal[:, None, None, None, :], new_scores, NEG)
    weights = jax.nn.softmax(jnp.concatenate([cache_scores, new_scores], axis=-1), axis=-1)
    mixed = jnp.einsum('trkgc,krcd->trkgd', weights[..., :CACHE_LEN], stored_values)
    mixed = mixed + jnp.einsum('trkgu,urkd->trkgd', weights[..., CACHE_LEN:], dv.astype(jnp.float32))
    mixed = mixed.astype(jnp.bfloat16).reshape(STEPS * SLOTS, HQ * HD)
    decode_out = jnp.dot(mixed, w_out, preferred_element_type=jnp.float32).astype(jnp.bfloat16).reshape(STEPS, SLOTS, D)
    return (prefill_out, handed_kv, decode_out)
```

```python
import functools

import jax
import jax.numpy as jnp
import numpy as np
from jax import lax
from jax.experimental import pallas as pl
from jax.experimental.pallas import tpu as pltpu
from jax.sharding import PartitionSpec as P

D = 4096
HD = 128
GROUP = 8
WIDTH = GROUP * HD
LP = 256
SLOTS = 4
STEPS = 4
ROWS = SLOTS * STEPS
CACHE = 512
NS = 32
NH = 4
EACH = LP // NS
EPS = 1e-06
THETA = 1000000.0
NEG = -1e30
SCALE = HD ** (-0.5)
LOG2E = 1.4426950408889634
TILE = 256
NT = WIDTH // TILE
F32 = jnp.float32
BF16 = jnp.bfloat16


def dot(a, b):
    return jnp.dot(a, b, preferred_element_type=F32)


def dot_nt(a, b):
    return lax.dot_general(a, b, (((1,), (1,)), ((), ())), preferred_element_type=F32)


def iota(shape, dim):
    return lax.broadcasted_iota(jnp.int32, shape, dim)


def rotation(positions, freq, gain):
    angle = positions.astype(F32) * freq
    sign = jnp.where(iota((1, HD), 1) < HD // 2, -1.0, 1.0)
    return jnp.cos(angle) * gain, jnp.sin(angle) * (pltpu.roll(gain, HD // 2, 1) * sign)


def normrot(a, first, second):
    inverse = lax.rsqrt(jnp.mean(a * a, axis=-1, keepdims=True) + EPS)
    return (a * first + pltpu.roll(a, HD // 2, 1) * second) * inverse


def kernel(
    plen,
    adm,
    clen,
    freq_ref,
    qg_ref,
    kg_ref,
    prompts,
    dec,
    wq,
    wk,
    wv,
    wo,
    cache,
    out,
    handed,
    dec_out,
    x_v,
    wkv_v,
    wq_v,
    wo_v,
    cache_v,
    tab_v,
    kv_v,
    give_v,
    hand_v,
    dq_v,
    dkv_v,
    pa_v,
    part_s,
    part_r,
    own_v,
    out_v,
    soft_s,
    soft_r,
    join_s,
    join_r,
    da_v,
    dpart_s,
    dpart_r,
    dout_v,
    in_sem,
    wq_sem,
    wo_sem,
    out_sem,
    part_ss,
    part_rs,
    seq_ss,
    seq_rs,
    dpart_ss,
    dpart_rs,
):
    y = lax.axis_index("head")
    me = lax.axis_index("seq")
    right = lax.rem(y + 1, NH)
    left = lax.rem(y + NH - 1, NH)

    def remote(src, dst, send, recv, **where):
        return pltpu.make_async_remote_copy(
            src_ref=src,
            dst_ref=dst,
            send_sem=send,
            recv_sem=recv,
            device_id=where,
            device_id_type=pl.DeviceIdType.MESH,
        )

    def rows(start, size):
        return pl.ds(pl.multiple_of(start, size), size)

    load_x0 = pltpu.make_async_copy(prompts.at[0:LP], x_v.at[0:LP], in_sem.at[0])
    load_k = pltpu.make_async_copy(wk, wkv_v.at[:, 0:HD], in_sem.at[1])
    load_v = pltpu.make_async_copy(wv, wkv_v.at[:, HD : 2 * HD], in_sem.at[2])
    load_dec = pltpu.make_async_copy(dec, x_v.at[LP : LP + ROWS], in_sem.at[3])
    load_x1 = pltpu.make_async_copy(
        prompts.at[LP : 2 * LP], x_v.at[LP + ROWS : 2 * LP + ROWS], in_sem.at[4]
    )
    load_cache = pltpu.make_async_copy(cache, cache_v, in_sem.at[5])

    def load_q(j):
        return pltpu.make_async_copy(wq.at[:, j * TILE : (j + 1) * TILE], wq_v.at[j], wq_sem.at[j])

    def load_o(k, j):
        start = lax.rem(y + k, NH) * WIDTH + j * TILE
        return pltpu.make_async_copy(
            wo.at[:, pl.ds(pl.multiple_of(start, TILE), TILE)], wo_v.at[k, j], wo_sem.at[k, j]
        )

    load_x0.start()
    load_k.start()
    load_v.start()
    load_dec.start()
    load_x1.start()
    for j in range(NT):
        load_q(j).start()
    for k in (2, 3, 1, 0):
        for j in range(NT):
            load_o(k, j).start()
    load_cache.start()

    barrier = pltpu.get_barrier_semaphore()

    def greet(i, carry):
        pl.semaphore_signal(
            barrier,
            inc=1,
            device_id={"seq": lax.rem(me + i, NS)},
            device_id_type=pl.DeviceIdType.MESH,
        )
        return carry

    lax.fori_loop(1, NS, greet, 0)
    for k in range(1, NH):
        pl.semaphore_signal(
            barrier,
            inc=1,
            device_id={"head": lax.rem(y + k, NH)},
            device_id_type=pl.DeviceIdType.MESH,
        )

    freq = freq_ref[...]
    q_gain = qg_ref[...]
    k_gain = kg_ref[...]
    spots = iota((LP, HD), 0)
    tab_v[0], tab_v[1] = rotation(spots, freq, q_gain)
    tab_v[2], tab_v[3] = rotation(spots, freq, k_gain)
    admitted = [adm[r] for r in range(SLOTS)]
    handed_len = [plen[jnp.maximum(admitted[r], 0)] for r in range(SLOTS)]
    is_new = [admitted[r] >= 0 for r in range(SLOTS)]
    eff_len = [jnp.where(is_new[r], handed_len[r], clen[r]) for r in range(SLOTS)]

    def per_slot(slot, values):
        picked = jnp.full(slot.shape, values[0], jnp.int32)
        for r in range(1, SLOTS):
            picked = jnp.where(slot == r, values[r], picked)
        return picked

    token = iota((ROWS, HD), 0)
    places = per_slot(token & (SLOTS - 1), eff_len) + (token >> 2)
    dq_first, dq_second = rotation(places, freq, q_gain)
    dk_first, dk_second = rotation(places, freq, k_gain)

    load_x0.wait()
    load_k.wait()
    load_v.wait()
    load_dec.wait()
    kv = dot(x_v[0 : LP + ROWS, :], wkv_v[...])
    kv_v[0:LP, 0:HD] = normrot(kv[0:LP, 0:HD], tab_v[2], tab_v[3]).astype(BF16)
    kv_v[0:LP, HD : 2 * HD] = kv[0:LP, HD : 2 * HD].astype(BF16)
    dkv_v[...] = jnp.zeros_like(dkv_v)
    dkv_v[0:ROWS, 0:HD] = normrot(kv[LP : LP + ROWS, 0:HD], dk_first, dk_second).astype(BF16)
    dkv_v[0:ROWS, HD : 2 * HD] = kv[LP : LP + ROWS, HD : 2 * HD].astype(BF16)
    load_x1.wait()
    kv = dot(x_v[LP + ROWS : 2 * LP + ROWS, :], wkv_v[...])
    kv_v[LP : 2 * LP, 0:HD] = normrot(kv[:, 0:HD], tab_v[2], tab_v[3]).astype(BF16)
    kv_v[LP : 2 * LP, HD : 2 * HD] = kv[:, HD : 2 * HD].astype(BF16)

    place = iota((2 * LP, 2 * LP), 0)
    source = (((place >> 3) & 1) << 8) + ((place & 7) << 5) + (place >> 4)
    pick = jnp.where(source == iota((2 * LP, 2 * LP), 1), 1.0, 0.0).astype(BF16)
    give_v[...] = dot(pick, kv_v[...]).astype(BF16)
    hand_v[rows(me * 16, 16), :] = give_v[rows(me * 16, 16), :]

    pl.semaphore_wait(barrier, NS - 1 + NH - 1)

    def hand(i, way):
        other = lax.rem(me + i, NS)
        return remote(
            give_v.at[rows(other * 16, 16)],
            hand_v.at[rows(way * 16, 16)],
            seq_ss.at[0, other],
            seq_rs.at[0, way],
            seq=other,
        )

    def hand_start(i, carry):
        hand(i, me).start()
        return carry

    lax.fori_loop(1, NS, hand_start, 0)

    order = iota((LP, LP), 0) >= iota((LP, LP), 1)

    def attend(p):
        length = plen[2 * me + p]
        allowed = order & (iota((LP, LP), 1) < length)
        first = 0 if p == 0 else LP + ROWS
        count = LP + ROWS if p == 0 else LP

        def pair(j, carry):
            if p == 0:
                pltpu.make_async_copy(wq.at[:, 0:TILE], wq_v.at[j], wq_sem.at[j]).wait()
            query = dot(x_v[first : first + count, :], wq_v[j])
            parts = []
            for b in range(TILE // HD):
                mine = query[:, b * HD : (b + 1) * HD]
                q_one = normrot(mine[0:LP], tab_v[0], tab_v[1]).astype(BF16)
                if p == 0:
                    new = normrot(mine[LP : LP + ROWS], dq_first, dq_second).astype(BF16)
                    dq_v[rows((j * 2 + b) * ROWS, ROWS), :] = new
                scores = dot_nt(q_one, kv_v[p * LP : (p + 1) * LP, 0:HD])
                scores = jnp.where(allowed, scores, NEG)
                top = jnp.max(scores, axis=-1, keepdims=True)
                expo = jnp.exp2((scores - top) * (SCALE * LOG2E))
                weights = expo * (1.0 / jnp.sum(expo, axis=-1, keepdims=True))
                mixed = dot(weights.astype(BF16), kv_v[p * LP : (p + 1) * LP, HD : 2 * HD])
                parts.append(mixed.astype(BF16))
            pa_v[p, :, rows(j * TILE, TILE)] = jnp.concatenate(parts, axis=1)
            return carry

        lax.fori_loop(0, NT, pair, 0)

    def project(p, k, j):
        return dot(pa_v[p], wo_v[k, j])

    def part(slot, j):
        to = right if slot in (0, 2, 3) else left
        return remote(
            part_s.at[slot, j], part_r.at[slot, j], part_ss.at[slot, j], part_rs.at[slot, j], head=to
        )

    def wait_o(k, j):
        pltpu.make_async_copy(wo.at[:, 0:TILE], wo_v.at[k, j], wo_sem.at[k, j]).wait()

    def send(p, k, slot, far, j, first_use):
        if first_use:
            wait_o(k, j)
        value = project(p, k, j)
        if far is not None:
            part(far, j).wait_recv()
            value = value + part_r[far, j].astype(F32)
        part_s[slot, j] = value.astype(BF16)
        part(slot, j).start()

    attend(0)

    def first_parts(j, carry):
        send(0, 2, 0, None, j, True)
        send(0, 3, 4, None, j, True)
        return carry

    lax.fori_loop(0, NT, first_parts, 0)
    attend(1)

    def second_parts(j, carry):
        send(1, 1, 3, None, j, True)
        send(1, 2, 1, None, j, False)
        return carry

    lax.fori_loop(0, NT, second_parts, 0)

    load_cache.wait()

    def hand_wait(i, carry):
        other = lax.rem(me + i, NS)
        hand(i, other).wait_recv()
        return carry

    lax.fori_loop(1, NS, hand_wait, 0)
    save_hand = pltpu.make_async_copy(hand_v, handed, out_sem.at[0])
    save_hand.start()

    queries = dq_v[...]
    heads = GROUP * ROWS

    def pieces():
        for r in range(SLOTS):
            slot = iota((heads, CACHE), 0) & (SLOTS - 1)
            place = (iota((heads, CACHE), 1) << 5) + me
            limit = jnp.where(is_new[r], 0, clen[r])
            yield (
                dot_nt(queries, cache_v[r * CACHE : (r + 1) * CACHE, 0:HD]),
                (slot == r) & (place < limit),
                cache_v[r * CACHE : (r + 1) * CACHE, HD : 2 * HD],
            )
        slot = iota((heads, 2 * LP), 0) & (SLOTS - 1)
        column = iota((heads, 2 * LP), 1)
        prompt = column >> 3
        place = ((column & 7) << 5) + me
        yield (
            dot_nt(queries, hand_v[:, 0:HD]),
            (prompt == per_slot(slot, admitted)) & (place < per_slot(slot, handed_len)),
            hand_v[:, HD : 2 * HD],
        )
        row = iota((heads, HD), 0)
        column = iota((heads, HD), 1) + jnp.where(me == 0, 0, ROWS)
        yield (
            dot_nt(queries, dkv_v[:, 0:HD]),
            ((row & 3) == (column & 3)) & ((column >> 2) <= ((row >> 2) & 3)) & (column < ROWS),
            dkv_v[:, HD : 2 * HD],
        )

    parts = [(jnp.where(mask, s, NEG), mask, v) for s, mask, v in pieces()]
    top = functools.reduce(jnp.maximum, [jnp.max(s, axis=-1, keepdims=True) for s, _, _ in parts])
    total = jnp.zeros((heads, 1), F32)
    acc = jnp.zeros((heads, HD), F32)
    for s, mask, v in parts:
        expo = jnp.where(mask, jnp.exp2((s - top) * (SCALE * LOG2E)), 0.0)
        total = total + jnp.sum(expo, axis=-1, keepdims=True)
        acc = acc + dot(expo.astype(BF16), v)
    state = jnp.where(iota((heads, HD), 1) < HD // 2, top, total)
    for q in range(heads // NS):
        soft_s[pl.ds(q, NS, stride=8), :] = acc[q * NS : (q + 1) * NS, :]
        soft_s[pl.ds(q + 4, NS, stride=8), :] = state[q * NS : (q + 1) * NS, :]
    soft_r[rows(me * 8, 8), :] = soft_s[rows(me * 8, 8), :]

    def soft(i, way):
        other = lax.rem(me + i, NS)
        return remote(
            soft_s.at[rows(other * 8, 8)],
            soft_r.at[rows(way * 8, 8)],
            seq_ss.at[1, other],
            seq_rs.at[1, way],
            seq=other,
        )

    def soft_start(i, carry):
        soft(i, me).start()
        return carry

    def soft_wait(i, carry):
        soft(i, lax.rem(me + i, NS)).wait_recv()
        return carry

    lax.fori_loop(1, NS, soft_start, 0)

    def own_parts(j, carry):
        wait_o(0, j)
        own_v[0, j] = project(0, 0, j)
        own_v[1, j] = project(1, 0, j)
        return carry

    lax.fori_loop(0, NT, own_parts, 0)

    lax.fori_loop(1, NS, soft_wait, 0)
    joined = []
    for q in range(heads // NS):
        sums = soft_r[pl.ds(q, NS, stride=8), :]
        both = soft_r[pl.ds(q + 4, NS, stride=8), :]
        tops = both[:, 0:1]
        weight = jnp.exp2((tops - jnp.max(tops, axis=0, keepdims=True)) * (SCALE * LOG2E))
        whole = jnp.sum(weight * both[:, HD // 2 : HD // 2 + 1], axis=0, keepdims=True)
        joined.append(jnp.sum(weight * sums, axis=0, keepdims=True) / whole)
    for q in range(heads // NS):
        join_s[q : q + 1, :] = joined[q]
        join_s[q + 4 : q + 5, :] = joined[q]
    join_r[rows(me * 8, 8), :] = join_s[...]

    def join(i, way):
        other = lax.rem(me + i, NS)
        return remote(
            join_s, join_r.at[rows(way * 8, 8)], seq_ss.at[2, other], seq_rs.at[2, way], seq=other
        )

    def join_start(i, carry):
        join(i, me).start()
        return carry

    def join_wait(i, carry):
        join(i, lax.rem(me + i, NS)).wait_recv()
        return carry

    lax.fori_loop(1, NS, join_start, 0)

    def third_parts(j, carry):
        send(0, 1, 2, 0, j, False)
        return carry

    lax.fori_loop(0, NT, third_parts, 0)

    lax.fori_loop(1, NS, join_wait, 0)
    for head in range(GROUP):
        start = (head % 2) * ROWS * 8 + head // 2
        da_v[:, head * HD : (head + 1) * HD] = join_r[pl.ds(start, ROWS, stride=8), :].astype(BF16)

    def dpart(k):
        return remote(
            dpart_s.at[k],
            dpart_r.at[k],
            dpart_ss.at[k],
            dpart_rs.at[k],
            head=lax.rem(y + k, NH),
        )

    def dec_project(k):
        return jnp.concatenate([dot(da_v[...], wo_v[k, j]) for j in range(NT)], axis=1)

    for k in (2, 1, 3):
        dpart_s[k] = dec_project(k).astype(BF16)
        dpart(k).start()
    dec_own = dec_project(0)

    def fourth_parts(j, carry):
        send(1, 3, 5, 1, j, False)
        return carry

    lax.fori_loop(0, NT, fourth_parts, 0)

    for k in (1, 3, 2):
        dpart(k).wait_recv()
        dec_own = dec_own + dpart_r[k].astype(F32)
    dout_v[...] = dec_own.astype(BF16)
    save_dec = pltpu.make_async_copy(dout_v, dec_out, out_sem.at[1])
    save_dec.start()

    def save(p, j):
        return pltpu.make_async_copy(
            out_v.at[p, j], out.at[p * LP : (p + 1) * LP, rows(j * TILE, TILE)], out_sem.at[2 + p]
        )

    def finish(j, carry):
        for p in range(2):
            part(2 + p, j).wait_recv()
            part(4 + p, j).wait_recv()
            value = own_v[p, j] + part_r[2 + p, j].astype(F32) + part_r[4 + p, j].astype(F32)
            out_v[p, j] = value.astype(BF16)
            save(p, j).start()
        return carry

    lax.fori_loop(0, NT, finish, 0)

    def settle(j, carry):
        for slot in range(6):
            part(slot, j).wait_send()
        return carry

    lax.fori_loop(0, NT, settle, 0)

    def settle_seq(i, carry):
        hand(i, me).wait_send()
        soft(i, me).wait_send()
        join(i, me).wait_send()
        return carry

    lax.fori_loop(1, NS, settle_seq, 0)
    for k in range(1, NH):
        dpart(k).wait_send()
    save_hand.wait()
    save_dec.wait()
    for p in range(2):
        pltpu.make_async_copy(
            out.at[p * LP : (p + 1) * LP, :], out.at[p * LP : (p + 1) * LP, :], out_sem.at[2 + p]
        ).wait()


def local(
    prompts,
    prompt_len,
    admitted,
    cache_len,
    cache_kv,
    dec_tokens,
    w_query,
    w_key,
    w_value,
    w_out,
    q_gain,
    k_gain,
):
    half = HD // 2
    one = (THETA ** (-np.arange(half, dtype=np.float64) / half)).astype(np.float32)
    freq = jnp.asarray(np.concatenate([one, one])[None, :])
    smem = pl.BlockSpec(memory_space=pltpu.SMEM)
    vmem = pl.BlockSpec(memory_space=pltpu.VMEM)
    hbm = pl.BlockSpec(memory_space=pl.ANY)
    dma = pltpu.SemaphoreType.DMA
    out, handed, decoded = pl.pallas_call(
        kernel,
        out_shape=[
            jax.ShapeDtypeStruct((2 * LP, WIDTH), BF16),
            jax.ShapeDtypeStruct((2 * LP, 2 * HD), BF16),
            jax.ShapeDtypeStruct((ROWS, WIDTH), BF16),
        ],
        in_specs=[smem] * 3 + [vmem] * 3 + [hbm] * 7,
        out_specs=[hbm] * 3,
        scratch_shapes=[
            pltpu.VMEM((2 * LP + ROWS, D), BF16),
            pltpu.VMEM((D, 2 * HD), BF16),
            pltpu.VMEM((NT, D, TILE), BF16),
            pltpu.VMEM((NH, NT, WIDTH, TILE), BF16),
            pltpu.VMEM((SLOTS * CACHE, 2 * HD), BF16),
            pltpu.VMEM((4, LP, HD), F32),
            pltpu.VMEM((2 * LP, 2 * HD), BF16),
            pltpu.VMEM((2 * LP, 2 * HD), BF16),
            pltpu.VMEM((2 * LP, 2 * HD), BF16),
            pltpu.VMEM((GROUP * ROWS, HD), BF16),
            pltpu.VMEM((HD, 2 * HD), BF16),
            pltpu.VMEM((2, LP, WIDTH), BF16),
            pltpu.VMEM((6, NT, LP, TILE), BF16),
            pltpu.VMEM((6, NT, LP, TILE), BF16),
            pltpu.VMEM((2, NT, LP, TILE), F32),
            pltpu.VMEM((2, NT, LP, TILE), BF16),
            pltpu.VMEM((NS * 8, HD), F32),
            pltpu.VMEM((NS * 8, HD), F32),
            pltpu.VMEM((8, HD), F32),
            pltpu.VMEM((NS * 8, HD), F32),
            pltpu.VMEM((ROWS, WIDTH), BF16),
            pltpu.VMEM((NH, ROWS, WIDTH), BF16),
            pltpu.VMEM((NH, ROWS, WIDTH), BF16),
            pltpu.VMEM((ROWS, WIDTH), BF16),
            dma((6,)),
            dma((NT,)),
            dma((NH, NT)),
            dma((4,)),
            dma((6, NT)),
            dma((6, NT)),
            dma((3, NS)),
            dma((3, NS)),
            dma((NH,)),
            dma((NH,)),
        ],
        compiler_params=pltpu.CompilerParams(
            collective_id=0, has_side_effects=True, vmem_limit_bytes=56 * 2**20
        ),
        cost_estimate=pl.CostEstimate(
            flops=10_500_000_000, bytes_accessed=25_000_000, transcendentals=2_000_000
        ),
    )(
        prompt_len,
        admitted,
        cache_len,
        freq,
        q_gain[None, :],
        k_gain[None, :],
        prompts.reshape(2 * LP, D),
        dec_tokens.reshape(ROWS, D),
        w_query,
        w_key,
        w_value,
        w_out,
        cache_kv.reshape(SLOTS * CACHE, 2 * HD),
    )
    return (
        out.reshape(2, LP, WIDTH),
        handed.reshape(1, 2 * NS, EACH, 2 * HD),
        decoded.reshape(STEPS, SLOTS, WIDTH),
    )


def solution(mesh):
    placed = (
        P("seq", None, None),
        P(),
        P(),
        P(),
        P("head", None, "seq", None),
        P(),
        P(None, "head"),
        P(None, "head"),
        P(None, "head"),
        P("head", None),
        P(),
        P(),
    )
    return jax.shard_map(
        local,
        mesh=mesh,
        in_specs=placed,
        out_specs=(P("seq", None, "head"), P("head", None, "seq", None), P(None, None, "head")),
        check_vma=False,
    )
```

```python
import functools

import jax
import jax.numpy as jnp
import numpy as np
from jax import lax
from jax.experimental import pallas as pl
from jax.experimental.pallas import tpu as pltpu
from jax.sharding import PartitionSpec as P

D = 4096
HD = 128
GROUP = 8
WIDTH = GROUP * HD
LP = 256
HALF = LP // 2
SLOTS = 4
STEPS = 4
ROWS = SLOTS * STEPS
CACHE = 512
NS = 32
NH = 4
EACH = LP // NS
EPS = 1e-06
THETA = 1000000.0
NEG = -1e30
SCALE = HD ** (-0.5)
LOG2E = 1.4426950408889634
TILE = 256
NT = WIDTH // TILE
F32 = jnp.float32
BF16 = jnp.bfloat16


def dot(a, b):
    return jnp.dot(a, b, preferred_element_type=F32)


def dot_nt(a, b):
    return lax.dot_general(a, b, (((1,), (1,)), ((), ())), preferred_element_type=F32)


def iota(shape, dim):
    return lax.broadcasted_iota(jnp.int32, shape, dim)


def rotation(positions, freq):
    angle = positions.astype(F32) * freq
    sign = jnp.where(iota((1, HD), 1) < HD // 2, -1.0, 1.0)
    return jnp.cos(angle), jnp.sin(angle) * sign


def gained(cosine, sine, gain):
    return cosine * gain, sine * pltpu.roll(gain, HD // 2, 1)


def normrot(a, first, second):
    inverse = lax.rsqrt(jnp.mean(a * a, axis=-1, keepdims=True) + EPS)
    return (a * first + pltpu.roll(a, HD // 2, 1) * second) * inverse


def kernel(
    plen,
    adm,
    clen,
    freq_ref,
    qg_ref,
    kg_ref,
    prompts,
    dec,
    wq,
    wk,
    wv,
    wo,
    cache,
    out_v,
    hand_v,
    dout_v,
    x_v,
    dec_v,
    wkv_v,
    wq_v,
    wo_v,
    cache_v,
    tab_v,
    kv_v,
    give_v,
    q_v,
    dq_v,
    dkv_v,
    pa_v,
    part_s,
    part_r,
    own_v,
    soft_s,
    soft_r,
    join_s,
    join_r,
    da_v,
    dpart_s,
    dpart_r,
    x_sem,
    in_sem,
    wq_sem,
    wo_sem,
    part_ss,
    part_rs,
    seq_ss,
    seq_rs,
    dpart_ss,
    dpart_rs,
):
    y = lax.axis_index("head")
    me = lax.axis_index("seq")
    right = lax.rem(y + 1, NH)
    left = lax.rem(y + NH - 1, NH)

    def remote(src, dst, send, recv, **where):
        return pltpu.make_async_remote_copy(
            src_ref=src,
            dst_ref=dst,
            send_sem=send,
            recv_sem=recv,
            device_id=where,
            device_id_type=pl.DeviceIdType.MESH,
        )

    def rows(start, size):
        return pl.ds(pl.multiple_of(start, size), size)

    def load_x(half, p):
        source = p * LP + half * HALF
        target = half * (LP + ROWS) + p * HALF
        return pltpu.make_async_copy(
            prompts.at[source : source + HALF], x_v.at[target : target + HALF], x_sem.at[half, p]
        )

    load_k = pltpu.make_async_copy(wk, wkv_v.at[:, 0:HD], in_sem.at[0])
    load_v = pltpu.make_async_copy(wv, wkv_v.at[:, HD : 2 * HD], in_sem.at[1])
    load_dec = pltpu.make_async_copy(dec, dec_v, in_sem.at[2])
    load_cache = pltpu.make_async_copy(cache, cache_v, in_sem.at[3])

    def load_q(j):
        return pltpu.make_async_copy(wq.at[:, j * TILE : (j + 1) * TILE], wq_v.at[j], wq_sem.at[j])

    def load_o(k, j):
        start = lax.rem(y + k, NH) * WIDTH + j * TILE
        return pltpu.make_async_copy(
            wo.at[:, pl.ds(pl.multiple_of(start, TILE), TILE)], wo_v.at[k, j], wo_sem.at[k, j]
        )

    load_dec.start()
    load_k.start()
    load_v.start()
    load_x(0, 0).start()
    load_x(0, 1).start()
    for j in range(NT):
        load_q(j).start()
    for j in range(NT):
        load_o(2, j).start()
        load_o(3, j).start()
    load_x(1, 0).start()
    load_x(1, 1).start()
    for k in (1, 0):
        for j in range(NT):
            load_o(k, j).start()
    load_cache.start()

    barrier = pltpu.get_barrier_semaphore()

    def greet(i, carry):
        pl.semaphore_signal(
            barrier,
            inc=1,
            device_id={"seq": lax.rem(me + i, NS)},
            device_id_type=pl.DeviceIdType.MESH,
        )
        return carry

    for k in range(1, NH):
        pl.semaphore_signal(
            barrier,
            inc=1,
            device_id={"head": lax.rem(y + k, NH)},
            device_id_type=pl.DeviceIdType.MESH,
        )
    lax.fori_loop(1, NS, greet, 0)

    freq = freq_ref[...]
    q_gain = qg_ref[...]
    k_gain = kg_ref[...]
    for half in range(2):
        first, second = rotation(iota((HALF, HD), 0) + half * HALF, freq)
        tab_v[half, 0], tab_v[half, 1] = gained(first, second, q_gain)
        tab_v[half, 2], tab_v[half, 3] = gained(first, second, k_gain)
    admitted = [adm[r] for r in range(SLOTS)]
    handed_len = [plen[jnp.maximum(admitted[r], 0)] for r in range(SLOTS)]
    is_new = [admitted[r] >= 0 for r in range(SLOTS)]
    eff_len = [jnp.where(is_new[r], handed_len[r], clen[r]) for r in range(SLOTS)]

    def per_slot(slot, values):
        picked = jnp.full(slot.shape, values[0], jnp.int32)
        for r in range(1, SLOTS):
            picked = jnp.where(slot == r, values[r], picked)
        return picked

    token = iota((ROWS, HD), 0)
    places = per_slot(token & (SLOTS - 1), eff_len) + (token >> 2)
    first, second = rotation(places, freq)
    dq_first, dq_second = gained(first, second, q_gain)
    dk_first, dk_second = gained(first, second, k_gain)

    load_dec.wait()
    x_v[LP : LP + ROWS, :] = jnp.concatenate(
        [dec_v[t].astype(F32) for t in range(STEPS)], axis=0
    ).astype(BF16)

    def keys_values(half):
        start = half * (LP + ROWS)
        count = LP if half else LP + ROWS
        kv = dot(x_v[start : start + count, :], wkv_v[...])
        for p in range(2):
            mine = kv[p * HALF : (p + 1) * HALF]
            to = slice(p * LP + half * HALF, p * LP + (half + 1) * HALF)
            key = normrot(mine[:, 0:HD], tab_v[half, 2], tab_v[half, 3])
            kv_v[to, 0:HD] = key.astype(BF16)
            kv_v[to, HD : 2 * HD] = mine[:, HD : 2 * HD].astype(BF16)
        if half == 0:
            new = kv[LP : LP + ROWS]
            dkv_v[...] = jnp.zeros_like(dkv_v)
            dkv_v[0:ROWS, 0:HD] = normrot(new[:, 0:HD], dk_first, dk_second).astype(BF16)
            dkv_v[0:ROWS, HD : 2 * HD] = new[:, HD : 2 * HD].astype(BF16)

    def attend(half):
        start = half * (LP + ROWS)
        count = LP if half else LP + ROWS
        for j in range(NT):
            if half == 0:
                load_q(j).wait()
            query = dot(x_v[start : start + count, :], wq_v[j])
            for b in range(TILE // HD):
                head = j * 2 + b
                mine = query[:, b * HD : (b + 1) * HD]
                for p in range(2):
                    one = normrot(mine[p * HALF : (p + 1) * HALF], tab_v[half, 0], tab_v[half, 1])
                    q_v[p, head * HALF : (head + 1) * HALF, :] = one.astype(BF16)
                if half == 0:
                    one = normrot(mine[LP : LP + ROWS], dq_first, dq_second)
                    dq_v[head * ROWS : (head + 1) * ROWS, :] = one.astype(BF16)
        keys = (half + 1) * HALF
        at = iota((keys, HALF), 0)
        causal = at <= iota((keys, HALF), 1) + half * HALF
        for p in range(2):
            bias = jnp.where(causal & (at < plen[2 * me + p]), 0.0, NEG)
            scores = dot_nt(kv_v[p * LP : p * LP + keys, 0:HD], q_v[p])
            scores = scores + jnp.concatenate([bias] * GROUP, axis=1)
            top = jnp.max(scores, axis=0, keepdims=True)
            expo = jnp.exp2((scores - top) * (SCALE * LOG2E))
            weights = expo * (1.0 / jnp.sum(expo, axis=0, keepdims=True))
            values = kv_v[p * LP : p * LP + keys, HD : 2 * HD].astype(F32).T.astype(BF16)
            mixed = dot(values, weights.astype(BF16))
            for head in range(GROUP):
                one = mixed[:, head * HALF : (head + 1) * HALF].T.astype(BF16)
                pa_v[half, p * HALF : (p + 1) * HALF, head * HD : (head + 1) * HD] = one

    def part(slot, j):
        to = right if slot in (0, 2, 3) else left
        return remote(
            part_s.at[slot, j], part_r.at[slot, j], part_ss.at[slot, j], part_rs.at[slot, j], head=to
        )

    def project(half, k, j):
        return dot(pa_v[half], wo_v[k, j])

    def send(half, k, slot, j, far=None, loaded=False):
        if not loaded:
            load_o(k, j).wait()
        value = project(half, k, j)
        if far is not None:
            part(far, j).wait_recv()
            value = value + part_r[far, j].astype(F32)
        part_s[slot, j] = value.astype(BF16)
        part(slot, j).start()

    load_k.wait()
    load_v.wait()
    load_x(0, 0).wait()
    load_x(0, 1).wait()
    keys_values(0)
    attend(0)
    pl.semaphore_wait(barrier, NS - 1 + NH - 1)
    for j in range(NT):
        send(0, 2, 0, j)
        send(0, 3, 4, j)

    load_x(1, 0).wait()
    load_x(1, 1).wait()
    keys_values(1)

    place = iota((2 * LP, 2 * LP), 0)
    source = (((place >> 3) & 1) << 8) + ((place & 7) << 5) + (place >> 4)
    pick = jnp.where(source == iota((2 * LP, 2 * LP), 1), 1.0, 0.0).astype(BF16)
    give_v[...] = dot(pick, kv_v[...]).astype(BF16)
    hand_v[rows(me * 16, 16), :] = give_v[rows(me * 16, 16), :]

    def hand(i, way):
        other = lax.rem(me + i, NS)
        return remote(
            give_v.at[rows(other * 16, 16)],
            hand_v.at[rows(way * 16, 16)],
            seq_ss.at[0, other],
            seq_rs.at[0, way],
            seq=other,
        )

    def hand_start(i, carry):
        hand(i, me).start()
        return carry

    lax.fori_loop(1, NS, hand_start, 0)

    attend(1)
    for j in range(NT):
        send(1, 1, 3, j)
        send(1, 2, 1, j, loaded=True)

    load_cache.wait()

    def hand_wait(i, carry):
        other = lax.rem(me + i, NS)
        hand(i, other).wait_recv()
        return carry

    lax.fori_loop(1, NS, hand_wait, 0)

    queries = dq_v[...]
    heads = GROUP * ROWS

    def pieces():
        for r in range(SLOTS):
            slot = iota((heads, CACHE), 0) & (SLOTS - 1)
            at = (iota((heads, CACHE), 1) << 5) + me
            limit = jnp.where(is_new[r], 0, clen[r])
            yield (
                dot_nt(queries, cache_v[r * CACHE : (r + 1) * CACHE, 0:HD]),
                (slot == r) & (at < limit),
                cache_v[r * CACHE : (r + 1) * CACHE, HD : 2 * HD],
            )
        slot = iota((heads, 2 * LP), 0) & (SLOTS - 1)
        column = iota((heads, 2 * LP), 1)
        prompt = column >> 3
        at = ((column & 7) << 5) + me
        yield (
            dot_nt(queries, hand_v[:, 0:HD]),
            (prompt == per_slot(slot, admitted)) & (at < per_slot(slot, handed_len)),
            hand_v[:, HD : 2 * HD],
        )
        row = iota((heads, HD), 0)
        column = iota((heads, HD), 1) + jnp.where(me == 0, 0, ROWS)
        yield (
            dot_nt(queries, dkv_v[:, 0:HD]),
            ((row & 3) == (column & 3)) & ((column >> 2) <= ((row >> 2) & 3)) & (column < ROWS),
            dkv_v[:, HD : 2 * HD],
        )

    parts = [(jnp.where(mask, s, NEG), mask, v) for s, mask, v in pieces()]
    top = functools.reduce(jnp.maximum, [jnp.max(s, axis=-1, keepdims=True) for s, _, _ in parts])
    total = jnp.zeros((heads, 1), F32)
    acc = jnp.zeros((heads, HD), F32)
    for s, mask, v in parts:
        expo = jnp.where(mask, jnp.exp2((s - top) * (SCALE * LOG2E)), 0.0)
        total = total + jnp.sum(expo, axis=-1, keepdims=True)
        acc = acc + dot(expo.astype(BF16), v)
    state = jnp.where(iota((heads, HD), 1) < HD // 2, top, total)
    for q in range(heads // NS):
        soft_s[pl.ds(q, NS, stride=8), :] = acc[q * NS : (q + 1) * NS, :]
        soft_s[pl.ds(q + 4, NS, stride=8), :] = state[q * NS : (q + 1) * NS, :]
    soft_r[rows(me * 8, 8), :] = soft_s[rows(me * 8, 8), :]

    def soft(i, way):
        other = lax.rem(me + i, NS)
        return remote(
            soft_s.at[rows(other * 8, 8)],
            soft_r.at[rows(way * 8, 8)],
            seq_ss.at[1, other],
            seq_rs.at[1, way],
            seq=other,
        )

    def soft_start(i, carry):
        soft(i, me).start()
        return carry

    def soft_wait(i, carry):
        soft(i, lax.rem(me + i, NS)).wait_recv()
        return carry

    lax.fori_loop(1, NS, soft_start, 0)

    for j in range(NT):
        load_o(0, j).wait()
        own_v[0, j] = project(0, 0, j)
        own_v[1, j] = project(1, 0, j)

    lax.fori_loop(1, NS, soft_wait, 0)
    joined = []
    for q in range(heads // NS):
        sums = soft_r[pl.ds(q, NS, stride=8), :]
        both = soft_r[pl.ds(q + 4, NS, stride=8), :]
        tops = both[:, 0:1]
        weight = jnp.exp2((tops - jnp.max(tops, axis=0, keepdims=True)) * (SCALE * LOG2E))
        whole = jnp.sum(weight * both[:, HD // 2 : HD // 2 + 1], axis=0, keepdims=True)
        joined.append(jnp.sum(weight * sums, axis=0, keepdims=True) / whole)
    for q in range(heads // NS):
        join_s[q : q + 1, :] = joined[q]
        join_s[q + 4 : q + 5, :] = joined[q]
    join_r[rows(me * 8, 8), :] = join_s[...]

    def join(i, way):
        other = lax.rem(me + i, NS)
        return remote(
            join_s, join_r.at[rows(way * 8, 8)], seq_ss.at[2, other], seq_rs.at[2, way], seq=other
        )

    def join_start(i, carry):
        join(i, me).start()
        return carry

    def join_wait(i, carry):
        join(i, lax.rem(me + i, NS)).wait_recv()
        return carry

    lax.fori_loop(1, NS, join_start, 0)

    for j in range(NT):
        send(0, 1, 2, j, far=0, loaded=True)

    lax.fori_loop(1, NS, join_wait, 0)
    for head in range(GROUP):
        start = (head % 2) * ROWS * 8 + head // 2
        da_v[:, head * HD : (head + 1) * HD] = join_r[pl.ds(start, ROWS, stride=8), :].astype(BF16)

    def dpart(k):
        return remote(
            dpart_s.at[k],
            dpart_r.at[k],
            dpart_ss.at[k],
            dpart_rs.at[k],
            head=lax.rem(y + k, NH),
        )

    def dec_project(k):
        return jnp.concatenate([dot(da_v[...], wo_v[k, j]) for j in range(NT)], axis=1)

    for k in (2, 1, 3):
        dpart_s[k] = dec_project(k).astype(BF16)
        dpart(k).start()
    dec_own = dec_project(0)

    for j in range(NT):
        send(1, 3, 5, j, far=1, loaded=True)

    for k in (1, 3, 2):
        dpart(k).wait_recv()
        dec_own = dec_own + dpart_r[k].astype(F32)
    for t in range(STEPS):
        dout_v[t] = dec_own[t * SLOTS : (t + 1) * SLOTS].astype(BF16)

    for j in range(NT):
        for half in range(2):
            part(2 + half, j).wait_recv()
            part(4 + half, j).wait_recv()
            value = own_v[half, j] + part_r[2 + half, j].astype(F32)
            value = (value + part_r[4 + half, j].astype(F32)).astype(BF16)
            for p in range(2):
                to = p * LP + half * HALF
                out_v[to : to + HALF, j * TILE : (j + 1) * TILE] = value[p * HALF : (p + 1) * HALF]

    def settle(i, carry):
        hand(i, me).wait_send()
        soft(i, me).wait_send()
        join(i, me).wait_send()
        return carry

    lax.fori_loop(1, NS, settle, 0)
    for k in range(1, NH):
        dpart(k).wait_send()
    for slot in range(6):
        for j in range(NT):
            part(slot, j).wait_send()


def save(out_v, hand_v, dout_v, out, handed, dec_out, sem):
    copies = [
        pltpu.make_async_copy(out_v, out, sem.at[0]),
        pltpu.make_async_copy(hand_v, handed, sem.at[1]),
        pltpu.make_async_copy(dout_v, dec_out, sem.at[2]),
    ]
    for copy in copies:
        copy.start()
    for copy in copies:
        copy.wait()


def local(
    prompts,
    prompt_len,
    admitted,
    cache_len,
    cache_kv,
    dec_tokens,
    w_query,
    w_key,
    w_value,
    w_out,
    q_gain,
    k_gain,
):
    half = HD // 2
    one = (THETA ** (-np.arange(half, dtype=np.float64) / half)).astype(np.float32)
    freq = jnp.asarray(np.concatenate([one, one])[None, :])
    smem = pl.BlockSpec(memory_space=pltpu.SMEM)
    vmem = pl.BlockSpec(memory_space=pltpu.VMEM)
    hbm = pl.BlockSpec(memory_space=pl.ANY)
    dma = pltpu.SemaphoreType.DMA
    shapes = [(2 * LP, WIDTH), (2 * LP, 2 * HD), (STEPS, SLOTS, WIDTH)]
    results = pl.pallas_call(
        kernel,
        out_shape=[pltpu.VMEM(shape, BF16) for shape in shapes],
        in_specs=[smem] * 3 + [vmem] * 3 + [hbm] * 7,
        out_specs=[vmem] * 3,
        scratch_shapes=[
            pltpu.VMEM((2 * LP + ROWS, D), BF16),
            pltpu.VMEM((STEPS, SLOTS, D), BF16),
            pltpu.VMEM((D, 2 * HD), BF16),
            pltpu.VMEM((NT, D, TILE), BF16),
            pltpu.VMEM((NH, NT, WIDTH, TILE), BF16),
            pltpu.VMEM((SLOTS * CACHE, 2 * HD), BF16),
            pltpu.VMEM((2, 4, HALF, HD), F32),
            pltpu.VMEM((2 * LP, 2 * HD), BF16),
            pltpu.VMEM((2 * LP, 2 * HD), BF16),
            pltpu.VMEM((2, GROUP * HALF, HD), BF16),
            pltpu.VMEM((GROUP * ROWS, HD), BF16),
            pltpu.VMEM((HD, 2 * HD), BF16),
            pltpu.VMEM((2, LP, WIDTH), BF16),
            pltpu.VMEM((6, NT, LP, TILE), BF16),
            pltpu.VMEM((6, NT, LP, TILE), BF16),
            pltpu.VMEM((2, NT, LP, TILE), F32),
            pltpu.VMEM((NS * 8, HD), F32),
            pltpu.VMEM((NS * 8, HD), F32),
            pltpu.VMEM((8, HD), F32),
            pltpu.VMEM((NS * 8, HD), F32),
            pltpu.VMEM((ROWS, WIDTH), BF16),
            pltpu.VMEM((NH, ROWS, WIDTH), BF16),
            pltpu.VMEM((NH, ROWS, WIDTH), BF16),
            dma((2, 2)),
            dma((4,)),
            dma((NT,)),
            dma((NH, NT)),
            dma((6, NT)),
            dma((6, NT)),
            dma((3, NS)),
            dma((3, NS)),
            dma((NH,)),
            dma((NH,)),
        ],
        compiler_params=pltpu.CompilerParams(
            collective_id=0, has_side_effects=True, vmem_limit_bytes=52 * 2**20
        ),
        cost_estimate=pl.CostEstimate(
            flops=10_500_000_000, bytes_accessed=25_000_000, transcendentals=2_000_000
        ),
    )(
        prompt_len,
        admitted,
        cache_len,
        freq,
        q_gain[None, :],
        k_gain[None, :],
        prompts.reshape(2 * LP, D),
        dec_tokens,
        w_query,
        w_key,
        w_value,
        w_out,
        cache_kv.reshape(SLOTS * CACHE, 2 * HD),
    )
    out, handed, decoded = pl.pallas_call(
        save,
        out_shape=[jax.ShapeDtypeStruct(shape, BF16) for shape in shapes],
        in_specs=[vmem] * 3,
        out_specs=[hbm] * 3,
        scratch_shapes=[dma((3,))],
    )(*results)
    return (
        out.reshape(2, LP, WIDTH),
        handed.reshape(1, 2 * NS, EACH, 2 * HD),
        decoded,
    )


def solution(mesh):
    placed = (
        P("seq", None, None),
        P(),
        P(),
        P(),
        P("head", None, "seq", None),
        P(),
        P(None, "head"),
        P(None, "head"),
        P(None, "head"),
        P("head", None),
        P(),
        P(),
    )
    return jax.shard_map(
        local,
        mesh=mesh,
        in_specs=placed,
        out_specs=(P("seq", None, "head"), P("head", None, "seq", None), P(None, None, "head")),
        check_vma=False,
    )
```

```python
import functools

import jax
import jax.numpy as jnp
import numpy as np
from jax import lax
from jax.experimental import pallas as pl
from jax.experimental.pallas import tpu as pltpu
from jax.sharding import PartitionSpec as P

D = 4096
HD = 128
GROUP = 8
WIDTH = GROUP * HD
LP = 256
HALF = LP // 2
SLOTS = 4
STEPS = 4
ROWS = SLOTS * STEPS
CACHE = 512
NS = 32
NH = 4
EACH = LP // NS
EPS = 1e-06
THETA = 1000000.0
NEG = -1e30
SCALE = HD ** (-0.5)
LOG2E = 1.4426950408889634
TILE = 256
NT = WIDTH // TILE
F32 = jnp.float32
BF16 = jnp.bfloat16


def dot(a, b):
    return jnp.dot(a, b, preferred_element_type=F32)


def dot_nt(a, b):
    return lax.dot_general(a, b, (((1,), (1,)), ((), ())), preferred_element_type=F32)


def iota(shape, dim):
    return lax.broadcasted_iota(jnp.int32, shape, dim)


def rotation(positions, freq):
    angle = positions.astype(F32) * freq
    sign = jnp.where(iota((1, HD), 1) < HD // 2, -1.0, 1.0)
    return jnp.cos(angle), jnp.sin(angle) * sign


def gained(cosine, sine, gain):
    return cosine * gain, sine * pltpu.roll(gain, HD // 2, 1)


def normrot(a, first, second):
    inverse = lax.rsqrt(jnp.mean(a * a, axis=-1, keepdims=True) + EPS)
    return (a * first + pltpu.roll(a, HD // 2, 1) * second) * inverse


def kernel(
    plen_ref,
    adm_ref,
    clen_ref,
    freq_ref,
    qg_ref,
    kg_ref,
    prompts,
    dec,
    wq,
    wk,
    wv,
    wo,
    cache,
    out,
    handed,
    dec_out,
    plen,
    adm,
    clen,
    row_v,
    x_v,
    dec_v,
    w_v,
    wo_v,
    cache_v,
    tab_v,
    f_v,
    kv_v,
    give_v,
    hand_v,
    q_v,
    dq_v,
    dkv_v,
    pa_v,
    part_s,
    part_r,
    own_v,
    soft_s,
    soft_r,
    join_s,
    join_r,
    da_v,
    dpart_s,
    dpart_r,
    out_v,
    dout_v,
    small_sem,
    x_sem,
    in_sem,
    w_sem,
    wo_sem,
    out_sem,
    part_ss,
    part_rs,
    seq_ss,
    seq_rs,
    dpart_ss,
    dpart_rs,
):
    y = lax.axis_index("head")
    me = lax.axis_index("seq")
    right = lax.rem(y + 1, NH)
    left = lax.rem(y + NH - 1, NH)

    def remote(src, dst, send, recv, **where):
        return pltpu.make_async_remote_copy(
            src_ref=src,
            dst_ref=dst,
            send_sem=send,
            recv_sem=recv,
            device_id=where,
            device_id_type=pl.DeviceIdType.MESH,
        )

    def landed(ref, sem):
        pltpu.make_async_copy(ref, ref, sem).wait()

    def rows(start, size):
        return pl.ds(pl.multiple_of(start, size), size)

    def load_x(half, p):
        source = p * LP + half * HALF
        target = half * (LP + ROWS) + p * HALF
        return pltpu.make_async_copy(
            prompts.at[source : source + HALF], x_v.at[target : target + HALF], x_sem.at[half]
        )

    small = [
        pltpu.make_async_copy(ref, to, small_sem.at[i])
        for ref, to, i in (
            (freq_ref, row_v.at[0], 0),
            (qg_ref, row_v.at[1], 0),
            (kg_ref, row_v.at[2], 0),
            (plen_ref, plen, 1),
            (adm_ref, adm, 2),
            (clen_ref, clen, 3),
        )
    ]
    load_k = pltpu.make_async_copy(wk, w_v.at[0, :, 0:HD], w_sem.at[0])
    load_v = pltpu.make_async_copy(wv, w_v.at[0, :, HD : 2 * HD], w_sem.at[0])
    load_dec = pltpu.make_async_copy(dec, dec_v, in_sem.at[0])
    load_cache = pltpu.make_async_copy(cache, cache_v, in_sem.at[1])

    def load_q(t):
        return pltpu.make_async_copy(wq.at[:, rows((t - 1) * TILE, TILE)], w_v.at[t], w_sem.at[t])

    def load_o(k, j):
        start = lax.rem(y + k, NH) * WIDTH + j * TILE
        sem = wo_sem.at[j if k in (2, 3) else NT + k]
        return pltpu.make_async_copy(wo.at[:, rows(start, TILE)], wo_v.at[k, j], sem)

    load_dec.start()
    load_k.start()
    load_v.start()
    load_x(0, 0).start()
    load_x(0, 1).start()
    for load in small:
        load.start()

    barrier = pltpu.get_barrier_semaphore()

    def greet(i, carry):
        pl.semaphore_signal(
            barrier,
            inc=1,
            device_id={"seq": lax.rem(me + i, NS)},
            device_id_type=pl.DeviceIdType.MESH,
        )
        return carry

    for k in range(1, NH):
        pl.semaphore_signal(
            barrier,
            inc=1,
            device_id={"head": lax.rem(y + k, NH)},
            device_id_type=pl.DeviceIdType.MESH,
        )
    lax.fori_loop(1, NS, greet, 0)

    load_q(1).start()
    load_q(2).start()

    landed(row_v, small_sem.at[0])
    for load in small[3:]:
        load.wait()
    freq, q_gain, k_gain = row_v[0], row_v[1], row_v[2]
    for half in range(2):
        first, second = rotation(iota((HALF, HD), 0) + half * HALF, freq)
        tab_v[half, 0], tab_v[half, 1] = gained(first, second, q_gain)
        tab_v[half, 2], tab_v[half, 3] = gained(first, second, k_gain)
    admitted = [adm[r] for r in range(SLOTS)]
    handed_len = [plen[jnp.maximum(admitted[r], 0)] for r in range(SLOTS)]
    is_new = [admitted[r] >= 0 for r in range(SLOTS)]
    eff_len = [jnp.where(is_new[r], handed_len[r], clen[r]) for r in range(SLOTS)]

    def per_slot(slot, values):
        picked = jnp.full(slot.shape, values[0], jnp.int32)
        for r in range(1, SLOTS):
            picked = jnp.where(slot == r, values[r], picked)
        return picked

    token = iota((ROWS, HD), 0)
    places = per_slot(token & (SLOTS - 1), eff_len) + (token >> 2)
    first, second = rotation(places, freq)
    dq_first, dq_second = gained(first, second, q_gain)
    dk_first, dk_second = gained(first, second, k_gain)

    load_dec.wait()
    x_v[LP : LP + ROWS, :] = jnp.concatenate(
        [dec_v[t].astype(F32) for t in range(STEPS)], axis=0
    ).astype(BF16)

    def finish_query(half, t, count):
        slot = lax.rem(t + 5, 6)
        for b in range(TILE // HD):
            mine = f_v[t, 0:count, b * HD : (b + 1) * HD]
            for p in range(2):
                one = normrot(mine[p * HALF : (p + 1) * HALF], tab_v[half, 0], tab_v[half, 1])
                q_v[p, rows(slot * TILE + b * HD, HD), :] = one.astype(BF16)
            if half == 0:
                one = normrot(mine[LP : LP + ROWS], dq_first, dq_second)
                dq_v[rows((slot * 2 + b) * ROWS, ROWS), :] = one.astype(BF16)

    def multiply(half, after_keys=None):
        start = half * (LP + ROWS)
        count = LP if half else LP + ROWS

        def tile(t, carry):
            if half == 0:
                landed(w_v.at[t], w_sem.at[t])

                @pl.when(t < NT - 2)
                def _():
                    load_q(t + 3).start()

                @pl.when(t < NT)
                def _():
                    load_o(2, t).start()
                    load_o(3, t).start()

            if after_keys is not None:
                pl.when(t == 1)(after_keys)

            finish_query(half, lax.rem(t + 5, 6), count)
            f_v[t, 0:count, :] = dot(x_v[start : start + count, :], w_v[t])
            return carry

        lax.fori_loop(0, 1 + NT, tile, 0)
        finish_query(half, NT, count)

    def keys_values(half):
        for p in range(2):
            mine = f_v[0, p * HALF : (p + 1) * HALF, :]
            to = slice(p * LP + half * HALF, p * LP + (half + 1) * HALF)
            key = normrot(mine[:, 0:HD], tab_v[half, 2], tab_v[half, 3])
            kv_v[to, 0:HD] = key.astype(BF16)
            kv_v[to, HD : 2 * HD] = mine[:, HD : 2 * HD].astype(BF16)
        if half == 0:
            new = f_v[0, LP : LP + ROWS, :]
            dkv_v[...] = jnp.zeros_like(dkv_v)
            dkv_v[0:ROWS, 0:HD] = normrot(new[:, 0:HD], dk_first, dk_second).astype(BF16)
            dkv_v[0:ROWS, HD : 2 * HD] = new[:, HD : 2 * HD].astype(BF16)

    def attend(half):
        keys = (half + 1) * HALF
        at = iota((keys, HALF), 0)
        causal = at <= iota((keys, HALF), 1) + half * HALF
        for p in range(2):
            bias = jnp.where(causal & (at < plen[2 * me + p]), 0.0, NEG)
            scores = dot_nt(kv_v[p * LP : p * LP + keys, 0:HD], q_v[p, 0 : GROUP * HALF])
            scores = scores + jnp.concatenate([bias] * GROUP, axis=1)
            top = jnp.max(scores, axis=0, keepdims=True)
            expo = jnp.exp2((scores - top) * (SCALE * LOG2E))
            weights = expo * (1.0 / jnp.sum(expo, axis=0, keepdims=True))
            values = kv_v[p * LP : p * LP + keys, HD : 2 * HD].astype(F32).T.astype(BF16)
            mixed = dot(values, weights.astype(BF16))
            for head in range(GROUP):
                one = mixed[:, head * HALF : (head + 1) * HALF].T.astype(BF16)
                pa_v[half, p * HALF : (p + 1) * HALF, head * HD : (head + 1) * HD] = one

    def part(slot, j):
        to = right if slot in (0, 2, 3) else left
        return remote(
            part_s.at[slot, j],
            part_r.at[slot, j],
            part_ss.at[0],
            part_rs.at[slot, 0 if slot in (3, 4) else j],
            head=to,
        )

    def send_all(half, targets, tiles, far=None, load=False):
        def tile(j, carry):
            if load:
                landed(wo_v.at[2:4, j], wo_sem.at[j])
            if far is not None:
                landed(part_r.at[far, j], part_rs.at[far, j])
            values = [dot(pa_v[half], wo_v[k, j]) for k, slot in targets]
            for (k, slot), value in zip(targets, values):
                if far is not None:
                    value = value + part_r[far, j].astype(F32)
                part_s[slot, j] = value.astype(BF16)
                part(slot, j).start()
            return carry

        lax.fori_loop(*tiles, tile, 0)

    landed(x_v.at[0:LP], x_sem.at[0])
    multiply(0)
    load_x(1, 0).start()
    load_x(1, 1).start()
    for j in range(NT):
        load_o(1, j).start()
    for j in range(NT):
        load_o(0, j).start()
    load_cache.start()
    keys_values(0)
    attend(0)
    pl.semaphore_wait(barrier, NS - 1 + NH - 1)
    send_all(0, ((2, 0), (3, 4)), (0, NT), load=True)

    landed(x_v.at[LP + ROWS : 2 * LP + ROWS], x_sem.at[1])
    def hand(i, way):
        other = lax.rem(me + i, NS)
        return remote(
            give_v.at[rows(other * 16, 16)],
            hand_v.at[rows(way * 16, 16)],
            seq_ss.at[0],
            seq_rs.at[0],
            seq=other,
        )

    def hand_over():
        keys_values(1)
        place = iota((2 * LP, 2 * LP), 0)
        source = (((place >> 3) & 1) << 8) + ((place & 7) << 5) + (place >> 4)
        pick = jnp.where(source == iota((2 * LP, 2 * LP), 1), 1.0, 0.0).astype(BF16)
        give_v[...] = dot(pick, kv_v[...]).astype(BF16)
        hand_v[rows(me * 16, 16), :] = give_v[rows(me * 16, 16), :]

        def hand_start(i, carry):
            hand(i, me).start()
            return carry

        lax.fori_loop(1, NS, hand_start, 0)

    multiply(1, hand_over)
    attend(1)
    landed(wo_v.at[1], wo_sem.at[NT + 1])
    send_all(1, ((1, 3), (2, 1)), (0, NT))
    load_cache.wait()

    landed(hand_v.at[0 : (NS - 1) * 16], seq_rs.at[0])
    save_hand = pltpu.make_async_copy(hand_v, handed, out_sem.at[0])
    save_hand.start()

    heads = GROUP * ROWS
    queries = dq_v[0:heads]

    def pieces():
        for r in range(SLOTS):
            slot = iota((heads, CACHE), 0) & (SLOTS - 1)
            at = (iota((heads, CACHE), 1) << 5) + me
            limit = jnp.where(is_new[r], 0, clen[r])
            yield (
                dot_nt(queries, cache_v[r * CACHE : (r + 1) * CACHE, 0:HD]),
                (slot == r) & (at < limit),
                cache_v[r * CACHE : (r + 1) * CACHE, HD : 2 * HD],
            )
        slot = iota((heads, 2 * LP), 0) & (SLOTS - 1)
        column = iota((heads, 2 * LP), 1)
        prompt = column >> 3
        at = ((column & 7) << 5) + me
        yield (
            dot_nt(queries, hand_v[:, 0:HD]),
            (prompt == per_slot(slot, admitted)) & (at < per_slot(slot, handed_len)),
            hand_v[:, HD : 2 * HD],
        )
        row = iota((heads, HD), 0)
        column = iota((heads, HD), 1) + jnp.where(me == 0, 0, ROWS)
        yield (
            dot_nt(queries, dkv_v[:, 0:HD]),
            ((row & 3) == (column & 3)) & ((column >> 2) <= ((row >> 2) & 3)) & (column < ROWS),
            dkv_v[:, HD : 2 * HD],
        )

    parts = [(jnp.where(mask, s, NEG), mask, v) for s, mask, v in pieces()]
    top = functools.reduce(jnp.maximum, [jnp.max(s, axis=-1, keepdims=True) for s, _, _ in parts])
    total = jnp.zeros((heads, 1), F32)
    acc = jnp.zeros((heads, HD), F32)
    for s, mask, v in parts:
        expo = jnp.where(mask, jnp.exp2((s - top) * (SCALE * LOG2E)), 0.0)
        total = total + jnp.sum(expo, axis=-1, keepdims=True)
        acc = acc + dot(expo.astype(BF16), v)
    state = jnp.where(iota((heads, HD), 1) < HD // 2, top, total)
    for q in range(heads // NS):
        soft_s[pl.ds(q, NS, stride=8), :] = acc[q * NS : (q + 1) * NS, :]
        soft_s[pl.ds(q + 4, NS, stride=8), :] = state[q * NS : (q + 1) * NS, :]
    soft_r[rows(me * 8, 8), :] = soft_s[rows(me * 8, 8), :]

    def soft(i, way):
        other = lax.rem(me + i, NS)
        return remote(
            soft_s.at[rows(other * 8, 8)],
            soft_r.at[rows(way * 8, 8)],
            seq_ss.at[1],
            seq_rs.at[1],
            seq=other,
        )

    def soft_start(i, carry):
        soft(i, me).start()
        return carry

    lax.fori_loop(1, NS, soft_start, 0)

    send_all(0, ((1, 2),), (0, NT), far=0)

    landed(wo_v.at[0], wo_sem.at[NT])

    def own(j, carry):
        own_v[0, j] = dot(pa_v[0], wo_v[0, j])
        own_v[1, j] = dot(pa_v[1], wo_v[0, j])
        return carry

    lax.fori_loop(0, NT, own, 0)

    landed(soft_r.at[0 : (NS - 1) * 8], seq_rs.at[1])
    joined = []
    for q in range(heads // NS):
        sums = soft_r[pl.ds(q, NS, stride=8), :]
        both = soft_r[pl.ds(q + 4, NS, stride=8), :]
        tops = both[:, 0:1]
        weight = jnp.exp2((tops - jnp.max(tops, axis=0, keepdims=True)) * (SCALE * LOG2E))
        whole = jnp.sum(weight * both[:, HD // 2 : HD // 2 + 1], axis=0, keepdims=True)
        joined.append(jnp.sum(weight * sums, axis=0, keepdims=True) / whole)
    for q in range(heads // NS):
        join_s[q : q + 1, :] = joined[q]
        join_s[q + 4 : q + 5, :] = joined[q]
    join_r[rows(me * 8, 8), :] = join_s[...]

    def join(i, way):
        other = lax.rem(me + i, NS)
        return remote(
            join_s, join_r.at[rows(way * 8, 8)], seq_ss.at[2], seq_rs.at[2], seq=other
        )

    def join_start(i, carry):
        join(i, me).start()
        return carry

    lax.fori_loop(1, NS, join_start, 0)


    send_all(1, ((3, 5),), (0, NT - 1), far=1)
    landed(join_r.at[0 : (NS - 1) * 8], seq_rs.at[2])
    for head in range(GROUP):
        start = (head % 2) * ROWS * 8 + head // 2
        da_v[:, head * HD : (head + 1) * HD] = join_r[pl.ds(start, ROWS, stride=8), :].astype(BF16)

    def dpart(k):
        return remote(
            dpart_s.at[k],
            dpart_r.at[k],
            dpart_ss.at[0],
            dpart_rs.at[0],
            head=lax.rem(y + k, NH),
        )

    def dec_project(k):
        return jnp.concatenate([dot(da_v[...], wo_v[k, j]) for j in range(NT)], axis=1)

    for k in (2, 1, 3):
        dpart_s[k] = dec_project(k).astype(BF16)
        dpart(k).start()
    dec_own = dec_project(0)

    send_all(1, ((3, 5),), (NT - 1, NT), far=1)
    landed(hand_v.at[0 : (NS - 1) * 16], seq_ss.at[0])
    landed(soft_r.at[0 : (NS - 1) * 8], seq_ss.at[1])
    landed(join_r.at[0 : (NS - 1) * 8], seq_ss.at[2])
    save_hand.wait()

    landed(part_r.at[3], part_rs.at[3, 0])
    landed(part_r.at[4], part_rs.at[4, 0])

    def finish(j, carry):
        for half in range(2):
            late = 5 if half else 2
            landed(part_r.at[late, j], part_rs.at[late, j])
        for half in range(2):
            value = own_v[half, j] + part_r[2 + half, j].astype(F32)
            value = (value + part_r[4 + half, j].astype(F32)).astype(BF16)
            for p in range(2):
                out_v[half, j, p] = value[p * HALF : (p + 1) * HALF]
            pltpu.make_async_copy(
                out_v.at[half, j],
                out.at[:, half * HALF : (half + 1) * HALF, rows(j * TILE, TILE)],
                out_sem.at[2],
            ).start()
        return carry

    lax.fori_loop(0, NT, finish, 0)

    landed(dpart_r.at[1:NH], dpart_rs.at[0])
    for k in (1, 3, 2):
        dec_own = dec_own + dpart_r[k].astype(F32)
    for t in range(STEPS):
        dout_v[t] = dec_own[t * SLOTS : (t + 1) * SLOTS].astype(BF16)
    save_dec = pltpu.make_async_copy(dout_v, dec_out, out_sem.at[1])
    save_dec.start()

    landed(dpart_s.at[1:NH], dpart_ss.at[0])
    landed(part_s, part_ss.at[0])
    landed(out_v, out_sem.at[2])
    save_dec.wait()


def local(
    prompts,
    prompt_len,
    admitted,
    cache_len,
    cache_kv,
    dec_tokens,
    w_query,
    w_key,
    w_value,
    w_out,
    q_gain,
    k_gain,
):
    half = HD // 2
    one = (THETA ** (-np.arange(half, dtype=np.float64) / half)).astype(np.float32)
    freq = jnp.asarray(np.concatenate([one, one])[None, :])
    hbm = pl.BlockSpec(memory_space=pl.ANY)
    dma = pltpu.SemaphoreType.DMA
    shapes = [(2, LP, WIDTH), (2 * LP, 2 * HD), (STEPS, SLOTS, WIDTH)]
    out, handed, decoded = pl.pallas_call(
        kernel,
        out_shape=[pltpu.VMEM(shape, BF16) for shape in shapes],
        in_specs=[hbm] * 13,
        out_specs=[hbm] * 3,
        scratch_shapes=[
            pltpu.SMEM((2 * NS,), jnp.int32),
            pltpu.SMEM((SLOTS,), jnp.int32),
            pltpu.SMEM((SLOTS,), jnp.int32),
            pltpu.VMEM((3, 1, HD), F32),
            pltpu.VMEM((2 * LP + ROWS, D), BF16),
            pltpu.VMEM((STEPS, SLOTS, D), BF16),
            pltpu.VMEM((1 + NT, D, TILE), BF16),
            pltpu.VMEM((NH, NT, WIDTH, TILE), BF16),
            pltpu.VMEM((SLOTS * CACHE, 2 * HD), BF16),
            pltpu.VMEM((2, 4, HALF, HD), F32),
            pltpu.VMEM((2 + NT, LP + ROWS, TILE), F32),
            pltpu.VMEM((2 * LP, 2 * HD), BF16),
            pltpu.VMEM((2 * LP, 2 * HD), BF16),
            pltpu.VMEM((2 * LP, 2 * HD), BF16),
            pltpu.VMEM((2, (GROUP + 4) * HALF, HD), BF16),
            pltpu.VMEM(((GROUP + 4) * ROWS, HD), BF16),
            pltpu.VMEM((HD, 2 * HD), BF16),
            pltpu.VMEM((2, LP, WIDTH), BF16),
            pltpu.VMEM((6, NT, LP, TILE), BF16),
            pltpu.VMEM((6, NT, LP, TILE), BF16),
            pltpu.VMEM((2, NT, LP, TILE), F32),
            pltpu.VMEM((NS * 8, HD), F32),
            pltpu.VMEM((NS * 8, HD), F32),
            pltpu.VMEM((8, HD), F32),
            pltpu.VMEM((NS * 8, HD), F32),
            pltpu.VMEM((ROWS, WIDTH), BF16),
            pltpu.VMEM((NH, ROWS, WIDTH), BF16),
            pltpu.VMEM((NH, ROWS, WIDTH), BF16),
            pltpu.VMEM((2, NT, 2, HALF, TILE), BF16),
            pltpu.VMEM((STEPS, SLOTS, WIDTH), BF16),
            dma((4,)),
            dma((2,)),
            dma((2,)),
            dma((1 + NT,)),
            dma((NT + 2,)),
            dma((3,)),
            dma((1,)),
            dma((6, NT)),
            dma((3,)),
            dma((3,)),
            dma((1,)),
            dma((1,)),
        ],
        compiler_params=pltpu.CompilerParams(
            collective_id=0, has_side_effects=True, vmem_limit_bytes=56 * 2**20
        ),
        cost_estimate=pl.CostEstimate(
            flops=10_500_000_000, bytes_accessed=25_000_000, transcendentals=2_000_000
        ),
    )(
        prompt_len,
        admitted,
        cache_len,
        freq,
        q_gain[None, :],
        k_gain[None, :],
        prompts.reshape(2 * LP, D),
        dec_tokens,
        w_query,
        w_key,
        w_value,
        w_out,
        cache_kv.reshape(SLOTS * CACHE, 2 * HD),
    )
    return (
        out,
        handed.reshape(1, 2 * NS, EACH, 2 * HD),
        decoded,
    )


def solution(mesh):
    placed = (
        P("seq", None, None),
        P(),
        P(),
        P(),
        P("head", None, "seq", None),
        P(),
        P(None, "head"),
        P(None, "head"),
        P(None, "head"),
        P("head", None),
        P(),
        P(),
    )
    return jax.shard_map(
        local,
        mesh=mesh,
        in_specs=placed,
        out_specs=(P("seq", None, "head"), P("head", None, "seq", None), P(None, None, "head")),
        check_vma=False,
    )
```

```python
import functools

import jax
import jax.numpy as jnp
import numpy as np
from jax import lax
from jax.experimental import pallas as pl
from jax.experimental.pallas import tpu as pltpu
from jax.sharding import PartitionSpec as P

D = 4096
HD = 128
GROUP = 8
WIDTH = GROUP * HD
LP = 256
HALF = LP // 2
SLOTS = 4
STEPS = 4
ROWS = SLOTS * STEPS
CACHE = 512
NS = 32
NH = 4
NB = WIDTH // HD
EACH = LP // NS
EPS = 1e-06
THETA = 1000000.0
NEG = -1e30
SCALE = HD ** (-0.5)
LOG2E = 1.4426950408889634
TILE = 256
NT = WIDTH // TILE
WIDE = 2 * TILE
F32 = jnp.float32
BF16 = jnp.bfloat16


def dot(a, b):
    return jnp.dot(a, b, preferred_element_type=F32)


def dot_nt(a, b):
    return lax.dot_general(a, b, (((1,), (1,)), ((), ())), preferred_element_type=F32)


def iota(shape, dim):
    return lax.broadcasted_iota(jnp.int32, shape, dim)


def rotation(positions, freq):
    angle = positions.astype(F32) * freq
    sign = jnp.where(iota((1, HD), 1) < HD // 2, -1.0, 1.0)
    return jnp.cos(angle), jnp.sin(angle) * sign


def gained(cosine, sine, gain):
    return cosine * gain, sine * pltpu.roll(gain, HD // 2, 1)


def normrot(a, first, second):
    inverse = lax.rsqrt(jnp.mean(a * a, axis=-1, keepdims=True) + EPS)
    return (a * first + pltpu.roll(a, HD // 2, 1) * second) * inverse


def kernel(
    plen_ref,
    adm_ref,
    clen_ref,
    freq_ref,
    qg_ref,
    kg_ref,
    prompts,
    dec,
    wq,
    wk,
    wv,
    wo,
    cache,
    out,
    handed,
    dec_out,
    plen,
    adm,
    clen,
    row_v,
    x_v,
    dec_v,
    w_v,
    wo_v,
    cache_v,
    tab_v,
    f_v,
    kv_v,
    give_v,
    hand_v,
    q_v,
    dq_v,
    dkv_v,
    pa_v,
    part_s,
    part_r,
    own_v,
    soft_s,
    soft_r,
    join_s,
    join_r,
    da_v,
    dpart_s,
    dpart_r,
    dcol_s,
    dcol_r,
    out_v,
    dout_v,
    small_sem,
    x_sem,
    in_sem,
    w_sem,
    wo_sem,
    out_sem,
    part_ss,
    part_rs,
    seq_ss,
    seq_rs,
    dpart_ss,
    dpart_rs,
    dcol_sem,
):
    y = lax.axis_index("head")
    me = lax.axis_index("seq")
    right = lax.rem(y + 1, NH)
    left = lax.rem(y + NH - 1, NH)

    def remote(src, dst, send, recv, **where):
        return pltpu.make_async_remote_copy(
            src_ref=src,
            dst_ref=dst,
            send_sem=send,
            recv_sem=recv,
            device_id=where,
            device_id_type=pl.DeviceIdType.MESH,
        )

    def landed(ref, sem):
        pltpu.make_async_copy(ref, ref, sem).wait()

    def rows(start, size):
        return pl.ds(pl.multiple_of(start, size), size)

    def load_x(half, p):
        source = p * LP + half * HALF
        target = half * LP + p * HALF
        return pltpu.make_async_copy(
            prompts.at[source : source + HALF], x_v.at[target : target + HALF], x_sem.at[half]
        )

    small = [
        pltpu.make_async_copy(ref, to, small_sem.at[i])
        for ref, to, i in (
            (freq_ref, row_v.at[0], 0),
            (qg_ref, row_v.at[1], 0),
            (kg_ref, row_v.at[2], 0),
            (plen_ref, plen, 1),
            (adm_ref, adm, 2),
            (clen_ref, clen, 3),
        )
    ]
    load_k = pltpu.make_async_copy(wk, w_v.at[0, :, 0:HD], w_sem.at[0])
    load_v = pltpu.make_async_copy(wv, w_v.at[0, :, HD : 2 * HD], w_sem.at[0])
    load_dec = pltpu.make_async_copy(dec, dec_v, in_sem.at[0])
    load_cache = pltpu.make_async_copy(cache, cache_v, in_sem.at[1])

    def load_q(t):
        return pltpu.make_async_copy(wq.at[:, rows((t - 1) * TILE, TILE)], w_v.at[t], w_sem.at[t])

    def load_o(k, j):
        start = lax.rem(y + k, NH) * WIDTH + j * TILE
        sem = wo_sem.at[j // 2 if k in (2, 3) else 2 + k]
        return pltpu.make_async_copy(wo.at[:, rows(start, TILE)], wo_v.at[k, j], sem)

    load_k.start()
    load_v.start()
    load_x(0, 0).start()
    load_x(0, 1).start()
    for load in small:
        load.start()

    barrier = pltpu.get_barrier_semaphore()

    def greet(i, carry):
        pl.semaphore_signal(
            barrier,
            inc=1,
            device_id={"seq": lax.rem(me + i, NS)},
            device_id_type=pl.DeviceIdType.MESH,
        )
        return carry

    for k in range(1, NH):
        pl.semaphore_signal(
            barrier,
            inc=1,
            device_id={"head": lax.rem(y + k, NH)},
            device_id_type=pl.DeviceIdType.MESH,
        )
    lax.fori_loop(1, NS, greet, 0)

    load_q(1).start()
    load_q(2).start()

    landed(row_v, small_sem.at[0])
    for load in small[3:]:
        load.wait()
    freq, q_gain, k_gain = row_v[0], row_v[1], row_v[2]
    for half in range(2):
        first, second = rotation(iota((HALF, HD), 0) + half * HALF, freq)
        tab_v[half, 0], tab_v[half, 1] = gained(first, second, q_gain)
        tab_v[half, 2], tab_v[half, 3] = gained(first, second, k_gain)
    load_q(3).start()

    def finish_query(half, t, count):
        slot = lax.rem(t + 5, 6)
        for b in range(TILE // HD):
            mine = f_v[t, 0:count, b * HD : (b + 1) * HD]
            for p in range(2):
                one = normrot(mine[p * HALF : (p + 1) * HALF], tab_v[half, 0], tab_v[half, 1])
                q_v[p, rows(slot * TILE + b * HD, HD), :] = one.astype(BF16)
            if half == 1:
                one = normrot(mine[LP : LP + ROWS], dq_first, dq_second)
                dq_v[rows((slot * 2 + b) * ROWS, ROWS), :] = one.astype(BF16)

    def multiply(half, after_keys=None):
        start = half * LP
        count = LP + ROWS if half else LP

        def tile(t, carry):
            if half == 0:
                landed(w_v.at[t], w_sem.at[t])

                @pl.when(t == 0)
                def _():
                    load_q(4).start()

                for jj in range(2):

                    @pl.when(t == 1 + jj)
                    def _(jj=jj):
                        for j in (2 * jj, 2 * jj + 1):
                            load_o(2, j).start()
                            load_o(3, j).start()

            if after_keys is not None:
                pl.when(t == 1)(after_keys)

            finish_query(half, lax.rem(t + 5, 6), count)
            f_v[t, 0:count, :] = dot(x_v[start : start + count, :], w_v[t])
            return carry

        lax.fori_loop(0, 1 + NT, tile, 0)
        finish_query(half, NT, count)

    def keys_values(half):
        for p in range(2):
            mine = f_v[0, p * HALF : (p + 1) * HALF, :]
            to = slice(p * LP + half * HALF, p * LP + (half + 1) * HALF)
            key = normrot(mine[:, 0:HD], tab_v[half, 2], tab_v[half, 3])
            kv_v[to, 0:HD] = key.astype(BF16)
            kv_v[to, HD : 2 * HD] = mine[:, HD : 2 * HD].astype(BF16)
        if half == 1:
            new = f_v[0, LP : LP + ROWS, :]
            dkv_v[...] = jnp.zeros_like(dkv_v)
            dkv_v[0:ROWS, 0:HD] = normrot(new[:, 0:HD], dk_first, dk_second).astype(BF16)
            dkv_v[0:ROWS, HD : 2 * HD] = new[:, HD : 2 * HD].astype(BF16)

    def attend(half, p):
        keys = (half + 1) * HALF
        at = iota((keys, HALF), 0)
        causal = at <= iota((keys, HALF), 1) + half * HALF
        bias = jnp.where(causal & (at < plen[2 * me + p]), 0.0, NEG)
        mine = rows(p * LP, keys) if half else pl.ds(pl.multiple_of(p * LP, LP), keys)
        scores = dot_nt(kv_v[mine, 0:HD], q_v[p, 0 : GROUP * HALF])
        scores = scores + jnp.concatenate([bias] * GROUP, axis=1)
        top = jnp.max(scores, axis=0, keepdims=True)
        expo = jnp.exp2((scores - top) * (SCALE * LOG2E))
        weights = expo * (1.0 / jnp.sum(expo, axis=0, keepdims=True))
        values = kv_v[mine, HD : 2 * HD].astype(F32).T.astype(BF16)
        mixed = dot(values, weights.astype(BF16))
        for head in range(GROUP):
            one = mixed[:, head * HALF : (head + 1) * HALF].T.astype(BF16)
            pa_v[half, rows(p * HALF, HALF), head * HD : (head + 1) * HD] = one

    def arrival(slot, i):
        return {0: 0, 1: 4, 2: 8, 5: 12, 3: 16, 4: 17}[slot] + (0 if slot in (3, 4) else i)

    def part(slot, i):
        to = right if slot in (0, 2, 3) else left
        return remote(
            part_s.at[slot, i],
            part_r.at[slot, i],
            part_ss.at[0],
            part_rs.at[arrival(slot, i)],
            head=to,
        )

    def project(half, k, p, jj):
        mine = pa_v[half, rows(p * HALF, HALF), :]
        return jnp.concatenate([dot(mine, wo_v[k, 2 * jj + b]) for b in range(2)], axis=1)

    def send(half, targets, p, jj, far=None):
        i = p * 2 + jj
        if far is not None:
            landed(part_r.at[far, i], part_rs.at[arrival(far, i)])
        values = [project(half, k, p, jj) for k, slot in targets]
        for (k, slot), value in zip(targets, values):
            if far is not None:
                value = value + part_r[far, i].astype(F32)
            part_s[slot, i] = value.astype(BF16)
            part(slot, i).start()

    def send_range(half, targets, first, last, far):
        def tile(i, carry):
            send(half, targets, i // 2, lax.rem(i, 2), far)
            return carry

        lax.fori_loop(first, last, tile, 0)

    def attend_and_send(half, targets, load):
        def prompt(p, carry):
            attend(half, p)

            def tile(jj, carry):
                if load:

                    @pl.when(p == 0)
                    def _():
                        landed(wo_v.at[2:4, pl.ds(2 * jj, 2)], wo_sem.at[jj])

                send(half, targets, p, jj)
                return carry

            lax.fori_loop(0, 2, tile, 0)
            return carry

        lax.fori_loop(0, 2, prompt, 0)

    landed(x_v.at[0:LP], x_sem.at[0])
    multiply(0)
    load_dec.start()
    load_x(1, 0).start()
    load_x(1, 1).start()
    for j in range(NT):
        load_o(1, j).start()
    for j in range(NT):
        load_o(0, j).start()
    load_cache.start()
    keys_values(0)
    pl.semaphore_wait(barrier, NS - 1 + NH - 1)
    attend_and_send(0, ((2, 0), (3, 4)), True)

    admitted = [adm[r] for r in range(SLOTS)]
    handed_len = [plen[jnp.maximum(admitted[r], 0)] for r in range(SLOTS)]
    is_new = [admitted[r] >= 0 for r in range(SLOTS)]
    eff_len = [jnp.where(is_new[r], handed_len[r], clen[r]) for r in range(SLOTS)]

    def per_slot(slot, values):
        picked = jnp.full(slot.shape, values[0], jnp.int32)
        for r in range(1, SLOTS):
            picked = jnp.where(slot == r, values[r], picked)
        return picked

    token = iota((ROWS, HD), 0)
    places = per_slot(token & (SLOTS - 1), eff_len) + (token >> 2)
    first, second = rotation(places, freq)
    dq_first, dq_second = gained(first, second, q_gain)
    dk_first, dk_second = gained(first, second, k_gain)

    landed(x_v.at[LP : 2 * LP], x_sem.at[1])
    load_dec.wait()
    x_v[2 * LP : 2 * LP + ROWS, :] = jnp.concatenate(
        [dec_v[t].astype(F32) for t in range(STEPS)], axis=0
    ).astype(BF16)
    def hand(i, way):
        other = lax.rem(me + i, NS)
        return remote(
            give_v.at[rows(other * 16, 16)],
            hand_v.at[rows(way * 16, 16)],
            seq_ss.at[0],
            seq_rs.at[0],
            seq=other,
        )

    def hand_over():
        keys_values(1)
        place = iota((2 * LP, 2 * LP), 0)
        source = (((place >> 3) & 1) << 8) + ((place & 7) << 5) + (place >> 4)
        pick = jnp.where(source == iota((2 * LP, 2 * LP), 1), 1.0, 0.0).astype(BF16)
        give_v[...] = dot(pick, kv_v[...]).astype(BF16)
        hand_v[rows(me * 16, 16), :] = give_v[rows(me * 16, 16), :]

        def hand_start(i, carry):
            hand(i, me).start()
            return carry

        lax.fori_loop(1, NS, hand_start, 0)

    multiply(1, hand_over)
    landed(wo_v.at[1], wo_sem.at[3])
    attend_and_send(1, ((1, 3), (2, 1)), False)
    load_cache.wait()

    landed(hand_v.at[0 : (NS - 1) * 16], seq_rs.at[0])
    save_hand = pltpu.make_async_copy(hand_v, handed, out_sem.at[0])
    save_hand.start()

    heads = GROUP * ROWS
    queries = dq_v[0:heads]

    def pieces():
        for r in range(SLOTS):
            slot = iota((heads, CACHE), 0) & (SLOTS - 1)
            at = (iota((heads, CACHE), 1) << 5) + me
            limit = jnp.where(is_new[r], 0, clen[r])
            yield (
                dot_nt(queries, cache_v[r * CACHE : (r + 1) * CACHE, 0:HD]),
                (slot == r) & (at < limit),
                cache_v[r * CACHE : (r + 1) * CACHE, HD : 2 * HD],
            )
        slot = iota((heads, 2 * LP), 0) & (SLOTS - 1)
        column = iota((heads, 2 * LP), 1)
        prompt = column >> 3
        at = ((column & 7) << 5) + me
        yield (
            dot_nt(queries, hand_v[:, 0:HD]),
            (prompt == per_slot(slot, admitted)) & (at < per_slot(slot, handed_len)),
            hand_v[:, HD : 2 * HD],
        )
        row = iota((heads, HD), 0)
        column = iota((heads, HD), 1) + jnp.where(me == 0, 0, ROWS)
        yield (
            dot_nt(queries, dkv_v[:, 0:HD]),
            ((row & 3) == (column & 3)) & ((column >> 2) <= ((row >> 2) & 3)) & (column < ROWS),
            dkv_v[:, HD : 2 * HD],
        )

    parts = [(jnp.where(mask, s, NEG), mask, v) for s, mask, v in pieces()]
    top = functools.reduce(jnp.maximum, [jnp.max(s, axis=-1, keepdims=True) for s, _, _ in parts])
    total = jnp.zeros((heads, 1), F32)
    acc = jnp.zeros((heads, HD), F32)
    for s, mask, v in parts:
        expo = jnp.where(mask, jnp.exp2((s - top) * (SCALE * LOG2E)), 0.0)
        total = total + jnp.sum(expo, axis=-1, keepdims=True)
        acc = acc + dot(expo.astype(BF16), v)
    state = jnp.where(iota((heads, HD), 1) < HD // 2, top, total)
    for q in range(heads // NS):
        soft_s[pl.ds(q, NS, stride=8), :] = acc[q * NS : (q + 1) * NS, :]
        soft_s[pl.ds(q + 4, NS, stride=8), :] = state[q * NS : (q + 1) * NS, :]
    soft_r[rows(me * 8, 8), :] = soft_s[rows(me * 8, 8), :]

    def soft(i, way):
        other = lax.rem(me + i, NS)
        return remote(
            soft_s.at[rows(other * 8, 8)],
            soft_r.at[rows(way * 8, 8)],
            seq_ss.at[1],
            seq_rs.at[1],
            seq=other,
        )

    def soft_start(i, carry):
        soft(i, me).start()
        return carry

    lax.fori_loop(1, NS, soft_start, 0)

    send_range(0, ((1, 2),), 0, 1, 0)

    landed(wo_v.at[0], wo_sem.at[2])

    def own(i, carry):
        for half in range(2):
            own_v[half, i] = project(half, 0, i // 2, lax.rem(i, 2))
        return carry

    lax.fori_loop(0, 4, own, 0)

    landed(soft_r.at[0 : (NS - 1) * 8], seq_rs.at[1])
    joined = []
    for q in range(heads // NS):
        sums = soft_r[pl.ds(q, NS, stride=8), :]
        both = soft_r[pl.ds(q + 4, NS, stride=8), :]
        tops = both[:, 0:1]
        weight = jnp.exp2((tops - jnp.max(tops, axis=0, keepdims=True)) * (SCALE * LOG2E))
        whole = jnp.sum(weight * both[:, HD // 2 : HD // 2 + 1], axis=0, keepdims=True)
        joined.append(jnp.sum(weight * sums, axis=0, keepdims=True) / whole)
    for q in range(heads // NS):
        join_s[q : q + 1, :] = joined[q]
        join_s[q + 4 : q + 5, :] = joined[q]
    join_r[rows(me * 8, 8), :] = join_s[...]

    def join(i, way):
        other = lax.rem(me + i, NS)
        return remote(
            join_s, join_r.at[rows(way * 8, 8)], seq_ss.at[2], seq_rs.at[2], seq=other
        )

    def join_start(i, carry):
        join(i, me).start()
        return carry

    lax.fori_loop(1, NS, join_start, 0)


    send_range(1, ((3, 5),), 0, 1, 1)
    landed(join_r.at[0 : (NS - 1) * 8], seq_rs.at[2])
    for head in range(GROUP):
        start = (head % 2) * ROWS * 8 + head // 2
        da_v[:, head * HD : (head + 1) * HD] = join_r[pl.ds(start, ROWS, stride=8), :].astype(BF16)

    block = lax.rem(me, NB)

    def dpart(k):
        return remote(
            dpart_s.at[k],
            dpart_r.at[k],
            dpart_ss.at[0],
            dpart_rs.at[0],
            head=lax.rem(y + k, NH),
        )

    def dec_project(k):
        lanes = rows(lax.rem(block, 2) * HD, HD)
        return dot(da_v[...], wo_v[k, block // 2, :, lanes])

    for k in (2, 1, 3):
        dpart_s[k] = dec_project(k).astype(BF16)
        dpart(k).start()
    dec_own = dec_project(0)

    def mixed(i, carry):
        send(0, ((1, 2),), i // 2, lax.rem(i, 2), 0)
        send(1, ((3, 5),), i // 2, lax.rem(i, 2), 1)
        return carry

    lax.fori_loop(1, 4, mixed, 0)

    landed(dpart_r.at[1:NH], dpart_rs.at[0])
    for k in (1, 3, 2):
        dec_own = dec_own + dpart_r[k].astype(F32)
    dcol_s[...] = dec_own
    dcol_r[block] = dec_own

    def dcol(i):
        other = lax.rem(block + i, NB)
        return remote(
            dcol_s, dcol_r.at[block], dcol_sem.at[0], dcol_sem.at[1], seq=me - block + other
        )

    def dcol_start(i, carry):
        dcol(i).start()
        return carry

    lax.fori_loop(1, NB, dcol_start, 0)
    landed(hand_v.at[0 : (NS - 1) * 16], seq_ss.at[0])
    landed(soft_r.at[0 : (NS - 1) * 8], seq_ss.at[1])
    landed(join_r.at[0 : (NS - 1) * 8], seq_ss.at[2])
    save_hand.wait()

    landed(part_r.at[3], part_rs.at[arrival(3, 0)])
    landed(part_r.at[4], part_rs.at[arrival(4, 0)])

    def finish(i, carry):
        landed(part_r.at[2, i], part_rs.at[arrival(2, i)])
        landed(part_r.at[5, i], part_rs.at[arrival(5, i)])
        p, jj = i // 2, lax.rem(i, 2)
        for half in range(2):
            value = own_v[half, i] + part_r[2 + half, i].astype(F32)
            out_v[half, i] = (value + part_r[4 + half, i].astype(F32)).astype(BF16)
            pltpu.make_async_copy(
                out_v.at[half, i],
                out.at[p, half * HALF : (half + 1) * HALF, rows(jj * WIDE, WIDE)],
                out_sem.at[2],
            ).start()
        return carry

    def save_decoded():
        landed(dcol_r.at[0 : NB - 1], dcol_sem.at[1])
        for b in range(NB):
            for t in range(STEPS):
                mine = dcol_r[b, t * SLOTS : (t + 1) * SLOTS, :]
                dout_v[t, :, b * HD : (b + 1) * HD] = mine.astype(BF16)
        pltpu.make_async_copy(dout_v, dec_out, out_sem.at[1]).start()

    lax.fori_loop(0, 3, finish, 0)
    save_decoded()
    lax.fori_loop(3, 4, finish, 0)

    landed(dpart_s.at[1:NH], dpart_ss.at[0])
    landed(part_s, part_ss.at[0])
    landed(out_v, out_sem.at[2])
    landed(dout_v, out_sem.at[1])
    landed(dcol_r.at[0 : NB - 1], dcol_sem.at[0])


def store(out_v, hand_v, dec_v, out, handed, dec_out, sem):
    copies = [
        pltpu.make_async_copy(source, target, sem.at[i])
        for i, (source, target) in enumerate([(out_v, out), (hand_v, handed), (dec_v, dec_out)])
    ]
    for copy in copies:
        copy.start()
    for copy in copies:
        copy.wait()


def local(
    prompts,
    prompt_len,
    admitted,
    cache_len,
    cache_kv,
    dec_tokens,
    w_query,
    w_key,
    w_value,
    w_out,
    q_gain,
    k_gain,
):
    half = HD // 2
    one = (THETA ** (-np.arange(half, dtype=np.float64) / half)).astype(np.float32)
    freq = jnp.asarray(np.concatenate([one, one])[None, :])
    hbm = pl.BlockSpec(memory_space=pl.ANY)
    dma = pltpu.SemaphoreType.DMA
    shapes = [(2, LP, WIDTH), (2 * LP, 2 * HD), (STEPS, SLOTS, WIDTH)]
    results = pl.pallas_call(
        kernel,
        out_shape=[pltpu.VMEM(shape, BF16) for shape in shapes],
        in_specs=[hbm] * 13,
        out_specs=[hbm] * 3,
        scratch_shapes=[
            pltpu.SMEM((2 * NS,), jnp.int32),
            pltpu.SMEM((SLOTS,), jnp.int32),
            pltpu.SMEM((SLOTS,), jnp.int32),
            pltpu.VMEM((3, 1, HD), F32),
            pltpu.VMEM((2 * LP + ROWS, D), BF16),
            pltpu.VMEM((STEPS, SLOTS, D), BF16),
            pltpu.VMEM((1 + NT, D, TILE), BF16),
            pltpu.VMEM((NH, NT, WIDTH, TILE), BF16),
            pltpu.VMEM((SLOTS * CACHE, 2 * HD), BF16),
            pltpu.VMEM((2, 4, HALF, HD), F32),
            pltpu.VMEM((2 + NT, LP + ROWS, TILE), F32),
            pltpu.VMEM((2 * LP, 2 * HD), BF16),
            pltpu.VMEM((2 * LP, 2 * HD), BF16),
            pltpu.VMEM((2 * LP, 2 * HD), BF16),
            pltpu.VMEM((2, (GROUP + 4) * HALF, HD), BF16),
            pltpu.VMEM(((GROUP + 4) * ROWS, HD), BF16),
            pltpu.VMEM((HD, 2 * HD), BF16),
            pltpu.VMEM((2, LP, WIDTH), BF16),
            pltpu.VMEM((6, 4, HALF, WIDE), BF16),
            pltpu.VMEM((6, 4, HALF, WIDE), BF16),
            pltpu.VMEM((2, 4, HALF, WIDE), F32),
            pltpu.VMEM((NS * 8, HD), F32),
            pltpu.VMEM((NS * 8, HD), F32),
            pltpu.VMEM((8, HD), F32),
            pltpu.VMEM((NS * 8, HD), F32),
            pltpu.VMEM((ROWS, WIDTH), BF16),
            pltpu.VMEM((NH, ROWS, HD), BF16),
            pltpu.VMEM((NH, ROWS, HD), BF16),
            pltpu.VMEM((ROWS, HD), F32),
            pltpu.VMEM((NB, ROWS, HD), F32),
            pltpu.VMEM((2, 4, HALF, WIDE), BF16),
            pltpu.VMEM((STEPS, SLOTS, WIDTH), BF16),
            dma((4,)),
            dma((2,)),
            dma((2,)),
            dma((1 + NT,)),
            dma((4,)),
            dma((3,)),
            dma((1,)),
            dma((18,)),
            dma((3,)),
            dma((3,)),
            dma((1,)),
            dma((1,)),
            dma((2,)),
        ],
        compiler_params=pltpu.CompilerParams(
            collective_id=0, has_side_effects=True, vmem_limit_bytes=56 * 2**20
        ),
        cost_estimate=pl.CostEstimate(
            flops=10_500_000_000, bytes_accessed=25_000_000, transcendentals=2_000_000
        ),
    )(
        prompt_len,
        admitted,
        cache_len,
        freq,
        q_gain[None, :],
        k_gain[None, :],
        prompts.reshape(2 * LP, D),
        dec_tokens,
        w_query,
        w_key,
        w_value,
        w_out,
        cache_kv.reshape(SLOTS * CACHE, 2 * HD),
    )
    out, handed, decoded = pl.pallas_call(
        store,
        out_shape=[jax.ShapeDtypeStruct(shape, BF16) for shape in shapes],
        in_specs=[hbm] * 3,
        out_specs=[hbm] * 3,
        scratch_shapes=[dma((3,))],
        compiler_params=pltpu.CompilerParams(vmem_limit_bytes=2**20),
    )(*results)
    return (
        out,
        handed.reshape(1, 2 * NS, EACH, 2 * HD),
        decoded,
    )


def solution(mesh):
    placed = (
        P("seq", None, None),
        P(),
        P(),
        P(),
        P("head", None, "seq", None),
        P(),
        P(None, "head"),
        P(None, "head"),
        P(None, "head"),
        P("head", None),
        P(),
        P(),
    )
    return jax.shard_map(
        local,
        mesh=mesh,
        in_specs=placed,
        out_specs=(P("seq", None, "head"), P("head", None, "seq", None), P(None, None, "head")),
        check_vma=False,
    )
```

```python
import functools

import jax
import jax.numpy as jnp
import numpy as np
from jax import lax
from jax.experimental import pallas as pl
from jax.experimental.pallas import tpu as pltpu
from jax.sharding import PartitionSpec as P

D = 4096
HD = 128
GROUP = 8
WIDTH = GROUP * HD
LP = 256
HALF = LP // 2
SLOTS = 4
STEPS = 4
ROWS = SLOTS * STEPS
CACHE = 512
NS = 32
NH = 4
EACH = LP // NS
EPS = 1e-06
THETA = 1000000.0
NEG = -1e30
SCALE = HD ** (-0.5)
LOG2E = 1.4426950408889634
TILE = 256
NT = WIDTH // TILE
WIDE = 2 * TILE
F32 = jnp.float32
BF16 = jnp.bfloat16


def dot(a, b):
    return jnp.dot(a, b, preferred_element_type=F32)


def dot_nt(a, b):
    return lax.dot_general(a, b, (((1,), (1,)), ((), ())), preferred_element_type=F32)


def iota(shape, dim):
    return lax.broadcasted_iota(jnp.int32, shape, dim)


def rotation(positions, freq):
    angle = positions.astype(F32) * freq
    sign = jnp.where(iota((1, HD), 1) < HD // 2, -1.0, 1.0)
    return jnp.cos(angle), jnp.sin(angle) * sign


def gained(cosine, sine, gain):
    return cosine * gain, sine * pltpu.roll(gain, HD // 2, 1)


def normrot(a, first, second):
    inverse = lax.rsqrt(jnp.mean(a * a, axis=-1, keepdims=True) + EPS)
    return (a * first + pltpu.roll(a, HD // 2, 1) * second) * inverse


def kernel(
    plen_ref,
    adm_ref,
    clen_ref,
    freq_ref,
    qg_ref,
    kg_ref,
    prompts,
    dec,
    wq,
    wk,
    wv,
    wo,
    cache,
    out,
    handed,
    dec_out,
    plen,
    adm,
    clen,
    row_v,
    x_v,
    dec_v,
    w_v,
    wo_v,
    cache_v,
    tab_v,
    f_v,
    kv_v,
    give_v,
    hand_v,
    q_v,
    dq_v,
    dkv_v,
    pa_v,
    part_s,
    part_r,
    own_v,
    soft_s,
    soft_r,
    join_s,
    join_r,
    dpart_s,
    dpart_r,
    out_v,
    dout_v,
    small_sem,
    x_sem,
    in_sem,
    w_sem,
    wo_sem,
    out_sem,
    part_ss,
    part_rs,
    seq_ss,
    seq_rs,
    dpart_ss,
    dpart_rs,
):
    y = lax.axis_index("head")
    me = lax.axis_index("seq")
    right = lax.rem(y + 1, NH)
    left = lax.rem(y + NH - 1, NH)

    def remote(src, dst, send, recv, **where):
        return pltpu.make_async_remote_copy(
            src_ref=src,
            dst_ref=dst,
            send_sem=send,
            recv_sem=recv,
            device_id=where,
            device_id_type=pl.DeviceIdType.MESH,
        )

    def landed(ref, sem):
        pltpu.make_async_copy(ref, ref, sem).wait()

    def rows(start, size):
        return pl.ds(pl.multiple_of(start, size), size)

    def load_x(half, p):
        source = p * LP + half * HALF
        target = half * LP + p * HALF
        return pltpu.make_async_copy(
            prompts.at[source : source + HALF], x_v.at[target : target + HALF], x_sem.at[half + (p if half == 0 else 1)]
        )

    small = [
        pltpu.make_async_copy(ref, to, small_sem.at[i])
        for ref, to, i in (
            (freq_ref, row_v.at[0], 0),
            (qg_ref, row_v.at[1], 0),
            (kg_ref, row_v.at[2], 0),
            (plen_ref, plen, 1),
            (adm_ref, adm, 2),
            (clen_ref, clen, 3),
        )
    ]
    load_k = pltpu.make_async_copy(wk, w_v.at[0, :, 0:HD], w_sem.at[0])
    load_v = pltpu.make_async_copy(wv, w_v.at[0, :, HD : 2 * HD], w_sem.at[0])
    load_dec = pltpu.make_async_copy(dec, dec_v, in_sem.at[0])
    load_cache = pltpu.make_async_copy(cache, cache_v, in_sem.at[1])

    def load_q(t):
        return pltpu.make_async_copy(wq.at[:, rows((t - 1) * TILE, TILE)], w_v.at[t], w_sem.at[t])

    def load_o(k, j):
        start = lax.rem(y + k, NH) * WIDTH + j * TILE
        sem = wo_sem.at[j // 2 if k in (2, 3) else 2 + k]
        return pltpu.make_async_copy(wo.at[:, rows(start, TILE)], wo_v.at[k, j], sem)

    load_k.start()
    load_x(0, 0).start()
    load_v.start()
    for load in small:
        load.start()
    load_q(1).start()

    barrier = pltpu.get_barrier_semaphore()

    def greet(i, carry):
        pl.semaphore_signal(
            barrier,
            inc=1,
            device_id={"seq": lax.rem(me + i, NS)},
            device_id_type=pl.DeviceIdType.MESH,
        )
        return carry

    for k in range(1, NH):
        pl.semaphore_signal(
            barrier,
            inc=1,
            device_id={"head": lax.rem(y + k, NH)},
            device_id_type=pl.DeviceIdType.MESH,
        )
    lax.fori_loop(1, NS, greet, 0)

    load_q(2).start()

    landed(row_v, small_sem.at[0])
    for load in small[3:]:
        load.wait()
    freq, q_gain, k_gain = row_v[0], row_v[1], row_v[2]
    for half in range(2):
        first, second = rotation(iota((HALF, HD), 0) + half * HALF, freq)
        tab_v[half, 0], tab_v[half, 1] = gained(first, second, q_gain)
        tab_v[half, 2], tab_v[half, 3] = gained(first, second, k_gain)
    load_q(3).start()

    def finish_query(half, p, t, base):
        slot = lax.rem(t + 5, 6)
        for b in range(TILE // HD):
            mine = f_v[t, base : base + HALF, b * HD : (b + 1) * HD]
            one = normrot(mine, tab_v[half, 0], tab_v[half, 1])
            q_v[p, rows(slot * TILE + b * HD, HD), :] = one.astype(BF16)

    def finish_token(t):
        slot = lax.rem(t + 5, 6)
        for b in range(TILE // HD):
            mine = f_v[t, LP : LP + ROWS, b * HD : (b + 1) * HD]
            one = normrot(mine, dq_first, dq_second)
            dq_v[rows((slot * 2 + b) * ROWS, ROWS), :] = one.astype(BF16)

    def keys_values(half, p, base):
        mine = f_v[0, base : base + HALF, :]
        to = rows(p * LP + half * HALF, HALF)
        kv_v[to, 0:HD] = normrot(mine[:, 0:HD], tab_v[half, 2], tab_v[half, 3]).astype(BF16)
        kv_v[to, HD : 2 * HD] = mine[:, HD : 2 * HD].astype(BF16)

    def multiply_first(p):
        def tile(t, carry):
            @pl.when(p == 0)
            def _():
                landed(w_v.at[t], w_sem.at[t])

                @pl.when(t == 0)
                def _():
                    load_q(4).start()

                for jj in range(2):

                    @pl.when(t == 1 + jj)
                    def _(jj=jj):
                        for j in (2 * jj, 2 * jj + 1):
                            load_o(2, j).start()
                            load_o(3, j).start()

                @pl.when(t == 2)
                def _():
                    load_x(0, 1).start()

            finish_query(0, p, lax.rem(t + 5, 6), 0)
            f_v[t, 0:HALF, :] = dot(x_v[rows(p * HALF, HALF), :], w_v[t])
            return carry

        lax.fori_loop(0, 1 + NT, tile, 0)
        finish_query(0, p, NT, 0)
        keys_values(0, p, 0)

    def multiply_second(after_keys):
        def finish(t):
            for p in range(2):
                finish_query(1, p, t, p * HALF)
            finish_token(t)

        def tile(t, carry):
            pl.when(t == 1)(after_keys)
            finish(lax.rem(t + 5, 6))
            f_v[t] = dot(x_v[LP : 2 * LP + ROWS, :], w_v[t])
            return carry

        lax.fori_loop(0, 1 + NT, tile, 0)
        finish(NT)

    def attend(half, p):
        keys = (half + 1) * HALF
        at = iota((keys, HALF), 0)
        causal = at <= iota((keys, HALF), 1) + half * HALF
        bias = jnp.where(causal & (at < plen[2 * me + p]), 0.0, NEG)
        mine = rows(p * LP, keys) if half else pl.ds(pl.multiple_of(p * LP, LP), keys)
        scores = dot_nt(kv_v[mine, 0:HD], q_v[p, 0 : GROUP * HALF])
        scores = scores + jnp.concatenate([bias] * GROUP, axis=1)
        top = jnp.max(scores, axis=0, keepdims=True)
        expo = jnp.exp2((scores - top) * (SCALE * LOG2E))
        weights = expo * (1.0 / jnp.sum(expo, axis=0, keepdims=True))
        values = kv_v[mine, HD : 2 * HD].astype(F32).T.astype(BF16)
        mixed = dot(values, weights.astype(BF16))
        for head in range(GROUP):
            one = mixed[:, head * HALF : (head + 1) * HALF].T.astype(BF16)
            pa_v[half, rows(p * HALF, HALF), head * HD : (head + 1) * HD] = one

    def arrival(slot, i):
        return {0: 0, 1: 1 + i // 3, 2: 3 + i // 3, 5: 5 + i // 3, 3: 7, 4: 8}[slot]

    def arrived(slot, first, last):
        landed(part_r.at[slot, first:last], part_rs.at[arrival(slot, first)])

    def part(slot, i):
        to = right if slot in (0, 2, 3) else left
        return remote(
            part_s.at[slot, i],
            part_r.at[slot, i],
            part_ss.at[0],
            part_rs.at[arrival(slot, i)],
            head=to,
        )

    def project(half, k, p, jj):
        mine = pa_v[half, rows(p * HALF, HALF), :]
        return jnp.concatenate([dot(mine, wo_v[k, 2 * jj + b]) for b in range(2)], axis=1)

    def send(half, targets, p, jj, far=None):
        i = p * 2 + jj
        values = [project(half, k, p, jj) for k, slot in targets]
        for (k, slot), value in zip(targets, values):
            if far is not None:
                value = value + part_r[far, i].astype(F32)
            part_s[slot, i] = value.astype(BF16)
            part(slot, i).start()

    def first_half(p, carry):
        @pl.when(p == 1)
        def _():
            landed(x_v.at[HALF:LP], x_sem.at[1])

        multiply_first(p)
        attend(0, p)

        def tile(jj, carry):
            @pl.when(p == 0)
            def _():
                landed(wo_v.at[2:4, pl.ds(2 * jj, 2)], wo_sem.at[jj])

                @pl.when(jj == 0)
                def _():
                    pl.semaphore_wait(barrier, NS - 1 + NH - 1)

            send(0, ((2, 0), (3, 4)), p, jj)
            return carry

        lax.fori_loop(0, 2, tile, 0)

        @pl.when(p == 0)
        def _():
            load_dec.start()
            load_x(1, 0).start()
            load_x(1, 1).start()
            for k in (1, 0):
                for j in range(NT):
                    load_o(k, j).start()
            load_cache.start()

        return carry

    def second_half(p):
        attend(1, p)

        def tile(jj, carry):
            send(1, ((1, 3), (2, 1)), p, jj)
            return carry

        lax.fori_loop(0, 2, tile, 0)

    landed(x_v.at[0:HALF], x_sem.at[0])
    lax.fori_loop(0, 2, first_half, 0)

    admitted = [adm[r] for r in range(SLOTS)]
    handed_len = [plen[jnp.maximum(admitted[r], 0)] for r in range(SLOTS)]
    is_new = [admitted[r] >= 0 for r in range(SLOTS)]
    eff_len = [jnp.where(is_new[r], handed_len[r], clen[r]) for r in range(SLOTS)]

    def per_slot(slot, values):
        picked = jnp.full(slot.shape, values[0], jnp.int32)
        for r in range(1, SLOTS):
            picked = jnp.where(slot == r, values[r], picked)
        return picked

    token = iota((ROWS, HD), 0)
    places = per_slot(token & (SLOTS - 1), eff_len) + (token >> 2)
    first, second = rotation(places, freq)
    dq_first, dq_second = gained(first, second, q_gain)
    dk_first, dk_second = gained(first, second, k_gain)

    landed(x_v.at[LP : 2 * LP], x_sem.at[2])
    load_dec.wait()
    x_v[2 * LP : 2 * LP + ROWS, :] = jnp.concatenate(
        [dec_v[t].astype(F32) for t in range(STEPS)], axis=0
    ).astype(BF16)
    def hand(i, way):
        other = lax.rem(me + i, NS)
        return remote(
            give_v.at[rows(other * 16, 16)],
            hand_v.at[rows(way * 16, 16)],
            seq_ss.at[0],
            seq_rs.at[0],
            seq=other,
        )

    def hand_over():
        for p in range(2):
            keys_values(1, p, p * HALF)
        new = f_v[0, LP : LP + ROWS, :]
        dkv_v[...] = jnp.zeros_like(dkv_v)
        dkv_v[0:ROWS, 0:HD] = normrot(new[:, 0:HD], dk_first, dk_second).astype(BF16)
        dkv_v[0:ROWS, HD : 2 * HD] = new[:, HD : 2 * HD].astype(BF16)
        place = iota((2 * LP, 2 * LP), 0)
        source = (((place >> 3) & 1) << 8) + ((place & 7) << 5) + (place >> 4)
        pick = jnp.where(source == iota((2 * LP, 2 * LP), 1), 1.0, 0.0).astype(BF16)
        give_v[...] = dot(pick, kv_v[...]).astype(BF16)
        hand_v[rows(me * 16, 16), :] = give_v[rows(me * 16, 16), :]

        def hand_start(i, carry):
            hand(i, me).start()
            return carry

        lax.fori_loop(1, NS, hand_start, 0)

    multiply_second(hand_over)
    landed(wo_v.at[1], wo_sem.at[3])
    second_half(0)
    load_cache.wait()

    landed(hand_v.at[0 : (NS - 1) * 16], seq_rs.at[0])
    save_hand = pltpu.make_async_copy(hand_v, handed, out_sem.at[0])
    save_hand.start()

    heads = GROUP * ROWS
    queries = dq_v[0:heads]

    def pieces():
        for r in range(SLOTS):
            slot = iota((heads, CACHE), 0) & (SLOTS - 1)
            at = (iota((heads, CACHE), 1) << 5) + me
            limit = jnp.where(is_new[r], 0, clen[r])
            yield (
                dot_nt(queries, cache_v[r * CACHE : (r + 1) * CACHE, 0:HD]),
                (slot == r) & (at < limit),
                cache_v[r * CACHE : (r + 1) * CACHE, HD : 2 * HD],
            )
        slot = iota((heads, 2 * LP), 0) & (SLOTS - 1)
        column = iota((heads, 2 * LP), 1)
        prompt = column >> 3
        at = ((column & 7) << 5) + me
        yield (
            dot_nt(queries, hand_v[:, 0:HD]),
            (prompt == per_slot(slot, admitted)) & (at < per_slot(slot, handed_len)),
            hand_v[:, HD : 2 * HD],
        )
        row = iota((heads, HD), 0)
        column = iota((heads, HD), 1) + jnp.where(me == 0, 0, ROWS)
        yield (
            dot_nt(queries, dkv_v[:, 0:HD]),
            ((row & 3) == (column & 3)) & ((column >> 2) <= ((row >> 2) & 3)) & (column < ROWS),
            dkv_v[:, HD : 2 * HD],
        )

    parts = [(jnp.where(mask, s, NEG), mask, v) for s, mask, v in pieces()]
    top = functools.reduce(jnp.maximum, [jnp.max(s, axis=-1, keepdims=True) for s, _, _ in parts])
    total = jnp.zeros((heads, 1), F32)
    acc = jnp.zeros((heads, HD), F32)
    for s, mask, v in parts:
        expo = jnp.where(mask, jnp.exp2((s - top) * (SCALE * LOG2E)), 0.0)
        total = total + jnp.sum(expo, axis=-1, keepdims=True)
        acc = acc + dot(expo.astype(BF16), v)
    state = jnp.where(iota((heads, HD), 1) < HD // 2, top, total)
    for head in range(GROUP):
        at = pl.ds(8 * (head // 4) + head % 4, ROWS, stride=16)
        soft_s[at, :] = acc[head * ROWS : (head + 1) * ROWS, :]
        also = pl.ds(8 * (head // 4) + head % 4 + 4, ROWS, stride=16)
        soft_s[also, :] = state[head * ROWS : (head + 1) * ROWS, :]
    soft_r[rows(me * 8, 8), :] = soft_s[rows(me * 8, 8), :]

    def soft(i, way):
        other = lax.rem(me + i, NS)
        return remote(
            soft_s.at[rows(other * 8, 8)],
            soft_r.at[rows(way * 8, 8)],
            seq_ss.at[1],
            seq_rs.at[1],
            seq=other,
        )

    def soft_start(i, carry):
        soft(i, me).start()
        return carry

    lax.fori_loop(1, NS, soft_start, 0)
    second_half(1)

    landed(wo_v.at[0], wo_sem.at[2])

    def own(i, carry):
        for half in range(2):
            own_v[half, i] = project(half, 0, i // 2, lax.rem(i, 2))
        return carry

    lax.fori_loop(0, 4, own, 0)

    landed(soft_r.at[0 : (NS - 1) * 8], seq_rs.at[1])
    joined = []
    for q in range(heads // NS):
        sums = soft_r[pl.ds(q, NS, stride=8), :]
        both = soft_r[pl.ds(q + 4, NS, stride=8), :]
        tops = both[:, 0:1]
        weight = jnp.exp2((tops - jnp.max(tops, axis=0, keepdims=True)) * (SCALE * LOG2E))
        whole = jnp.sum(weight * both[:, HD // 2 : HD // 2 + 1], axis=0, keepdims=True)
        joined.append((jnp.sum(weight * sums, axis=0, keepdims=True) / whole).astype(BF16))
    token_row = jnp.broadcast_to(jnp.concatenate(joined, axis=1).astype(F32), (16, WIDTH // 2))
    token_row = token_row.astype(BF16)

    core = lax.rem(me, 2)

    def dpart(k, e):
        return remote(
            dpart_s.at[2 * k + e],
            dpart_r.at[2 * k + e],
            dpart_ss.at[0],
            dpart_rs.at[0],
            head=lax.rem(y + k, NH),
            seq=me + e * (1 - 2 * core),
        )

    for k in (2, 1, 3, 0):
        for e in range(2):
            side = core + e * (1 - 2 * core)
            for b in range(2):
                tile = wo_v[k, 2 * side + b, rows(core * (WIDTH // 2), WIDTH // 2), :]
                value = dot(token_row, tile)[0:1]
                for lanes in range(2):
                    one = value[:, lanes * HD : (lanes + 1) * HD]
                    row = 2 * b + lanes
                    dpart_s[2 * k + e, row : row + 1, :] = one
                    dpart_s[2 * k + e, row + 4 : row + 5, :] = one
            if (k, e) != (0, 0):
                dpart(k, e).start()

    arrived(0, 0, 4)
    arrived(1, 0, 3)

    def mixed(i, carry):
        send(0, ((1, 2),), i // 2, lax.rem(i, 2), 0)
        send(1, ((3, 5),), i // 2, lax.rem(i, 2), 1)
        return carry

    lax.fori_loop(0, 3, mixed, 0)
    arrived(1, 3, 4)
    mixed(3, 0)

    landed(dpart_r.at[1 : 2 * NH], dpart_rs.at[0])
    total = dpart_s[0]
    for n in range(1, 2 * NH):
        total = total + dpart_r[n]
    join_s[...] = total
    join_r[rows(me * 8, 8), :] = total

    def join(i, way):
        other = lax.rem(me + i, NS)
        return remote(join_s, join_r.at[rows(way * 8, 8)], seq_ss.at[2], seq_rs.at[2], seq=other)

    def join_start(i, carry):
        join(i, me).start()
        return carry

    lax.fori_loop(1, NS, join_start, 0)

    landed(hand_v.at[0 : (NS - 1) * 16], seq_ss.at[0])
    landed(soft_r.at[0 : (NS - 1) * 8], seq_ss.at[1])
    save_hand.wait()

    arrived(3, 0, 4)
    arrived(4, 0, 4)

    def finish(i, carry):
        p, jj = i // 2, lax.rem(i, 2)
        for half in range(2):
            value = own_v[half, i] + part_r[2 + half, i].astype(F32)
            out_v[half, i] = (value + part_r[4 + half, i].astype(F32)).astype(BF16)
            pltpu.make_async_copy(
                out_v.at[half, i],
                out.at[p, half * HALF : (half + 1) * HALF, rows(jj * WIDE, WIDE)],
                out_sem.at[2],
            ).start()
        return carry

    def save_decoded():
        landed(join_r.at[0 : (NS - 1) * 8], seq_rs.at[2])
        for b in range(GROUP):
            mine = join_r[pl.ds(8 * (b // 4) + b % 4, ROWS, stride=16), :]
            for t in range(STEPS):
                one = mine[t * SLOTS : (t + 1) * SLOTS, :]
                dout_v[t, :, b * HD : (b + 1) * HD] = one.astype(BF16)
        pltpu.make_async_copy(dout_v, dec_out, out_sem.at[1]).start()

    arrived(2, 0, 3)
    arrived(5, 0, 3)
    lax.fori_loop(0, 3, finish, 0)
    save_decoded()
    arrived(2, 3, 4)
    arrived(5, 3, 4)
    finish(3, 0)

    landed(dpart_s.at[1 : 2 * NH], dpart_ss.at[0])
    landed(join_r.at[0 : (NS - 1) * 8], seq_ss.at[2])
    landed(part_s, part_ss.at[0])
    landed(out_v, out_sem.at[2])
    landed(dout_v, out_sem.at[1])


def store(out_v, hand_v, dec_v, out, handed, dec_out, sem):
    copies = [
        pltpu.make_async_copy(source, target, sem.at[i])
        for i, (source, target) in enumerate([(out_v, out), (hand_v, handed), (dec_v, dec_out)])
    ]
    for copy in copies:
        copy.start()
    for copy in copies:
        copy.wait()


def local(
    prompts,
    prompt_len,
    admitted,
    cache_len,
    cache_kv,
    dec_tokens,
    w_query,
    w_key,
    w_value,
    w_out,
    q_gain,
    k_gain,
):
    half = HD // 2
    one = (THETA ** (-np.arange(half, dtype=np.float64) / half)).astype(np.float32)
    freq = jnp.asarray(np.concatenate([one, one])[None, :])
    hbm = pl.BlockSpec(memory_space=pl.ANY)
    dma = pltpu.SemaphoreType.DMA
    shapes = [(2, LP, WIDTH), (2 * LP, 2 * HD), (STEPS, SLOTS, WIDTH)]
    results = pl.pallas_call(
        kernel,
        out_shape=[pltpu.VMEM(shape, BF16) for shape in shapes],
        in_specs=[hbm] * 13,
        out_specs=[hbm] * 3,
        scratch_shapes=[
            pltpu.SMEM((2 * NS,), jnp.int32),
            pltpu.SMEM((SLOTS,), jnp.int32),
            pltpu.SMEM((SLOTS,), jnp.int32),
            pltpu.VMEM((3, 1, HD), F32),
            pltpu.VMEM((2 * LP + ROWS, D), BF16),
            pltpu.VMEM((STEPS, SLOTS, D), BF16),
            pltpu.VMEM((1 + NT, D, TILE), BF16),
            pltpu.VMEM((NH, NT, WIDTH, TILE), BF16),
            pltpu.VMEM((SLOTS * CACHE, 2 * HD), BF16),
            pltpu.VMEM((2, 4, HALF, HD), F32),
            pltpu.VMEM((2 + NT, LP + ROWS, TILE), F32),
            pltpu.VMEM((2 * LP, 2 * HD), BF16),
            pltpu.VMEM((2 * LP, 2 * HD), BF16),
            pltpu.VMEM((2 * LP, 2 * HD), BF16),
            pltpu.VMEM((2, (GROUP + 4) * HALF, HD), BF16),
            pltpu.VMEM(((GROUP + 4) * ROWS, HD), BF16),
            pltpu.VMEM((HD, 2 * HD), BF16),
            pltpu.VMEM((2, LP, WIDTH), BF16),
            pltpu.VMEM((6, 4, HALF, WIDE), BF16),
            pltpu.VMEM((6, 4, HALF, WIDE), BF16),
            pltpu.VMEM((2, 4, HALF, WIDE), F32),
            pltpu.VMEM((NS * 8, HD), F32),
            pltpu.VMEM((NS * 8, HD), F32),
            pltpu.VMEM((8, HD), F32),
            pltpu.VMEM((NS * 8, HD), F32),
            pltpu.VMEM((2 * NH, 8, HD), F32),
            pltpu.VMEM((2 * NH, 8, HD), F32),
            pltpu.VMEM((2, 4, HALF, WIDE), BF16),
            pltpu.VMEM((STEPS, SLOTS, WIDTH), BF16),
            dma((4,)),
            dma((3,)),
            dma((2,)),
            dma((1 + NT,)),
            dma((4,)),
            dma((3,)),
            dma((1,)),
            dma((9,)),
            dma((3,)),
            dma((3,)),
            dma((1,)),
            dma((1,)),
        ],
        compiler_params=pltpu.CompilerParams(
            collective_id=0, has_side_effects=True, vmem_limit_bytes=56 * 2**20
        ),
        cost_estimate=pl.CostEstimate(
            flops=10_500_000_000, bytes_accessed=25_000_000, transcendentals=2_000_000
        ),
    )(
        prompt_len,
        admitted,
        cache_len,
        freq,
        q_gain[None, :],
        k_gain[None, :],
        prompts.reshape(2 * LP, D),
        dec_tokens,
        w_query,
        w_key,
        w_value,
        w_out,
        cache_kv.reshape(SLOTS * CACHE, 2 * HD),
    )
    out, handed, decoded = pl.pallas_call(
        store,
        out_shape=[jax.ShapeDtypeStruct(shape, BF16) for shape in shapes],
        in_specs=[hbm] * 3,
        out_specs=[hbm] * 3,
        scratch_shapes=[dma((3,))],
        compiler_params=pltpu.CompilerParams(vmem_limit_bytes=2**20),
    )(*results)
    return (
        out,
        handed.reshape(1, 2 * NS, EACH, 2 * HD),
        decoded,
    )


def solution(mesh):
    placed = (
        P("seq", None, None),
        P(),
        P(),
        P(),
        P("head", None, "seq", None),
        P(),
        P(None, "head"),
        P(None, "head"),
        P(None, "head"),
        P("head", None),
        P(),
        P(),
    )
    return jax.shard_map(
        local,
        mesh=mesh,
        in_specs=placed,
        out_specs=(P("seq", None, "head"), P("head", None, "seq", None), P(None, None, "head")),
        check_vma=False,
    )
```

```python
import functools

import jax
import jax.numpy as jnp
import numpy as np
from jax import lax
from jax.experimental import pallas as pl
from jax.experimental.pallas import tpu as pltpu
from jax.sharding import PartitionSpec as P

D = 4096
HD = 128
GROUP = 8
WIDTH = GROUP * HD
LP = 256
HALF = LP // 2
SLOTS = 4
STEPS = 4
ROWS = SLOTS * STEPS
CACHE = 512
NS = 32
NH = 4
EACH = LP // NS
EPS = 1e-06
THETA = 1000000.0
NEG = -1e30
SCALE = HD ** (-0.5)
LOG2E = 1.4426950408889634
TILE = 256
NT = WIDTH // TILE
WIDE = 2 * TILE
F32 = jnp.float32
BF16 = jnp.bfloat16


def dot(a, b):
    return jnp.dot(a, b, preferred_element_type=F32)


def dot_nt(a, b):
    return lax.dot_general(a, b, (((1,), (1,)), ((), ())), preferred_element_type=F32)


def iota(shape, dim):
    return lax.broadcasted_iota(jnp.int32, shape, dim)


def rotation(positions, freq):
    angle = positions.astype(F32) * freq
    sign = jnp.where(iota((1, HD), 1) < HD // 2, -1.0, 1.0)
    return jnp.cos(angle), jnp.sin(angle) * sign


def gained(cosine, sine, gain):
    return cosine * gain, sine * pltpu.roll(gain, HD // 2, 1)


def normrot(a, first, second):
    inverse = lax.rsqrt(jnp.mean(a * a, axis=-1, keepdims=True) + EPS)
    return (a * first + pltpu.roll(a, HD // 2, 1) * second) * inverse


def kernel(
    plen_ref,
    adm_ref,
    clen_ref,
    freq_ref,
    qg_ref,
    kg_ref,
    prompts,
    dec,
    wq,
    wk,
    wv,
    wo,
    cache,
    out,
    handed,
    dec_out,
    plen,
    adm,
    clen,
    row_v,
    x_v,
    dec_v,
    w_v,
    wo_v,
    cache_v,
    tab_v,
    f_v,
    kv_v,
    give_v,
    hand_v,
    q_v,
    dq_v,
    dkv_v,
    pa_v,
    part_s,
    part_r,
    own_v,
    soft_s,
    soft_r,
    join_s,
    join_r,
    dpart_s,
    dpart_r,
    small_sem,
    x_sem,
    in_sem,
    w_sem,
    wo_sem,
    out_sem,
    part_ss,
    part_rs,
    seq_ss,
    seq_rs,
    dpart_ss,
    dpart_rs,
):
    y = lax.axis_index("head")
    me = lax.axis_index("seq")
    right = lax.rem(y + 1, NH)
    left = lax.rem(y + NH - 1, NH)

    def remote(src, dst, send, recv, **where):
        return pltpu.make_async_remote_copy(
            src_ref=src,
            dst_ref=dst,
            send_sem=send,
            recv_sem=recv,
            device_id=where,
            device_id_type=pl.DeviceIdType.MESH,
        )

    def landed(ref, sem):
        pltpu.make_async_copy(ref, ref, sem).wait()

    def rows(start, size):
        return pl.ds(pl.multiple_of(start, size), size)

    def load_x(half, p):
        source = p * LP + half * HALF
        target = half * LP + p * HALF
        return pltpu.make_async_copy(
            prompts.at[source : source + HALF], x_v.at[target : target + HALF], x_sem.at[half + (p if half == 0 else 1)]
        )

    small = [
        pltpu.make_async_copy(ref, to, small_sem.at[i])
        for ref, to, i in (
            (freq_ref, row_v.at[0], 0),
            (qg_ref, row_v.at[1], 0),
            (kg_ref, row_v.at[2], 0),
            (plen_ref, plen, 1),
            (adm_ref, adm, 2),
            (clen_ref, clen, 3),
        )
    ]
    load_k = pltpu.make_async_copy(wk, w_v.at[0, :, 0:HD], w_sem.at[0])
    load_v = pltpu.make_async_copy(wv, w_v.at[0, :, HD : 2 * HD], w_sem.at[0])
    load_dec = pltpu.make_async_copy(dec, dec_v, in_sem.at[0])
    load_cache = pltpu.make_async_copy(cache, cache_v, in_sem.at[1])

    def load_q(t):
        return pltpu.make_async_copy(wq.at[:, rows((t - 1) * TILE, TILE)], w_v.at[t], w_sem.at[t])

    def load_o(k, j):
        start = lax.rem(y + k, NH) * WIDTH + j * TILE
        sem = wo_sem.at[j // 2 if k in (2, 3) else 2 + k]
        return pltpu.make_async_copy(wo.at[:, rows(start, TILE)], wo_v.at[k, j], sem)

    load_k.start()
    load_x(0, 0).start()
    load_v.start()
    for load in small:
        load.start()
    load_q(1).start()

    barrier = pltpu.get_barrier_semaphore()

    def greet(i, carry):
        pl.semaphore_signal(
            barrier,
            inc=1,
            device_id={"seq": lax.rem(me + i, NS)},
            device_id_type=pl.DeviceIdType.MESH,
        )
        return carry

    for k in range(1, NH):
        pl.semaphore_signal(
            barrier,
            inc=1,
            device_id={"head": lax.rem(y + k, NH)},
            device_id_type=pl.DeviceIdType.MESH,
        )
    lax.fori_loop(1, NS, greet, 0)

    load_q(2).start()

    landed(row_v, small_sem.at[0])
    for load in small[3:]:
        load.wait()
    freq, q_gain, k_gain = row_v[0], row_v[1], row_v[2]
    for half in range(2):
        first, second = rotation(iota((HALF, HD), 0) + half * HALF, freq)
        tab_v[half, 0], tab_v[half, 1] = gained(first, second, q_gain)
        tab_v[half, 2], tab_v[half, 3] = gained(first, second, k_gain)
    load_q(3).start()

    def finish_query(half, p, t, base):
        slot = lax.rem(t + 5, 6)
        for b in range(TILE // HD):
            mine = f_v[t, base : base + HALF, b * HD : (b + 1) * HD]
            one = normrot(mine, tab_v[half, 0], tab_v[half, 1])
            q_v[p, rows(slot * TILE + b * HD, HD), :] = one.astype(BF16)

    def finish_token(t):
        slot = lax.rem(t + 5, 6)
        for b in range(TILE // HD):
            mine = f_v[t, LP : LP + ROWS, b * HD : (b + 1) * HD]
            one = normrot(mine, dq_first, dq_second)
            dq_v[rows((slot * 2 + b) * ROWS, ROWS), :] = one.astype(BF16)

    def keys_values(half, p, base):
        mine = f_v[0, base : base + HALF, :]
        to = rows(p * LP + half * HALF, HALF)
        kv_v[to, 0:HD] = normrot(mine[:, 0:HD], tab_v[half, 2], tab_v[half, 3]).astype(BF16)
        kv_v[to, HD : 2 * HD] = mine[:, HD : 2 * HD].astype(BF16)

    def multiply_first(p):
        def tile(t, carry):
            @pl.when(p == 0)
            def _():
                landed(w_v.at[t], w_sem.at[t])

                @pl.when(t == 0)
                def _():
                    load_q(4).start()

                for jj in range(2):

                    @pl.when(t == 1 + jj)
                    def _(jj=jj):
                        for j in (2 * jj, 2 * jj + 1):
                            load_o(2, j).start()
                            load_o(3, j).start()

                @pl.when(t == 2)
                def _():
                    load_x(0, 1).start()

            finish_query(0, p, lax.rem(t + 5, 6), 0)
            f_v[t, 0:HALF, :] = dot(x_v[rows(p * HALF, HALF), :], w_v[t])
            return carry

        lax.fori_loop(0, 1 + NT, tile, 0)
        finish_query(0, p, NT, 0)
        keys_values(0, p, 0)

    def multiply_second(after_keys):
        def finish(t):
            for p in range(2):
                finish_query(1, p, t, p * HALF)
            finish_token(t)

        def tile(t, carry):
            pl.when(t == 1)(after_keys)
            finish(lax.rem(t + 5, 6))
            f_v[t] = dot(x_v[LP : 2 * LP + ROWS, :], w_v[t])
            return carry

        lax.fori_loop(0, 1 + NT, tile, 0)
        finish(NT)

    def attend(half, p):
        keys = (half + 1) * HALF
        at = iota((keys, HALF), 0)
        causal = at <= iota((keys, HALF), 1) + half * HALF
        bias = jnp.where(causal & (at < plen[2 * me + p]), 0.0, NEG)
        mine = rows(p * LP, keys) if half else pl.ds(pl.multiple_of(p * LP, LP), keys)
        scores = dot_nt(kv_v[mine, 0:HD], q_v[p, 0 : GROUP * HALF])
        scores = scores + jnp.concatenate([bias] * GROUP, axis=1)
        top = jnp.max(scores, axis=0, keepdims=True)
        expo = jnp.exp2((scores - top) * (SCALE * LOG2E))
        weights = expo * (1.0 / jnp.sum(expo, axis=0, keepdims=True))
        values = kv_v[mine, HD : 2 * HD].astype(F32).T.astype(BF16)
        mixed = dot(values, weights.astype(BF16))
        for head in range(GROUP):
            one = mixed[:, head * HALF : (head + 1) * HALF].T.astype(BF16)
            pa_v[half, rows(p * HALF, HALF), head * HD : (head + 1) * HD] = one

    def arrival(slot, i):
        return {0: 0, 1: 1 + i // 3, 2: 3 + i // 3, 5: 5 + i // 3, 3: 7, 4: 8}[slot]

    def arrived(slot, first, last):
        landed(part_r.at[slot, first:last], part_rs.at[arrival(slot, first)])

    def part(slot, i):
        to = right if slot in (0, 2, 3) else left
        return remote(
            part_s.at[slot, i],
            part_r.at[slot, i],
            part_ss.at[0],
            part_rs.at[arrival(slot, i)],
            head=to,
        )

    def project(half, k, p, jj):
        mine = pa_v[half, rows(p * HALF, HALF), :]
        return jnp.concatenate([dot(mine, wo_v[k, 2 * jj + b]) for b in range(2)], axis=1)

    def send(half, targets, p, jj, far=None):
        i = p * 2 + jj
        values = [project(half, k, p, jj) for k, slot in targets]
        for (k, slot), value in zip(targets, values):
            if far is not None:
                value = value + part_r[far, i].astype(F32)
            part_s[slot, i] = value.astype(BF16)
            part(slot, i).start()

    def first_half(p, carry):
        @pl.when(p == 1)
        def _():
            landed(x_v.at[HALF:LP], x_sem.at[1])

        multiply_first(p)
        attend(0, p)

        def tile(jj, carry):
            @pl.when(p == 0)
            def _():
                landed(wo_v.at[2:4, pl.ds(2 * jj, 2)], wo_sem.at[jj])

                @pl.when(jj == 0)
                def _():
                    pl.semaphore_wait(barrier, NS - 1 + NH - 1)

            send(0, ((2, 0), (3, 4)), p, jj)
            return carry

        lax.fori_loop(0, 2, tile, 0)

        @pl.when(p == 0)
        def _():
            load_dec.start()
            load_x(1, 0).start()
            load_x(1, 1).start()
            for k in (1, 0):
                for j in range(NT):
                    load_o(k, j).start()
            load_cache.start()

        return carry

    def second_half(p):
        attend(1, p)

        def tile(jj, carry):
            send(1, ((1, 3), (2, 1)), p, jj)
            return carry

        lax.fori_loop(0, 2, tile, 0)

    landed(x_v.at[0:HALF], x_sem.at[0])
    lax.fori_loop(0, 2, first_half, 0)

    admitted = [adm[r] for r in range(SLOTS)]
    handed_len = [plen[jnp.maximum(admitted[r], 0)] for r in range(SLOTS)]
    is_new = [admitted[r] >= 0 for r in range(SLOTS)]
    eff_len = [jnp.where(is_new[r], handed_len[r], clen[r]) for r in range(SLOTS)]

    def per_slot(slot, values):
        picked = jnp.full(slot.shape, values[0], jnp.int32)
        for r in range(1, SLOTS):
            picked = jnp.where(slot == r, values[r], picked)
        return picked

    token = iota((ROWS, HD), 0)
    places = per_slot(token & (SLOTS - 1), eff_len) + (token >> 2)
    first, second = rotation(places, freq)
    dq_first, dq_second = gained(first, second, q_gain)
    dk_first, dk_second = gained(first, second, k_gain)

    landed(x_v.at[LP : 2 * LP], x_sem.at[2])
    load_dec.wait()
    x_v[2 * LP : 2 * LP + ROWS, :] = jnp.concatenate(
        [dec_v[t].astype(F32) for t in range(STEPS)], axis=0
    ).astype(BF16)
    def hand(i, way):
        other = lax.rem(me + i, NS)
        return remote(
            give_v.at[rows(other * 16, 16)],
            hand_v.at[rows(way * 16, 16)],
            seq_ss.at[0],
            seq_rs.at[0],
            seq=other,
        )

    def hand_over():
        for p in range(2):
            keys_values(1, p, p * HALF)
        new = f_v[0, LP : LP + ROWS, :]
        dkv_v[...] = jnp.zeros_like(dkv_v)
        dkv_v[0:ROWS, 0:HD] = normrot(new[:, 0:HD], dk_first, dk_second).astype(BF16)
        dkv_v[0:ROWS, HD : 2 * HD] = new[:, HD : 2 * HD].astype(BF16)
        place = iota((2 * LP, 2 * LP), 0)
        source = (((place >> 3) & 1) << 8) + ((place & 7) << 5) + (place >> 4)
        pick = jnp.where(source == iota((2 * LP, 2 * LP), 1), 1.0, 0.0).astype(BF16)
        give_v[...] = dot(pick, kv_v[...]).astype(BF16)
        hand_v[rows(me * 16, 16), :] = give_v[rows(me * 16, 16), :]

        def hand_start(i, carry):
            hand(i, me).start()
            return carry

        lax.fori_loop(1, NS, hand_start, 0)

    multiply_second(hand_over)
    landed(wo_v.at[1], wo_sem.at[3])
    second_half(0)
    load_cache.wait()

    landed(hand_v.at[0 : (NS - 1) * 16], seq_rs.at[0])
    save_hand = pltpu.make_async_copy(hand_v, handed, out_sem.at[0])
    save_hand.start()

    heads = GROUP * ROWS
    queries = dq_v[0:heads]

    def pieces():
        for r in range(SLOTS):
            slot = iota((heads, CACHE), 0) & (SLOTS - 1)
            at = (iota((heads, CACHE), 1) << 5) + me
            limit = jnp.where(is_new[r], 0, clen[r])
            yield (
                dot_nt(queries, cache_v[r * CACHE : (r + 1) * CACHE, 0:HD]),
                (slot == r) & (at < limit),
                cache_v[r * CACHE : (r + 1) * CACHE, HD : 2 * HD],
            )
        slot = iota((heads, 2 * LP), 0) & (SLOTS - 1)
        column = iota((heads, 2 * LP), 1)
        prompt = column >> 3
        at = ((column & 7) << 5) + me
        yield (
            dot_nt(queries, hand_v[:, 0:HD]),
            (prompt == per_slot(slot, admitted)) & (at < per_slot(slot, handed_len)),
            hand_v[:, HD : 2 * HD],
        )
        row = iota((heads, HD), 0)
        column = iota((heads, HD), 1) + jnp.where(me == 0, 0, ROWS)
        yield (
            dot_nt(queries, dkv_v[:, 0:HD]),
            ((row & 3) == (column & 3)) & ((column >> 2) <= ((row >> 2) & 3)) & (column < ROWS),
            dkv_v[:, HD : 2 * HD],
        )

    parts = [(jnp.where(mask, s, NEG), mask, v) for s, mask, v in pieces()]
    top = functools.reduce(jnp.maximum, [jnp.max(s, axis=-1, keepdims=True) for s, _, _ in parts])
    total = jnp.zeros((heads, 1), F32)
    acc = jnp.zeros((heads, HD), F32)
    for s, mask, v in parts:
        expo = jnp.where(mask, jnp.exp2((s - top) * (SCALE * LOG2E)), 0.0)
        total = total + jnp.sum(expo, axis=-1, keepdims=True)
        acc = acc + dot(expo.astype(BF16), v)
    state = jnp.where(iota((heads, HD), 1) < HD // 2, top, total)
    for head in range(GROUP):
        at = pl.ds(8 * (head // 4) + head % 4, ROWS, stride=16)
        soft_s[at, :] = acc[head * ROWS : (head + 1) * ROWS, :]
        also = pl.ds(8 * (head // 4) + head % 4 + 4, ROWS, stride=16)
        soft_s[also, :] = state[head * ROWS : (head + 1) * ROWS, :]
    soft_r[rows(me * 8, 8), :] = soft_s[rows(me * 8, 8), :]

    def soft(i, way):
        other = lax.rem(me + i, NS)
        return remote(
            soft_s.at[rows(other * 8, 8)],
            soft_r.at[rows(way * 8, 8)],
            seq_ss.at[1],
            seq_rs.at[1],
            seq=other,
        )

    def soft_start(i, carry):
        soft(i, me).start()
        return carry

    lax.fori_loop(1, NS, soft_start, 0)
    second_half(1)

    landed(wo_v.at[0], wo_sem.at[2])

    def own(i, carry):
        for half in range(2):
            own_v[half, i] = project(half, 0, i // 2, lax.rem(i, 2))
        return carry

    lax.fori_loop(0, 4, own, 0)

    landed(soft_r.at[0 : (NS - 1) * 8], seq_rs.at[1])
    joined = []
    for q in range(heads // NS):
        sums = soft_r[pl.ds(q, NS, stride=8), :]
        both = soft_r[pl.ds(q + 4, NS, stride=8), :]
        tops = both[:, 0:1]
        weight = jnp.exp2((tops - jnp.max(tops, axis=0, keepdims=True)) * (SCALE * LOG2E))
        whole = jnp.sum(weight * both[:, HD // 2 : HD // 2 + 1], axis=0, keepdims=True)
        joined.append((jnp.sum(weight * sums, axis=0, keepdims=True) / whole).astype(BF16))
    token_row = jnp.broadcast_to(jnp.concatenate(joined, axis=1).astype(F32), (16, WIDTH // 2))
    token_row = token_row.astype(BF16)

    core = lax.rem(me, 2)

    def dpart(k, e):
        return remote(
            dpart_s.at[2 * k + e],
            dpart_r.at[2 * k + e],
            dpart_ss.at[0],
            dpart_rs.at[0],
            head=lax.rem(y + k, NH),
            seq=me + e * (1 - 2 * core),
        )

    for k in (2, 1, 3, 0):
        for e in range(2):
            side = core + e * (1 - 2 * core)
            for b in range(2):
                tile = wo_v[k, 2 * side + b, rows(core * (WIDTH // 2), WIDTH // 2), :]
                value = dot(token_row, tile)[0:1]
                for lanes in range(2):
                    one = value[:, lanes * HD : (lanes + 1) * HD]
                    row = 2 * b + lanes
                    dpart_s[2 * k + e, row : row + 1, :] = one
                    dpart_s[2 * k + e, row + 4 : row + 5, :] = one
            if (k, e) != (0, 0):
                dpart(k, e).start()

    arrived(0, 0, 4)
    arrived(1, 0, 3)

    def mixed(i, carry):
        send(0, ((1, 2),), i // 2, lax.rem(i, 2), 0)
        send(1, ((3, 5),), i // 2, lax.rem(i, 2), 1)
        return carry

    lax.fori_loop(0, 3, mixed, 0)
    arrived(1, 3, 4)
    mixed(3, 0)

    landed(dpart_r.at[1 : 2 * NH], dpart_rs.at[0])
    total = dpart_s[0]
    for n in range(1, 2 * NH):
        total = total + dpart_r[n]
    join_s[...] = total
    join_r[rows(me * 8, 8), :] = total

    def join(i, way):
        other = lax.rem(me + i, NS)
        return remote(join_s, join_r.at[rows(way * 8, 8)], seq_ss.at[2], seq_rs.at[2], seq=other)

    def join_start(i, carry):
        join(i, me).start()
        return carry

    lax.fori_loop(1, NS, join_start, 0)

    landed(hand_v.at[0 : (NS - 1) * 16], seq_ss.at[0])
    landed(soft_r.at[0 : (NS - 1) * 8], seq_ss.at[1])
    save_hand.wait()

    arrived(3, 0, 4)
    arrived(4, 0, 4)

    def finish(i, carry):
        p, jj = i // 2, lax.rem(i, 2)
        for half in range(2):
            value = own_v[half, i] + part_r[2 + half, i].astype(F32)
            value = (value + part_r[4 + half, i].astype(F32)).astype(BF16)
            out[p, half * HALF : (half + 1) * HALF, rows(jj * WIDE, WIDE)] = value
        return carry

    def save_decoded():
        landed(join_r.at[0 : (NS - 1) * 8], seq_rs.at[2])
        for b in range(GROUP):
            mine = join_r[pl.ds(8 * (b // 4) + b % 4, ROWS, stride=16), :]
            for t in range(STEPS):
                one = mine[t * SLOTS : (t + 1) * SLOTS, :]
                dec_out[t, :, b * HD : (b + 1) * HD] = one.astype(BF16)

    arrived(2, 0, 3)
    arrived(5, 0, 3)
    lax.fori_loop(0, 3, finish, 0)
    save_decoded()
    arrived(2, 3, 4)
    arrived(5, 3, 4)
    finish(3, 0)

    landed(dpart_s.at[1 : 2 * NH], dpart_ss.at[0])
    landed(join_r.at[0 : (NS - 1) * 8], seq_ss.at[2])
    landed(part_s, part_ss.at[0])


def store(out_v, hand_v, dec_v, out, handed, dec_out, sem):
    copies = [
        pltpu.make_async_copy(source, target, sem.at[i])
        for i, (source, target) in enumerate([(out_v, out), (hand_v, handed), (dec_v, dec_out)])
    ]
    for copy in copies:
        copy.start()
    for copy in copies:
        copy.wait()


def local(
    prompts,
    prompt_len,
    admitted,
    cache_len,
    cache_kv,
    dec_tokens,
    w_query,
    w_key,
    w_value,
    w_out,
    q_gain,
    k_gain,
):
    half = HD // 2
    one = (THETA ** (-np.arange(half, dtype=np.float64) / half)).astype(np.float32)
    freq = jnp.asarray(np.concatenate([one, one])[None, :])
    hbm = pl.BlockSpec(memory_space=pl.ANY)
    vmem = pl.BlockSpec(memory_space=pltpu.VMEM)
    dma = pltpu.SemaphoreType.DMA
    shapes = [(2, LP, WIDTH), (2 * LP, 2 * HD), (STEPS, SLOTS, WIDTH)]
    results = pl.pallas_call(
        kernel,
        out_shape=[pltpu.VMEM(shape, BF16) for shape in shapes],
        in_specs=[hbm] * 13,
        out_specs=[vmem, hbm, vmem],
        scratch_shapes=[
            pltpu.SMEM((2 * NS,), jnp.int32),
            pltpu.SMEM((SLOTS,), jnp.int32),
            pltpu.SMEM((SLOTS,), jnp.int32),
            pltpu.VMEM((3, 1, HD), F32),
            pltpu.VMEM((2 * LP + ROWS, D), BF16),
            pltpu.VMEM((STEPS, SLOTS, D), BF16),
            pltpu.VMEM((1 + NT, D, TILE), BF16),
            pltpu.VMEM((NH, NT, WIDTH, TILE), BF16),
            pltpu.VMEM((SLOTS * CACHE, 2 * HD), BF16),
            pltpu.VMEM((2, 4, HALF, HD), F32),
            pltpu.VMEM((2 + NT, LP + ROWS, TILE), F32),
            pltpu.VMEM((2 * LP, 2 * HD), BF16),
            pltpu.VMEM((2 * LP, 2 * HD), BF16),
            pltpu.VMEM((2 * LP, 2 * HD), BF16),
            pltpu.VMEM((2, (GROUP + 4) * HALF, HD), BF16),
            pltpu.VMEM(((GROUP + 4) * ROWS, HD), BF16),
            pltpu.VMEM((HD, 2 * HD), BF16),
            pltpu.VMEM((2, LP, WIDTH), BF16),
            pltpu.VMEM((6, 4, HALF, WIDE), BF16),
            pltpu.VMEM((6, 4, HALF, WIDE), BF16),
            pltpu.VMEM((2, 4, HALF, WIDE), F32),
            pltpu.VMEM((NS * 8, HD), F32),
            pltpu.VMEM((NS * 8, HD), F32),
            pltpu.VMEM((8, HD), F32),
            pltpu.VMEM((NS * 8, HD), F32),
            pltpu.VMEM((2 * NH, 8, HD), F32),
            pltpu.VMEM((2 * NH, 8, HD), F32),
            dma((4,)),
            dma((3,)),
            dma((2,)),
            dma((1 + NT,)),
            dma((4,)),
            dma((1,)),
            dma((1,)),
            dma((9,)),
            dma((3,)),
            dma((3,)),
            dma((1,)),
            dma((1,)),
        ],
        compiler_params=pltpu.CompilerParams(
            collective_id=0, has_side_effects=True, vmem_limit_bytes=56 * 2**20
        ),
        cost_estimate=pl.CostEstimate(
            flops=10_500_000_000, bytes_accessed=25_000_000, transcendentals=2_000_000
        ),
    )(
        prompt_len,
        admitted,
        cache_len,
        freq,
        q_gain[None, :],
        k_gain[None, :],
        prompts.reshape(2 * LP, D),
        dec_tokens,
        w_query,
        w_key,
        w_value,
        w_out,
        cache_kv.reshape(SLOTS * CACHE, 2 * HD),
    )
    out, handed, decoded = pl.pallas_call(
        store,
        out_shape=[jax.ShapeDtypeStruct(shape, BF16) for shape in shapes],
        in_specs=[hbm] * 3,
        out_specs=[hbm] * 3,
        scratch_shapes=[dma((3,))],
        compiler_params=pltpu.CompilerParams(vmem_limit_bytes=2**20),
    )(*results)
    return (
        out,
        handed.reshape(1, 2 * NS, EACH, 2 * HD),
        decoded,
    )


def solution(mesh):
    placed = (
        P("seq", None, None),
        P(),
        P(),
        P(),
        P("head", None, "seq", None),
        P(),
        P(None, "head"),
        P(None, "head"),
        P(None, "head"),
        P("head", None),
        P(),
        P(),
    )
    return jax.shard_map(
        local,
        mesh=mesh,
        in_specs=placed,
        out_specs=(P("seq", None, "head"), P("head", None, "seq", None), P(None, None, "head")),
        check_vma=False,
    )
```

```python
import functools

import jax
import jax.numpy as jnp
import numpy as np
from jax import lax
from jax.experimental import pallas as pl
from jax.experimental.pallas import tpu as pltpu
from jax.sharding import PartitionSpec as P

D = 4096
HD = 128
GROUP = 8
WIDTH = GROUP * HD
LP = 256
HALF = LP // 2
SLOTS = 4
STEPS = 4
ROWS = SLOTS * STEPS
CACHE = 512
NS = 32
NH = 4
NX = 4
PER_X = NS // NX
EACH = LP // NS
EPS = 1e-06
THETA = 1000000.0
NEG = -1e30
SCALE = HD ** (-0.5)
LOG2E = 1.4426950408889634
TILE = 256
NT = WIDTH // TILE
WIDE = 2 * TILE
F32 = jnp.float32
BF16 = jnp.bfloat16


def dot(a, b):
    return jnp.dot(a, b, preferred_element_type=F32)


def dot_nt(a, b):
    return lax.dot_general(a, b, (((1,), (1,)), ((), ())), preferred_element_type=F32)


def iota(shape, dim):
    return lax.broadcasted_iota(jnp.int32, shape, dim)


def rotation(positions, freq):
    angle = positions.astype(F32) * freq
    sign = jnp.where(iota((1, HD), 1) < HD // 2, -1.0, 1.0)
    return jnp.cos(angle), jnp.sin(angle) * sign


def gained(cosine, sine, gain):
    return cosine * gain, sine * pltpu.roll(gain, HD // 2, 1)


def normrot(a, first, second):
    inverse = lax.rsqrt(jnp.mean(a * a, axis=-1, keepdims=True) + EPS)
    return (a * first + pltpu.roll(a, HD // 2, 1) * second) * inverse


def kernel(
    plen_ref,
    adm_ref,
    clen_ref,
    freq_ref,
    qg_ref,
    kg_ref,
    prompts,
    dec,
    wq,
    wk,
    wv,
    wo,
    cache,
    out,
    handed,
    dec_out,
    plen,
    adm,
    clen,
    row_v,
    x_v,
    dec_v,
    w_v,
    wo_v,
    cache_v,
    tab_v,
    f_v,
    kv_v,
    give_v,
    hand_v,
    q_v,
    dq_v,
    dkv_v,
    pa_v,
    part_s,
    part_r,
    own_v,
    soft_s,
    soft_r,
    join_s,
    join_r,
    dpart_s,
    dpart_r,
    small_sem,
    x_sem,
    in_sem,
    w_sem,
    wo_sem,
    out_sem,
    part_ss,
    part_rs,
    seq_ss,
    seq_rs,
    dpart_ss,
    dpart_rs,
    row_sem,
):
    y = lax.axis_index("head")
    me = lax.axis_index("seq")
    right = lax.rem(y + 1, NH)
    left = lax.rem(y + NH - 1, NH)

    def remote(src, dst, send, recv, **where):
        return pltpu.make_async_remote_copy(
            src_ref=src,
            dst_ref=dst,
            send_sem=send,
            recv_sem=recv,
            device_id=where,
            device_id_type=pl.DeviceIdType.MESH,
        )

    def landed(ref, sem):
        pltpu.make_async_copy(ref, ref, sem).wait()

    def rows(start, size):
        return pl.ds(pl.multiple_of(start, size), size)

    def load_x(half, p):
        source = p * LP + half * HALF
        target = half * LP + p * HALF
        return pltpu.make_async_copy(
            prompts.at[source : source + HALF], x_v.at[target : target + HALF], x_sem.at[half + (p if half == 0 else 1)]
        )

    small = [
        pltpu.make_async_copy(ref, to, small_sem.at[i])
        for ref, to, i in (
            (freq_ref, row_v.at[0], 0),
            (qg_ref, row_v.at[1], 0),
            (kg_ref, row_v.at[2], 0),
            (plen_ref, plen, 1),
            (adm_ref, adm, 2),
            (clen_ref, clen, 3),
        )
    ]
    load_k = pltpu.make_async_copy(wk, w_v.at[0, :, 0:HD], w_sem.at[0])
    load_v = pltpu.make_async_copy(wv, w_v.at[0, :, HD : 2 * HD], w_sem.at[0])
    load_dec = pltpu.make_async_copy(dec, dec_v, in_sem.at[0])
    load_cache = pltpu.make_async_copy(cache, cache_v, in_sem.at[1])

    def load_q(t):
        return pltpu.make_async_copy(wq.at[:, rows((t - 1) * TILE, TILE)], w_v.at[t], w_sem.at[t])

    def load_o(k, j):
        start = lax.rem(y + k, NH) * WIDTH + j * TILE
        sem = wo_sem.at[j // 2 if k in (2, 3) else 2 + k]
        return pltpu.make_async_copy(wo.at[:, rows(start, TILE)], wo_v.at[k, j], sem)

    load_k.start()
    load_x(0, 0).start()
    load_v.start()
    for load in small:
        load.start()
    load_q(1).start()

    barrier = pltpu.get_barrier_semaphore()

    def signal(sem, **where):
        pl.semaphore_signal(sem, inc=1, device_id=where, device_id_type=pl.DeviceIdType.MESH)

    def signal_x(sem):
        for i in range(1, NX):
            signal(sem, seq=lax.rem(me + i * PER_X, NS))

    for k in range(1, NH):
        signal(barrier, head=lax.rem(y + k, NH))
    signal_x(barrier)
    for i in range(1, PER_X):
        signal(barrier, seq=me - lax.rem(me, PER_X) + lax.rem(me + i, PER_X))

    load_q(2).start()

    landed(row_v, small_sem.at[0])
    for load in small[3:]:
        load.wait()
    freq, q_gain, k_gain = row_v[0], row_v[1], row_v[2]
    for half in range(2):
        first, second = rotation(iota((HALF, HD), 0) + half * HALF, freq)
        tab_v[half, 0], tab_v[half, 1] = gained(first, second, q_gain)
        tab_v[half, 2], tab_v[half, 3] = gained(first, second, k_gain)
    load_q(3).start()

    def finish_query(half, p, t, base):
        slot = lax.rem(t + 5, 6)
        for b in range(TILE // HD):
            mine = f_v[t, base : base + HALF, b * HD : (b + 1) * HD]
            one = normrot(mine, tab_v[half, 0], tab_v[half, 1])
            q_v[p, rows(slot * TILE + b * HD, HD), :] = one.astype(BF16)

    def finish_token(t):
        slot = lax.rem(t + 5, 6)
        for b in range(TILE // HD):
            mine = f_v[t, LP : LP + ROWS, b * HD : (b + 1) * HD]
            one = normrot(mine, dq_first, dq_second)
            dq_v[rows((slot * 2 + b) * ROWS, ROWS), :] = one.astype(BF16)

    def keys_values(half, p, base):
        mine = f_v[0, base : base + HALF, :]
        to = rows(p * LP + half * HALF, HALF)
        kv_v[to, 0:HD] = normrot(mine[:, 0:HD], tab_v[half, 2], tab_v[half, 3]).astype(BF16)
        kv_v[to, HD : 2 * HD] = mine[:, HD : 2 * HD].astype(BF16)

    def multiply_first(p):
        def tile(t, carry):
            @pl.when(p == 0)
            def _():
                landed(w_v.at[t], w_sem.at[t])

                @pl.when(t == 0)
                def _():
                    load_q(4).start()

                for jj in range(2):

                    @pl.when(t == 1 + jj)
                    def _(jj=jj):
                        for j in (2 * jj, 2 * jj + 1):
                            load_o(2, j).start()
                            load_o(3, j).start()

                @pl.when(t == 2)
                def _():
                    load_x(0, 1).start()

            finish_query(0, p, lax.rem(t + 5, 6), 0)
            f_v[t, 0:HALF, :] = dot(x_v[rows(p * HALF, HALF), :], w_v[t])
            return carry

        lax.fori_loop(0, 1 + NT, tile, 0)
        finish_query(0, p, NT, 0)
        keys_values(0, p, 0)

    def multiply_second(after_keys):
        def finish(t):
            for p in range(2):
                finish_query(1, p, t, p * HALF)
            finish_token(t)

        def tile(t, carry):
            pl.when(t == 1)(after_keys)
            finish(lax.rem(t + 5, 6))
            f_v[t] = dot(x_v[LP : 2 * LP + ROWS, :], w_v[t])
            return carry

        lax.fori_loop(0, 1 + NT, tile, 0)
        finish(NT)

    def attend(half, p):
        keys = (half + 1) * HALF
        at = iota((keys, HALF), 0)
        causal = at <= iota((keys, HALF), 1) + half * HALF
        bias = jnp.where(causal & (at < plen[2 * me + p]), 0.0, NEG)
        mine = rows(p * LP, keys) if half else pl.ds(pl.multiple_of(p * LP, LP), keys)
        scores = dot_nt(kv_v[mine, 0:HD], q_v[p, 0 : GROUP * HALF])
        scores = scores + jnp.concatenate([bias] * GROUP, axis=1)
        top = jnp.max(scores, axis=0, keepdims=True)
        expo = jnp.exp2((scores - top) * (SCALE * LOG2E))
        weights = expo * (1.0 / jnp.sum(expo, axis=0, keepdims=True))
        values = kv_v[mine, HD : 2 * HD].astype(F32).T.astype(BF16)
        mixed = dot(values, weights.astype(BF16))
        for head in range(GROUP):
            one = mixed[:, head * HALF : (head + 1) * HALF].T.astype(BF16)
            pa_v[half, rows(p * HALF, HALF), head * HD : (head + 1) * HD] = one

    def arrival(slot, i):
        return {
            0: (i + 2) // 3,
            1: 2 + (i + 1) // 2,
            2: 5 + i // 3,
            5: 7 + i // 3,
            3: 9,
            4: 10,
        }[slot]

    def arrived(slot, first, last):
        landed(part_r.at[slot, first:last], part_rs.at[arrival(slot, first)])

    def part(slot, i):
        to = right if slot in (0, 2, 3) else left
        return remote(
            part_s.at[slot, i],
            part_r.at[slot, i],
            part_ss.at[0],
            part_rs.at[arrival(slot, i)],
            head=to,
        )

    def project(half, k, p, jj):
        mine = pa_v[half, rows(p * HALF, HALF), :]
        return jnp.concatenate([dot(mine, wo_v[k, 2 * jj + b]) for b in range(2)], axis=1)

    def send(half, targets, p, jj, far=None):
        i = p * 2 + jj
        values = [project(half, k, p, jj) for k, slot in targets]
        for (k, slot), value in zip(targets, values):
            if far is not None:
                value = value + part_r[far, i].astype(F32)
            part_s[slot, i] = value.astype(BF16)
            part(slot, i).start()

    def first_half(p, carry):
        @pl.when(p == 1)
        def _():
            landed(x_v.at[HALF:LP], x_sem.at[1])

        multiply_first(p)
        attend(0, p)

        def tile(jj, carry):
            @pl.when(p == 0)
            def _():
                landed(wo_v.at[2:4, pl.ds(2 * jj, 2)], wo_sem.at[jj])

                @pl.when(jj == 0)
                def _():
                    pl.semaphore_wait(barrier, NH - 1 + NX - 1 + PER_X - 1)

            send(0, ((2, 0), (3, 4)), p, jj)
            return carry

        lax.fori_loop(0, 2, tile, 0)

        @pl.when(p == 0)
        def _():
            signal_x(row_sem)
            load_dec.start()
            load_x(1, 0).start()
            load_x(1, 1).start()
            for k in (1, 0):
                for j in range(NT):
                    load_o(k, j).start()
            load_cache.start()

        return carry

    def second_half(p):
        attend(1, p)

        def tile(jj, carry):
            send(1, ((1, 3), (2, 1)), p, jj)
            return carry

        lax.fori_loop(0, 2, tile, 0)

    landed(x_v.at[0:HALF], x_sem.at[0])
    lax.fori_loop(0, 2, first_half, 0)

    admitted = [adm[r] for r in range(SLOTS)]
    handed_len = [plen[jnp.maximum(admitted[r], 0)] for r in range(SLOTS)]
    is_new = [admitted[r] >= 0 for r in range(SLOTS)]
    eff_len = [jnp.where(is_new[r], handed_len[r], clen[r]) for r in range(SLOTS)]

    def per_slot(slot, values):
        picked = jnp.full(slot.shape, values[0], jnp.int32)
        for r in range(1, SLOTS):
            picked = jnp.where(slot == r, values[r], picked)
        return picked

    token = iota((ROWS, HD), 0)
    places = per_slot(token & (SLOTS - 1), eff_len) + (token >> 2)
    first, second = rotation(places, freq)
    dq_first, dq_second = gained(first, second, q_gain)
    dk_first, dk_second = gained(first, second, k_gain)

    landed(x_v.at[LP : 2 * LP], x_sem.at[2])
    load_dec.wait()
    x_v[2 * LP : 2 * LP + ROWS, :] = jnp.concatenate(
        [dec_v[t].astype(F32) for t in range(STEPS)], axis=0
    ).astype(BF16)
    def hand(i, way):
        other = lax.rem(me + i, NS)
        return remote(
            give_v.at[rows(other * 16, 16)],
            hand_v.at[rows(way * 16, 16)],
            seq_ss.at[0],
            seq_rs.at[0],
            seq=other,
        )

    def hand_over():
        for p in range(2):
            keys_values(1, p, p * HALF)
        new = f_v[0, LP : LP + ROWS, :]
        dkv_v[...] = jnp.zeros_like(dkv_v)
        dkv_v[0:ROWS, 0:HD] = normrot(new[:, 0:HD], dk_first, dk_second).astype(BF16)
        dkv_v[0:ROWS, HD : 2 * HD] = new[:, HD : 2 * HD].astype(BF16)
        place = iota((2 * LP, 2 * LP), 0)
        source = (((place >> 3) & 1) << 8) + ((place & 7) << 5) + (place >> 4)
        pick = jnp.where(source == iota((2 * LP, 2 * LP), 1), 1.0, 0.0).astype(BF16)
        give_v[...] = dot(pick, kv_v[...]).astype(BF16)
        hand_v[rows(me * 16, 16), :] = give_v[rows(me * 16, 16), :]

        def hand_start(i, carry):
            hand(i, me).start()
            return carry

        pl.semaphore_wait(row_sem, NX - 1)
        lax.fori_loop(1, NS, hand_start, 0)

    multiply_second(hand_over)
    landed(wo_v.at[1], wo_sem.at[3])
    def mixed_right(i):
        send(0, ((1, 2),), i // 2, lax.rem(i, 2), 0)

    def mixed_left(i):
        send(1, ((3, 5),), i // 2, lax.rem(i, 2), 1)

    def mixed_rows(half, k, slot, far, start):
        some = pl.ds(start, HALF // 2)
        mine = pa_v[half, some, :]
        value = jnp.concatenate([dot(mine, wo_v[k, b]) for b in range(2)], axis=1)
        value = value + part_r[far, 0, some, :].astype(F32)
        part_s[slot, 0, some, :] = value.astype(BF16)
        remote(
            part_s.at[slot, 0, some],
            part_r.at[slot, 0, some],
            part_ss.at[0],
            part_rs.at[arrival(slot, 0)],
            head=right if slot == 2 else left,
        ).start()

    second_half(0)
    arrived(0, 0, 1)
    mixed_rows(0, 1, 2, 0, 0)
    load_cache.wait()

    landed(hand_v.at[0 : (NS - 1) * 16], seq_rs.at[0])
    save_hand = pltpu.make_async_copy(hand_v, handed, out_sem.at[0])
    save_hand.start()

    heads = GROUP * ROWS
    queries = dq_v[0:heads]

    def pieces():
        for r in range(SLOTS):
            slot = iota((heads, CACHE), 0) & (SLOTS - 1)
            at = (iota((heads, CACHE), 1) << 5) + me
            limit = jnp.where(is_new[r], 0, clen[r])
            yield (
                dot_nt(queries, cache_v[r * CACHE : (r + 1) * CACHE, 0:HD]),
                (slot == r) & (at < limit),
                cache_v[r * CACHE : (r + 1) * CACHE, HD : 2 * HD],
            )
        slot = iota((heads, 2 * LP), 0) & (SLOTS - 1)
        column = iota((heads, 2 * LP), 1)
        prompt = column >> 3
        at = ((column & 7) << 5) + me
        yield (
            dot_nt(queries, hand_v[:, 0:HD]),
            (prompt == per_slot(slot, admitted)) & (at < per_slot(slot, handed_len)),
            hand_v[:, HD : 2 * HD],
        )
        row = iota((heads, HD), 0)
        column = iota((heads, HD), 1) + jnp.where(me == 0, 0, ROWS)
        yield (
            dot_nt(queries, dkv_v[:, 0:HD]),
            ((row & 3) == (column & 3)) & ((column >> 2) <= ((row >> 2) & 3)) & (column < ROWS),
            dkv_v[:, HD : 2 * HD],
        )

    parts = [(jnp.where(mask, s, NEG), mask, v) for s, mask, v in pieces()]
    top = functools.reduce(jnp.maximum, [jnp.max(s, axis=-1, keepdims=True) for s, _, _ in parts])
    total = jnp.zeros((heads, 1), F32)
    acc = jnp.zeros((heads, HD), F32)
    for s, mask, v in parts:
        expo = jnp.where(mask, jnp.exp2((s - top) * (SCALE * LOG2E)), 0.0)
        total = total + jnp.sum(expo, axis=-1, keepdims=True)
        acc = acc + dot(expo.astype(BF16), v)
    state = jnp.where(iota((heads, HD), 1) < HD // 2, top, total)
    for head in range(GROUP):
        at = pl.ds(8 * (head // 4) + head % 4, ROWS, stride=16)
        soft_s[at, :] = acc[head * ROWS : (head + 1) * ROWS, :]
        also = pl.ds(8 * (head // 4) + head % 4 + 4, ROWS, stride=16)
        soft_s[also, :] = state[head * ROWS : (head + 1) * ROWS, :]
    soft_r[rows(me * 8, 8), :] = soft_s[rows(me * 8, 8), :]

    def soft(i, way):
        other = lax.rem(me + i, NS)
        return remote(
            soft_s.at[rows(other * 8, 8)],
            soft_r.at[rows(way * 8, 8)],
            seq_ss.at[1],
            seq_rs.at[1],
            seq=other,
        )

    def soft_start(i, carry):
        soft(i, me).start()
        return carry

    lax.fori_loop(1, NS, soft_start, 0)
    second_half(1)

    landed(wo_v.at[0], wo_sem.at[2])

    def own(i, carry):
        for half in range(2):
            own_v[half, i] = project(half, 0, i // 2, lax.rem(i, 2))
        return carry

    lax.fori_loop(0, 4, own, 0)

    arrived(1, 0, 1)
    mixed_rows(1, 3, 5, 1, 0)

    landed(soft_r.at[0 : (NS - 1) * 8], seq_rs.at[1])
    joined = []
    for q in range(heads // NS):
        sums = soft_r[pl.ds(q, NS, stride=8), :]
        both = soft_r[pl.ds(q + 4, NS, stride=8), :]
        tops = both[:, 0:1]
        weight = jnp.exp2((tops - jnp.max(tops, axis=0, keepdims=True)) * (SCALE * LOG2E))
        whole = jnp.sum(weight * both[:, HD // 2 : HD // 2 + 1], axis=0, keepdims=True)
        joined.append((jnp.sum(weight * sums, axis=0, keepdims=True) / whole).astype(BF16))
    token_row = jnp.broadcast_to(jnp.concatenate(joined, axis=1).astype(F32), (16, WIDTH // 2))
    token_row = token_row.astype(BF16)

    core = lax.rem(me, 2)

    def dpart(k, e):
        return remote(
            dpart_s.at[2 * k + e],
            dpart_r.at[2 * k + e],
            dpart_ss.at[0],
            dpart_rs.at[0],
            head=lax.rem(y + k, NH),
            seq=me + e * (1 - 2 * core),
        )

    for k in (2, 1, 3, 0):
        for e in range(2):
            side = core + e * (1 - 2 * core)
            for b in range(2):
                tile = wo_v[k, 2 * side + b, rows(core * (WIDTH // 2), WIDTH // 2), :]
                value = dot(token_row, tile)[0:1]
                for lanes in range(2):
                    one = value[:, lanes * HD : (lanes + 1) * HD]
                    row = 2 * b + lanes
                    dpart_s[2 * k + e, row : row + 1, :] = one
                    dpart_s[2 * k + e, row + 4 : row + 5, :] = one
            if (k, e) != (0, 0):
                dpart(k, e).start()

    def right_tile(i, carry):
        mixed_right(i)
        return carry

    mixed_rows(0, 1, 2, 0, HALF // 2)
    mixed_rows(1, 3, 5, 1, HALF // 2)
    arrived(0, 1, 4)
    lax.fori_loop(1, 4, right_tile, 0)
    arrived(1, 1, 3)
    for i in (1, 2):
        mixed_left(i)
    arrived(1, 3, 4)
    mixed_left(3)

    landed(dpart_r.at[1 : 2 * NH], dpart_rs.at[0])
    total = dpart_s[0]
    for n in range(1, 2 * NH):
        total = total + dpart_r[n]
    join_s[...] = total
    join_r[rows(me * 8, 8), :] = total

    def join(i, way):
        other = lax.rem(me + i, NS)
        return remote(join_s, join_r.at[rows(way * 8, 8)], seq_ss.at[2], seq_rs.at[2], seq=other)

    def join_start(i, carry):
        join(i, me).start()
        return carry

    lax.fori_loop(1, NS, join_start, 0)

    landed(hand_v.at[0 : (NS - 1) * 16], seq_ss.at[0])
    landed(soft_r.at[0 : (NS - 1) * 8], seq_ss.at[1])
    save_hand.wait()

    arrived(3, 0, 4)
    arrived(4, 0, 4)

    def finish(i, carry):
        p, jj = i // 2, lax.rem(i, 2)
        for half in range(2):
            value = own_v[half, i] + part_r[2 + half, i].astype(F32)
            value = (value + part_r[4 + half, i].astype(F32)).astype(BF16)
            out[p, half * HALF : (half + 1) * HALF, rows(jj * WIDE, WIDE)] = value
        return carry

    def save_decoded():
        landed(join_r.at[0 : (NS - 1) * 8], seq_rs.at[2])
        for b in range(GROUP):
            mine = join_r[pl.ds(8 * (b // 4) + b % 4, ROWS, stride=16), :]
            for t in range(STEPS):
                one = mine[t * SLOTS : (t + 1) * SLOTS, :]
                dec_out[t, :, b * HD : (b + 1) * HD] = one.astype(BF16)

    arrived(2, 0, 3)
    arrived(5, 0, 3)
    lax.fori_loop(0, 3, finish, 0)
    save_decoded()
    arrived(2, 3, 4)
    arrived(5, 3, 4)
    finish(3, 0)

    landed(dpart_s.at[1 : 2 * NH], dpart_ss.at[0])
    landed(join_r.at[0 : (NS - 1) * 8], seq_ss.at[2])
    landed(part_s, part_ss.at[0])


def store(out_v, hand_v, dec_v, out, handed, dec_out, sem):
    copies = [
        pltpu.make_async_copy(source, target, sem.at[i])
        for i, (source, target) in enumerate([(out_v, out), (hand_v, handed), (dec_v, dec_out)])
    ]
    for copy in copies:
        copy.start()
    for copy in copies:
        copy.wait()


def local(
    prompts,
    prompt_len,
    admitted,
    cache_len,
    cache_kv,
    dec_tokens,
    w_query,
    w_key,
    w_value,
    w_out,
    q_gain,
    k_gain,
):
    half = HD // 2
    one = (THETA ** (-np.arange(half, dtype=np.float64) / half)).astype(np.float32)
    freq = jnp.asarray(np.concatenate([one, one])[None, :])
    hbm = pl.BlockSpec(memory_space=pl.ANY)
    vmem = pl.BlockSpec(memory_space=pltpu.VMEM)
    dma = pltpu.SemaphoreType.DMA
    shapes = [(2, LP, WIDTH), (2 * LP, 2 * HD), (STEPS, SLOTS, WIDTH)]
    results = pl.pallas_call(
        kernel,
        out_shape=[pltpu.VMEM(shape, BF16) for shape in shapes],
        in_specs=[hbm] * 13,
        out_specs=[vmem, hbm, vmem],
        scratch_shapes=[
            pltpu.SMEM((2 * NS,), jnp.int32),
            pltpu.SMEM((SLOTS,), jnp.int32),
            pltpu.SMEM((SLOTS,), jnp.int32),
            pltpu.VMEM((3, 1, HD), F32),
            pltpu.VMEM((2 * LP + ROWS, D), BF16),
            pltpu.VMEM((STEPS, SLOTS, D), BF16),
            pltpu.VMEM((1 + NT, D, TILE), BF16),
            pltpu.VMEM((NH, NT, WIDTH, TILE), BF16),
            pltpu.VMEM((SLOTS * CACHE, 2 * HD), BF16),
            pltpu.VMEM((2, 4, HALF, HD), F32),
            pltpu.VMEM((2 + NT, LP + ROWS, TILE), F32),
            pltpu.VMEM((2 * LP, 2 * HD), BF16),
            pltpu.VMEM((2 * LP, 2 * HD), BF16),
            pltpu.VMEM((2 * LP, 2 * HD), BF16),
            pltpu.VMEM((2, (GROUP + 4) * HALF, HD), BF16),
            pltpu.VMEM(((GROUP + 4) * ROWS, HD), BF16),
            pltpu.VMEM((HD, 2 * HD), BF16),
            pltpu.VMEM((2, LP, WIDTH), BF16),
            pltpu.VMEM((6, 4, HALF, WIDE), BF16),
            pltpu.VMEM((6, 4, HALF, WIDE), BF16),
            pltpu.VMEM((2, 4, HALF, WIDE), F32),
            pltpu.VMEM((NS * 8, HD), F32),
            pltpu.VMEM((NS * 8, HD), F32),
            pltpu.VMEM((8, HD), F32),
            pltpu.VMEM((NS * 8, HD), F32),
            pltpu.VMEM((2 * NH, 8, HD), F32),
            pltpu.VMEM((2 * NH, 8, HD), F32),
            dma((4,)),
            dma((3,)),
            dma((2,)),
            dma((1 + NT,)),
            dma((4,)),
            dma((1,)),
            dma((1,)),
            dma((11,)),
            dma((3,)),
            dma((3,)),
            dma((1,)),
            dma((1,)),
            pltpu.SemaphoreType.REGULAR,
        ],
        compiler_params=pltpu.CompilerParams(
            collective_id=0, has_side_effects=True, vmem_limit_bytes=56 * 2**20
        ),
        cost_estimate=pl.CostEstimate(
            flops=10_500_000_000, bytes_accessed=25_000_000, transcendentals=2_000_000
        ),
    )(
        prompt_len,
        admitted,
        cache_len,
        freq,
        q_gain[None, :],
        k_gain[None, :],
        prompts.reshape(2 * LP, D),
        dec_tokens,
        w_query,
        w_key,
        w_value,
        w_out,
        cache_kv.reshape(SLOTS * CACHE, 2 * HD),
    )
    out, handed, decoded = pl.pallas_call(
        store,
        out_shape=[jax.ShapeDtypeStruct(shape, BF16) for shape in shapes],
        in_specs=[hbm] * 3,
        out_specs=[hbm] * 3,
        scratch_shapes=[dma((3,))],
        compiler_params=pltpu.CompilerParams(vmem_limit_bytes=2**20),
    )(*results)
    return (
        out,
        handed.reshape(1, 2 * NS, EACH, 2 * HD),
        decoded,
    )


def solution(mesh):
    placed = (
        P("seq", None, None),
        P(),
        P(),
        P(),
        P("head", None, "seq", None),
        P(),
        P(None, "head"),
        P(None, "head"),
        P(None, "head"),
        P("head", None),
        P(),
        P(),
    )
    return jax.shard_map(
        local,
        mesh=mesh,
        in_specs=placed,
        out_specs=(P("seq", None, "head"), P("head", None, "seq", None), P(None, None, "head")),
        check_vma=False,
    )
```

```python
import functools

import jax
import jax.numpy as jnp
import numpy as np
from jax import lax
from jax.experimental import pallas as pl
from jax.experimental.pallas import tpu as pltpu
from jax.sharding import PartitionSpec as P

D = 4096
HD = 128
GROUP = 8
WIDTH = GROUP * HD
LP = 256
HALF = LP // 2
SLOTS = 4
STEPS = 4
ROWS = SLOTS * STEPS
CACHE = 512
NS = 32
NH = 4
NX = 4
PER_X = NS // NX
EACH = LP // NS
EPS = 1e-06
THETA = 1000000.0
NEG = -1e30
SCALE = HD ** (-0.5)
LOG2E = 1.4426950408889634
TILE = 256
NT = WIDTH // TILE
WIDE = 2 * TILE
F32 = jnp.float32
BF16 = jnp.bfloat16


def dot(a, b):
    return jnp.dot(a, b, preferred_element_type=F32)


def dot_nt(a, b):
    return lax.dot_general(a, b, (((1,), (1,)), ((), ())), preferred_element_type=F32)


def iota(shape, dim):
    return lax.broadcasted_iota(jnp.int32, shape, dim)


def rotation(positions, freq):
    angle = positions.astype(F32) * freq
    sign = jnp.where(iota((1, HD), 1) < HD // 2, -1.0, 1.0)
    return jnp.cos(angle), jnp.sin(angle) * sign


def gained(cosine, sine, gain):
    return cosine * gain, sine * pltpu.roll(gain, HD // 2, 1)


def normrot(a, first, second):
    inverse = lax.rsqrt(jnp.mean(a * a, axis=-1, keepdims=True) + EPS)
    return (a * first + pltpu.roll(a, HD // 2, 1) * second) * inverse


def kernel(
    plen_ref,
    adm_ref,
    clen_ref,
    freq_ref,
    qg_ref,
    kg_ref,
    prompts,
    dec,
    wq,
    wk,
    wv,
    wo,
    cache,
    out,
    handed,
    dec_out,
    plen,
    adm,
    clen,
    row_v,
    x_v,
    dec_v,
    w_v,
    wo_v,
    cache_v,
    tab_v,
    f_v,
    kv_v,
    give_v,
    hand_v,
    q_v,
    dq_v,
    dkv_v,
    pa_v,
    part_s,
    part_r,
    own_v,
    soft_s,
    soft_r,
    join_s,
    join_r,
    dpart_s,
    dpart_r,
    small_sem,
    x_sem,
    in_sem,
    w_sem,
    wo_sem,
    out_sem,
    part_ss,
    part_rs,
    seq_ss,
    seq_rs,
    dpart_ss,
    dpart_rs,
    row_sem,
):
    y = lax.axis_index("head")
    me = lax.axis_index("seq")
    right = lax.rem(y + 1, NH)
    left = lax.rem(y + NH - 1, NH)

    def remote(src, dst, send, recv, **where):
        return pltpu.make_async_remote_copy(
            src_ref=src,
            dst_ref=dst,
            send_sem=send,
            recv_sem=recv,
            device_id=where,
            device_id_type=pl.DeviceIdType.MESH,
        )

    def landed(ref, sem):
        pltpu.make_async_copy(ref, ref, sem).wait()

    def rows(start, size):
        return pl.ds(pl.multiple_of(start, size), size)

    def load_x(half, p):
        source = p * LP + half * HALF
        target = half * LP + p * HALF
        return pltpu.make_async_copy(
            prompts.at[source : source + HALF], x_v.at[target : target + HALF], x_sem.at[half + (p if half == 0 else 1)]
        )

    small = [
        pltpu.make_async_copy(ref, to, small_sem.at[i])
        for ref, to, i in (
            (freq_ref, row_v.at[0], 0),
            (qg_ref, row_v.at[1], 0),
            (kg_ref, row_v.at[2], 0),
            (plen_ref, plen, 1),
            (adm_ref, adm, 2),
            (clen_ref, clen, 3),
        )
    ]
    load_k = pltpu.make_async_copy(wk, w_v.at[0, :, 0:HD], w_sem.at[0])
    load_v = pltpu.make_async_copy(wv, w_v.at[0, :, HD : 2 * HD], w_sem.at[0])
    load_dec = pltpu.make_async_copy(dec, dec_v, in_sem.at[0])
    load_cache = pltpu.make_async_copy(cache, cache_v, in_sem.at[1])

    def load_q(t):
        return pltpu.make_async_copy(wq.at[:, rows((t - 1) * TILE, TILE)], w_v.at[t], w_sem.at[t])

    def load_o(k, j):
        start = lax.rem(y + k, NH) * WIDTH + j * TILE
        sem = wo_sem.at[j // 2 if k in (2, 3) else 2 + k]
        return pltpu.make_async_copy(wo.at[:, rows(start, TILE)], wo_v.at[k, j], sem)

    load_k.start()
    load_x(0, 0).start()
    load_v.start()
    for load in small:
        load.start()
    load_q(1).start()

    barrier = pltpu.get_barrier_semaphore()

    def signal(sem, **where):
        pl.semaphore_signal(sem, inc=1, device_id=where, device_id_type=pl.DeviceIdType.MESH)

    def signal_x(sem):
        for i in range(1, NX):
            signal(sem, seq=lax.rem(me + i * PER_X, NS))

    for k in range(1, NH):
        signal(barrier, head=lax.rem(y + k, NH))
    signal_x(barrier)
    for i in range(1, PER_X):
        signal(barrier, seq=me - lax.rem(me, PER_X) + lax.rem(me + i, PER_X))

    load_q(2).start()

    landed(row_v, small_sem.at[0])
    for load in small[3:]:
        load.wait()
    freq, q_gain, k_gain = row_v[0], row_v[1], row_v[2]
    for half in range(2):
        first, second = rotation(iota((HALF, HD), 0) + half * HALF, freq)
        tab_v[half, 0], tab_v[half, 1] = gained(first, second, q_gain)
        tab_v[half, 2], tab_v[half, 3] = gained(first, second, k_gain)
    load_q(3).start()

    def finish_query(half, p, t, base):
        slot = lax.rem(t + 5, 6)
        for b in range(TILE // HD):
            mine = f_v[t, base : base + HALF, b * HD : (b + 1) * HD]
            one = normrot(mine, tab_v[half, 0], tab_v[half, 1])
            q_v[p, rows(slot * TILE + b * HD, HD), :] = one.astype(BF16)

    def finish_token(t):
        slot = lax.rem(t + 5, 6)
        for b in range(TILE // HD):
            mine = f_v[t, LP : LP + ROWS, b * HD : (b + 1) * HD]
            one = normrot(mine, dq_first, dq_second)
            dq_v[rows((slot * 2 + b) * ROWS, ROWS), :] = one.astype(BF16)

    def keys_values(half, p, base):
        mine = f_v[0, base : base + HALF, :]
        to = rows(p * LP + half * HALF, HALF)
        kv_v[to, 0:HD] = normrot(mine[:, 0:HD], tab_v[half, 2], tab_v[half, 3]).astype(BF16)
        kv_v[to, HD : 2 * HD] = mine[:, HD : 2 * HD].astype(BF16)

    def multiply_first(p):
        def tile(t, carry):
            @pl.when(p == 0)
            def _():
                landed(w_v.at[t], w_sem.at[t])

                @pl.when(t == 0)
                def _():
                    load_q(4).start()

                for jj in range(2):

                    @pl.when(t == 1 + jj)
                    def _(jj=jj):
                        for j in (2 * jj, 2 * jj + 1):
                            load_o(2, j).start()
                            load_o(3, j).start()

                @pl.when(t == 2)
                def _():
                    load_x(0, 1).start()

            @pl.when(t == 2)
            def _():
                keys_values(0, p, 0)

            finish_query(0, p, lax.rem(t + 5, 6), 0)
            f_v[t, 0:HALF, :] = dot(x_v[rows(p * HALF, HALF), :], w_v[t])
            return carry

        lax.fori_loop(0, 1 + NT, tile, 0)
        finish_query(0, p, NT, 0)

    def multiply_second(after_keys):
        def finish(t):
            for p in range(2):
                finish_query(1, p, t, p * HALF)
            finish_token(t)

        def tile(t, carry):
            pl.when(t == 1)(after_keys)
            finish(lax.rem(t + 5, 6))
            f_v[t] = dot(x_v[LP : 2 * LP + ROWS, :], w_v[t])
            return carry

        lax.fori_loop(0, 1 + NT, tile, 0)
        finish(NT)

    def attend(half, p):
        keys = (half + 1) * HALF
        at = iota((keys, HALF), 0)
        causal = at <= iota((keys, HALF), 1) + half * HALF
        bias = jnp.where(causal & (at < plen[2 * me + p]), 0.0, NEG)
        mine = rows(p * LP, keys) if half else pl.ds(pl.multiple_of(p * LP, LP), keys)
        scores = dot_nt(kv_v[mine, 0:HD], q_v[p, 0 : GROUP * HALF])
        scores = scores + jnp.concatenate([bias] * GROUP, axis=1)
        top = jnp.max(scores, axis=0, keepdims=True)
        expo = jnp.exp2((scores - top) * (SCALE * LOG2E))
        weights = expo * (1.0 / jnp.sum(expo, axis=0, keepdims=True))
        values = kv_v[mine, HD : 2 * HD].astype(F32).T.astype(BF16)
        mixed = dot(values, weights.astype(BF16))
        for head in range(GROUP):
            one = mixed[:, head * HALF : (head + 1) * HALF].T.astype(BF16)
            pa_v[half, rows(p * HALF, HALF), head * HD : (head + 1) * HD] = one

    def arrival(slot, i):
        return {
            0: (i + 2) // 3,
            1: 2 + (i + 1) // 2,
            2: 5 + i // 3,
            5: 7 + i // 3,
            3: 9,
            4: 10,
        }[slot]

    def arrived(slot, first, last):
        landed(part_r.at[slot, first:last], part_rs.at[arrival(slot, first)])

    def part(slot, i):
        to = right if slot in (0, 2, 3) else left
        return remote(
            part_s.at[slot, i],
            part_r.at[slot, i],
            part_ss.at[0],
            part_rs.at[arrival(slot, i)],
            head=to,
        )

    def project(half, k, p, jj):
        mine = pa_v[half, rows(p * HALF, HALF), :]
        return jnp.concatenate([dot(mine, wo_v[k, 2 * jj + b]) for b in range(2)], axis=1)

    def send(half, targets, p, jj, far=None):
        i = p * 2 + jj
        values = [project(half, k, p, jj) for k, slot in targets]
        for (k, slot), value in zip(targets, values):
            if far is not None:
                value = value + part_r[far, i].astype(F32)
            part_s[slot, i] = value.astype(BF16)
            part(slot, i).start()

    def first_half(p, carry):
        @pl.when(p == 1)
        def _():
            landed(x_v.at[HALF:LP], x_sem.at[1])

        multiply_first(p)
        attend(0, p)

        def tile(jj, carry):
            @pl.when(p == 0)
            def _():
                landed(wo_v.at[2:4, pl.ds(2 * jj, 2)], wo_sem.at[jj])

                @pl.when(jj == 0)
                def _():
                    pl.semaphore_wait(barrier, NH - 1 + NX - 1 + PER_X - 1)

            send(0, ((2, 0), (3, 4)), p, jj)
            return carry

        lax.fori_loop(0, 2, tile, 0)

        @pl.when(p == 0)
        def _():
            signal_x(row_sem)
            load_dec.start()
            load_x(1, 0).start()
            load_x(1, 1).start()
            for k in (1, 0):
                for j in range(NT):
                    load_o(k, j).start()
            load_cache.start()

        return carry

    def second_half(p):
        attend(1, p)

        def tile(jj, carry):
            send(1, ((1, 3), (2, 1)), p, jj)
            return carry

        lax.fori_loop(0, 2, tile, 0)

    landed(x_v.at[0:HALF], x_sem.at[0])
    lax.fori_loop(0, 2, first_half, 0)

    admitted = [adm[r] for r in range(SLOTS)]
    handed_len = [plen[jnp.maximum(admitted[r], 0)] for r in range(SLOTS)]
    is_new = [admitted[r] >= 0 for r in range(SLOTS)]
    eff_len = [jnp.where(is_new[r], handed_len[r], clen[r]) for r in range(SLOTS)]

    def per_slot(slot, values):
        picked = jnp.full(slot.shape, values[0], jnp.int32)
        for r in range(1, SLOTS):
            picked = jnp.where(slot == r, values[r], picked)
        return picked

    token = iota((ROWS, HD), 0)
    places = per_slot(token & (SLOTS - 1), eff_len) + (token >> 2)
    first, second = rotation(places, freq)
    dq_first, dq_second = gained(first, second, q_gain)
    dk_first, dk_second = gained(first, second, k_gain)

    landed(x_v.at[LP : 2 * LP], x_sem.at[2])
    load_dec.wait()
    x_v[2 * LP : 2 * LP + ROWS, :] = jnp.concatenate(
        [dec_v[t].astype(F32) for t in range(STEPS)], axis=0
    ).astype(BF16)
    def hand(i, way):
        other = lax.rem(me + i, NS)
        return remote(
            give_v.at[rows(other * 16, 16)],
            hand_v.at[rows(way * 16, 16)],
            seq_ss.at[0],
            seq_rs.at[0],
            seq=other,
        )

    def hand_over():
        for p in range(2):
            keys_values(1, p, p * HALF)
        new = f_v[0, LP : LP + ROWS, :]
        dkv_v[...] = jnp.zeros_like(dkv_v)
        dkv_v[0:ROWS, 0:HD] = normrot(new[:, 0:HD], dk_first, dk_second).astype(BF16)
        dkv_v[0:ROWS, HD : 2 * HD] = new[:, HD : 2 * HD].astype(BF16)
        place = iota((2 * LP, 2 * LP), 0)
        source = (((place >> 3) & 1) << 8) + ((place & 7) << 5) + (place >> 4)
        pick = jnp.where(source == iota((2 * LP, 2 * LP), 1), 1.0, 0.0).astype(BF16)
        give_v[...] = dot(pick, kv_v[...]).astype(BF16)
        hand_v[rows(me * 16, 16), :] = give_v[rows(me * 16, 16), :]

        def hand_start(i, carry):
            hand(i, me).start()
            return carry

        pl.semaphore_wait(row_sem, NX - 1)
        lax.fori_loop(1, NS, hand_start, 0)

    multiply_second(hand_over)
    landed(wo_v.at[1], wo_sem.at[3])
    def mixed_right(i):
        send(0, ((1, 2),), i // 2, lax.rem(i, 2), 0)

    def mixed_left(i):
        send(1, ((3, 5),), i // 2, lax.rem(i, 2), 1)

    def mixed_rows(half, k, slot, far, start):
        some = pl.ds(start, HALF // 2)
        mine = pa_v[half, some, :]
        value = jnp.concatenate([dot(mine, wo_v[k, b]) for b in range(2)], axis=1)
        value = value + part_r[far, 0, some, :].astype(F32)
        part_s[slot, 0, some, :] = value.astype(BF16)
        remote(
            part_s.at[slot, 0, some],
            part_r.at[slot, 0, some],
            part_ss.at[0],
            part_rs.at[arrival(slot, 0)],
            head=right if slot == 2 else left,
        ).start()

    second_half(0)
    arrived(0, 0, 1)
    mixed_rows(0, 1, 2, 0, 0)
    load_cache.wait()

    landed(hand_v.at[0 : (NS - 1) * 16], seq_rs.at[0])
    save_hand = pltpu.make_async_copy(hand_v, handed, out_sem.at[0])
    save_hand.start()

    heads = GROUP * ROWS
    queries = dq_v[0:heads]

    def pieces():
        for r in range(SLOTS):
            slot = iota((heads, CACHE), 0) & (SLOTS - 1)
            at = (iota((heads, CACHE), 1) << 5) + me
            limit = jnp.where(is_new[r], 0, clen[r])
            yield (
                dot_nt(queries, cache_v[r * CACHE : (r + 1) * CACHE, 0:HD]),
                (slot == r) & (at < limit),
                cache_v[r * CACHE : (r + 1) * CACHE, HD : 2 * HD],
            )
        slot = iota((heads, 2 * LP), 0) & (SLOTS - 1)
        column = iota((heads, 2 * LP), 1)
        prompt = column >> 3
        at = ((column & 7) << 5) + me
        yield (
            dot_nt(queries, hand_v[:, 0:HD]),
            (prompt == per_slot(slot, admitted)) & (at < per_slot(slot, handed_len)),
            hand_v[:, HD : 2 * HD],
        )
        row = iota((heads, HD), 0)
        column = iota((heads, HD), 1) + jnp.where(me == 0, 0, ROWS)
        yield (
            dot_nt(queries, dkv_v[:, 0:HD]),
            ((row & 3) == (column & 3)) & ((column >> 2) <= ((row >> 2) & 3)) & (column < ROWS),
            dkv_v[:, HD : 2 * HD],
        )

    parts = [(jnp.where(mask, s, NEG), mask, v) for s, mask, v in pieces()]
    top = functools.reduce(jnp.maximum, [jnp.max(s, axis=-1, keepdims=True) for s, _, _ in parts])
    total = jnp.zeros((heads, 1), F32)
    acc = jnp.zeros((heads, HD), F32)
    for s, mask, v in parts:
        expo = jnp.where(mask, jnp.exp2((s - top) * (SCALE * LOG2E)), 0.0)
        total = total + jnp.sum(expo, axis=-1, keepdims=True)
        acc = acc + dot(expo.astype(BF16), v)
    state = jnp.where(iota((heads, HD), 1) < HD // 2, top, total)
    for head in range(GROUP):
        at = pl.ds(8 * (head // 4) + head % 4, ROWS, stride=16)
        soft_s[at, :] = acc[head * ROWS : (head + 1) * ROWS, :]
        also = pl.ds(8 * (head // 4) + head % 4 + 4, ROWS, stride=16)
        soft_s[also, :] = state[head * ROWS : (head + 1) * ROWS, :]
    soft_r[rows(me * 8, 8), :] = soft_s[rows(me * 8, 8), :]

    def soft(i, way):
        other = lax.rem(me + i, NS)
        return remote(
            soft_s.at[rows(other * 8, 8)],
            soft_r.at[rows(way * 8, 8)],
            seq_ss.at[1],
            seq_rs.at[1],
            seq=other,
        )

    def soft_start(i, carry):
        soft(i, me).start()
        return carry

    lax.fori_loop(1, NS, soft_start, 0)
    second_half(1)

    landed(wo_v.at[0], wo_sem.at[2])

    def own(i, carry):
        for half in range(2):
            own_v[half, i] = project(half, 0, i // 2, lax.rem(i, 2))
        return carry

    lax.fori_loop(0, 4, own, 0)

    arrived(1, 0, 1)
    mixed_rows(1, 3, 5, 1, 0)

    landed(soft_r.at[0 : (NS - 1) * 8], seq_rs.at[1])
    joined = []
    for q in range(heads // NS):
        sums = soft_r[pl.ds(q, NS, stride=8), :]
        both = soft_r[pl.ds(q + 4, NS, stride=8), :]
        tops = both[:, 0:1]
        weight = jnp.exp2((tops - jnp.max(tops, axis=0, keepdims=True)) * (SCALE * LOG2E))
        whole = jnp.sum(weight * both[:, HD // 2 : HD // 2 + 1], axis=0, keepdims=True)
        joined.append((jnp.sum(weight * sums, axis=0, keepdims=True) / whole).astype(BF16))
    token_row = jnp.broadcast_to(jnp.concatenate(joined, axis=1).astype(F32), (16, WIDTH // 2))
    token_row = token_row.astype(BF16)

    core = lax.rem(me, 2)

    def dpart(k, e):
        return remote(
            dpart_s.at[2 * k + e],
            dpart_r.at[2 * k + e],
            dpart_ss.at[0],
            dpart_rs.at[0],
            head=lax.rem(y + k, NH),
            seq=me + e * (1 - 2 * core),
        )

    for k in (2, 1, 3, 0):
        for e in range(2):
            side = core + e * (1 - 2 * core)
            for b in range(2):
                tile = wo_v[k, 2 * side + b, rows(core * (WIDTH // 2), WIDTH // 2), :]
                value = dot(token_row, tile)[0:1]
                for lanes in range(2):
                    one = value[:, lanes * HD : (lanes + 1) * HD]
                    row = 2 * b + lanes
                    dpart_s[2 * k + e, row : row + 1, :] = one
                    dpart_s[2 * k + e, row + 4 : row + 5, :] = one
            if (k, e) != (0, 0):
                dpart(k, e).start()

    def right_tile(i, carry):
        mixed_right(i)
        return carry

    mixed_rows(0, 1, 2, 0, HALF // 2)
    mixed_rows(1, 3, 5, 1, HALF // 2)
    arrived(0, 1, 4)
    lax.fori_loop(1, 4, right_tile, 0)
    arrived(1, 1, 3)
    for i in (1, 2):
        mixed_left(i)
    arrived(1, 3, 4)
    mixed_left(3)

    landed(dpart_r.at[1 : 2 * NH], dpart_rs.at[0])
    total = dpart_s[0]
    for n in range(1, 2 * NH):
        total = total + dpart_r[n]
    join_s[...] = total
    join_r[rows(me * 8, 8), :] = total

    def join(i, way):
        other = lax.rem(me + i, NS)
        return remote(join_s, join_r.at[rows(way * 8, 8)], seq_ss.at[2], seq_rs.at[2], seq=other)

    def join_start(i, carry):
        join(i, me).start()
        return carry

    lax.fori_loop(1, NS, join_start, 0)

    landed(hand_v.at[0 : (NS - 1) * 16], seq_ss.at[0])
    landed(soft_r.at[0 : (NS - 1) * 8], seq_ss.at[1])
    save_hand.wait()

    arrived(3, 0, 4)
    arrived(4, 0, 4)

    def early(i, carry):
        own_v[0, i] = own_v[0, i] + part_r[4, i].astype(F32)
        own_v[1, i] = own_v[1, i] + part_r[3, i].astype(F32)
        return carry

    lax.fori_loop(0, 4, early, 0)

    def finish(i, carry):
        p, jj = i // 2, lax.rem(i, 2)
        for half in range(2):
            value = own_v[half, i] + part_r[5 if half else 2, i].astype(F32)
            at = pl.ds(half * HALF, HALF)
            out[p, at, rows(jj * WIDE, WIDE)] = value.astype(BF16)
        return carry

    def save_decoded():
        landed(join_r.at[0 : (NS - 1) * 8], seq_rs.at[2])
        for b in range(GROUP):
            mine = join_r[pl.ds(8 * (b // 4) + b % 4, ROWS, stride=16), :]
            for t in range(STEPS):
                one = mine[t * SLOTS : (t + 1) * SLOTS, :]
                dec_out[t, :, b * HD : (b + 1) * HD] = one.astype(BF16)

    arrived(2, 0, 3)
    arrived(5, 0, 3)
    lax.fori_loop(0, 3, finish, 0)
    save_decoded()
    arrived(2, 3, 4)
    arrived(5, 3, 4)
    finish(3, 0)

    landed(dpart_s.at[1 : 2 * NH], dpart_ss.at[0])
    landed(join_r.at[0 : (NS - 1) * 8], seq_ss.at[2])
    landed(part_s, part_ss.at[0])


def store(out_v, hand_v, dec_v, out, handed, dec_out, sem):
    copies = [
        pltpu.make_async_copy(source, target, sem.at[i])
        for i, (source, target) in enumerate([(out_v, out), (hand_v, handed), (dec_v, dec_out)])
    ]
    for copy in copies:
        copy.start()
    for copy in copies:
        copy.wait()


def local(
    prompts,
    prompt_len,
    admitted,
    cache_len,
    cache_kv,
    dec_tokens,
    w_query,
    w_key,
    w_value,
    w_out,
    q_gain,
    k_gain,
):
    half = HD // 2
    one = (THETA ** (-np.arange(half, dtype=np.float64) / half)).astype(np.float32)
    freq = jnp.asarray(np.concatenate([one, one])[None, :])
    hbm = pl.BlockSpec(memory_space=pl.ANY)
    vmem = pl.BlockSpec(memory_space=pltpu.VMEM)
    dma = pltpu.SemaphoreType.DMA
    shapes = [(2, LP, WIDTH), (2 * LP, 2 * HD), (STEPS, SLOTS, WIDTH)]
    results = pl.pallas_call(
        kernel,
        out_shape=[pltpu.VMEM(shape, BF16) for shape in shapes],
        in_specs=[hbm] * 13,
        out_specs=[vmem, hbm, vmem],
        scratch_shapes=[
            pltpu.SMEM((2 * NS,), jnp.int32),
            pltpu.SMEM((SLOTS,), jnp.int32),
            pltpu.SMEM((SLOTS,), jnp.int32),
            pltpu.VMEM((3, 1, HD), F32),
            pltpu.VMEM((2 * LP + ROWS, D), BF16),
            pltpu.VMEM((STEPS, SLOTS, D), BF16),
            pltpu.VMEM((1 + NT, D, TILE), BF16),
            pltpu.VMEM((NH, NT, WIDTH, TILE), BF16),
            pltpu.VMEM((SLOTS * CACHE, 2 * HD), BF16),
            pltpu.VMEM((2, 4, HALF, HD), F32),
            pltpu.VMEM((2 + NT, LP + ROWS, TILE), F32),
            pltpu.VMEM((2 * LP, 2 * HD), BF16),
            pltpu.VMEM((2 * LP, 2 * HD), BF16),
            pltpu.VMEM((2 * LP, 2 * HD), BF16),
            pltpu.VMEM((2, (GROUP + 4) * HALF, HD), BF16),
            pltpu.VMEM(((GROUP + 4) * ROWS, HD), BF16),
            pltpu.VMEM((HD, 2 * HD), BF16),
            pltpu.VMEM((2, LP, WIDTH), BF16),
            pltpu.VMEM((6, 4, HALF, WIDE), BF16),
            pltpu.VMEM((6, 4, HALF, WIDE), BF16),
            pltpu.VMEM((2, 4, HALF, WIDE), F32),
            pltpu.VMEM((NS * 8, HD), F32),
            pltpu.VMEM((NS * 8, HD), F32),
            pltpu.VMEM((8, HD), F32),
            pltpu.VMEM((NS * 8, HD), F32),
            pltpu.VMEM((2 * NH, 8, HD), F32),
            pltpu.VMEM((2 * NH, 8, HD), F32),
            dma((4,)),
            dma((3,)),
            dma((2,)),
            dma((1 + NT,)),
            dma((4,)),
            dma((1,)),
            dma((1,)),
            dma((11,)),
            dma((3,)),
            dma((3,)),
            dma((1,)),
            dma((1,)),
            pltpu.SemaphoreType.REGULAR,
        ],
        compiler_params=pltpu.CompilerParams(
            collective_id=0, has_side_effects=True, vmem_limit_bytes=56 * 2**20
        ),
        cost_estimate=pl.CostEstimate(
            flops=10_500_000_000, bytes_accessed=25_000_000, transcendentals=2_000_000
        ),
    )(
        prompt_len,
        admitted,
        cache_len,
        freq,
        q_gain[None, :],
        k_gain[None, :],
        prompts.reshape(2 * LP, D),
        dec_tokens,
        w_query,
        w_key,
        w_value,
        w_out,
        cache_kv.reshape(SLOTS * CACHE, 2 * HD),
    )
    out, handed, decoded = pl.pallas_call(
        store,
        out_shape=[jax.ShapeDtypeStruct(shape, BF16) for shape in shapes],
        in_specs=[hbm] * 3,
        out_specs=[hbm] * 3,
        scratch_shapes=[dma((3,))],
        compiler_params=pltpu.CompilerParams(vmem_limit_bytes=2**20),
    )(*results)
    return (
        out,
        handed.reshape(1, 2 * NS, EACH, 2 * HD),
        decoded,
    )


def solution(mesh):
    placed = (
        P("seq", None, None),
        P(),
        P(),
        P(),
        P("head", None, "seq", None),
        P(),
        P(None, "head"),
        P(None, "head"),
        P(None, "head"),
        P("head", None),
        P(),
        P(),
    )
    return jax.shard_map(
        local,
        mesh=mesh,
        in_specs=placed,
        out_specs=(P("seq", None, "head"), P("head", None, "seq", None), P(None, None, "head")),
        check_vma=False,
    )
```

```python
import functools

import jax
import jax.numpy as jnp
import numpy as np
from jax import lax
from jax.experimental import pallas as pl
from jax.experimental.pallas import tpu as pltpu
from jax.sharding import PartitionSpec as P

D = 4096
HD = 128
GROUP = 8
WIDTH = GROUP * HD
LP = 256
HALF = LP // 2
SLOTS = 4
STEPS = 4
ROWS = SLOTS * STEPS
CACHE = 512
NS = 32
NH = 4
NX = 4
PER_X = NS // NX
EACH = LP // NS
EPS = 1e-06
THETA = 1000000.0
NEG = -1e30
SCALE = HD ** (-0.5)
LOG2E = 1.4426950408889634
TILE = 256
NT = WIDTH // TILE
WIDE = 2 * TILE
F32 = jnp.float32
BF16 = jnp.bfloat16


def dot(a, b):
    return jnp.dot(a, b, preferred_element_type=F32)


def dot_nt(a, b):
    return lax.dot_general(a, b, (((1,), (1,)), ((), ())), preferred_element_type=F32)


def iota(shape, dim):
    return lax.broadcasted_iota(jnp.int32, shape, dim)


def rotation(positions, freq):
    angle = positions.astype(F32) * freq
    sign = jnp.where(iota((1, HD), 1) < HD // 2, -1.0, 1.0)
    return jnp.cos(angle), jnp.sin(angle) * sign


def gained(cosine, sine, gain):
    return cosine * gain, sine * pltpu.roll(gain, HD // 2, 1)


def normrot(a, first, second):
    inverse = lax.rsqrt(jnp.mean(a * a, axis=-1, keepdims=True) + EPS)
    return (a * first + pltpu.roll(a, HD // 2, 1) * second) * inverse


def kernel(
    plen_ref,
    adm_ref,
    clen_ref,
    freq_ref,
    qg_ref,
    kg_ref,
    prompts,
    dec,
    wq,
    wk,
    wv,
    wo,
    cache,
    out,
    handed,
    dec_out,
    plen,
    adm,
    clen,
    row_v,
    x_v,
    dec_v,
    w_v,
    wo_v,
    cache_v,
    tab_v,
    f_v,
    kv_v,
    give_v,
    hand_v,
    mask_v,
    turned_v,
    q_v,
    dq_v,
    dkv_v,
    pa_v,
    part_s,
    part_r,
    own_v,
    soft_s,
    soft_r,
    join_s,
    join_r,
    dpart_s,
    dpart_r,
    small_sem,
    x_sem,
    in_sem,
    w_sem,
    wo_sem,
    out_sem,
    part_ss,
    part_rs,
    seq_ss,
    seq_rs,
    dpart_ss,
    dpart_rs,
    row_sem,
):
    y = lax.axis_index("head")
    me = lax.axis_index("seq")
    right = lax.rem(y + 1, NH)
    left = lax.rem(y + NH - 1, NH)

    def remote(src, dst, send, recv, **where):
        return pltpu.make_async_remote_copy(
            src_ref=src,
            dst_ref=dst,
            send_sem=send,
            recv_sem=recv,
            device_id=where,
            device_id_type=pl.DeviceIdType.MESH,
        )

    def landed(ref, sem):
        pltpu.make_async_copy(ref, ref, sem).wait()

    def rows(start, size):
        return pl.ds(pl.multiple_of(start, size), size)

    def load_x(half, p):
        source = p * LP + half * HALF
        target = half * LP + p * HALF
        return pltpu.make_async_copy(
            prompts.at[source : source + HALF], x_v.at[target : target + HALF], x_sem.at[half + (p if half == 0 else 1)]
        )

    small = [
        pltpu.make_async_copy(ref, to, small_sem.at[i])
        for ref, to, i in (
            (freq_ref, row_v.at[0], 0),
            (qg_ref, row_v.at[1], 0),
            (kg_ref, row_v.at[2], 0),
            (plen_ref, plen, 1),
            (adm_ref, adm, 2),
            (clen_ref, clen, 3),
        )
    ]
    load_k = pltpu.make_async_copy(wk, w_v.at[0, :, 0:HD], w_sem.at[0])
    load_v = pltpu.make_async_copy(wv, w_v.at[0, :, HD : 2 * HD], w_sem.at[0])
    load_dec = pltpu.make_async_copy(dec, dec_v, in_sem.at[0])
    load_cache = pltpu.make_async_copy(cache, cache_v, in_sem.at[1])

    def load_q(t):
        return pltpu.make_async_copy(wq.at[:, rows((t - 1) * TILE, TILE)], w_v.at[t], w_sem.at[t])

    def load_o(k, j):
        start = lax.rem(y + k, NH) * WIDTH + j * TILE
        sem = wo_sem.at[j // 2 if k in (2, 3) else 2 + k]
        return pltpu.make_async_copy(wo.at[:, rows(start, TILE)], wo_v.at[k, j], sem)

    load_k.start()
    load_x(0, 0).start()
    load_v.start()
    for load in small:
        load.start()
    load_q(1).start()

    barrier = pltpu.get_barrier_semaphore()

    def signal(sem, **where):
        pl.semaphore_signal(sem, inc=1, device_id=where, device_id_type=pl.DeviceIdType.MESH)

    def signal_x(sem):
        for i in range(1, NX):
            signal(sem, seq=lax.rem(me + i * PER_X, NS))

    for k in range(1, NH):
        signal(barrier, head=lax.rem(y + k, NH))
    signal_x(barrier)
    for i in range(1, PER_X):
        signal(barrier, seq=me - lax.rem(me, PER_X) + lax.rem(me + i, PER_X))

    load_q(2).start()

    landed(row_v, small_sem.at[0])
    for load in small[3:]:
        load.wait()
    freq, q_gain, k_gain = row_v[0], row_v[1], row_v[2]
    for half in range(2):
        first, second = rotation(iota((HALF, HD), 0) + half * HALF, freq)
        tab_v[half, 0], tab_v[half, 1] = gained(first, second, q_gain)
        tab_v[half, 2], tab_v[half, 3] = gained(first, second, k_gain)
    load_q(3).start()

    def finish_query(half, p, t, base):
        slot = lax.rem(t + 5, 6)
        for b in range(TILE // HD):
            mine = f_v[t, base : base + HALF, b * HD : (b + 1) * HD]
            one = normrot(mine, tab_v[half, 0], tab_v[half, 1])
            q_v[p, rows(slot * TILE + b * HD, HD), :] = one.astype(BF16)

    def finish_token(t):
        slot = lax.rem(t + 5, 6)
        for b in range(TILE // HD):
            mine = f_v[t, LP : LP + ROWS, b * HD : (b + 1) * HD]
            one = normrot(mine, dq_first, dq_second)
            dq_v[rows((slot * 2 + b) * ROWS, ROWS), :] = one.astype(BF16)

    def keys_values(half, p, base):
        mine = f_v[0, base : base + HALF, :]
        to = rows(p * LP + half * HALF, HALF)
        kv_v[to, 0:HD] = normrot(mine[:, 0:HD], tab_v[half, 2], tab_v[half, 3]).astype(BF16)
        kv_v[to, HD : 2 * HD] = mine[:, HD : 2 * HD].astype(BF16)

    def bias_of(half, p):
        keys = (half + 1) * HALF
        at = iota((keys, HALF), 0)
        causal = at <= iota((keys, HALF), 1) + half * HALF
        return jnp.where(causal & (at < plen[2 * me + p]), 0.0, NEG)

    def turned(half, p):
        mine = pl.ds(pl.multiple_of(p * LP, LP), (half + 1) * HALF)
        return kv_v[mine, HD : 2 * HD].astype(F32).T.astype(BF16)

    def multiply_first(p):
        def tile(t, carry):
            @pl.when(p == 0)
            def _():
                landed(w_v.at[t], w_sem.at[t])

                @pl.when(t == 0)
                def _():
                    load_q(4).start()

                for jj in range(2):

                    @pl.when(t == 1 + jj)
                    def _(jj=jj):
                        for j in (2 * jj, 2 * jj + 1):
                            load_o(2, j).start()
                            load_o(3, j).start()

                @pl.when(t == 2)
                def _():
                    load_x(0, 1).start()

            @pl.when(t == 2)
            def _():
                keys_values(0, p, 0)

            @pl.when(t == 3)
            def _():
                mask_v[...] = bias_of(0, p)
                turned_v[...] = turned(0, p)

            finish_query(0, p, lax.rem(t + 5, 6), 0)
            f_v[t, 0:HALF, :] = dot(x_v[rows(p * HALF, HALF), :], w_v[t])
            return carry

        lax.fori_loop(0, 1 + NT, tile, 0)
        finish_query(0, p, NT, 0)

    def multiply_second(after_keys):
        def finish(t):
            for p in range(2):
                finish_query(1, p, t, p * HALF)
            finish_token(t)

        def tile(t, carry):
            pl.when(t == 1)(after_keys)
            finish(lax.rem(t + 5, 6))
            f_v[t] = dot(x_v[LP : 2 * LP + ROWS, :], w_v[t])
            return carry

        lax.fori_loop(0, 1 + NT, tile, 0)
        finish(NT)

    def attend(half, p):
        keys = (half + 1) * HALF
        mine = rows(p * LP, keys) if half else pl.ds(pl.multiple_of(p * LP, LP), keys)
        bias = bias_of(1, p) if half else mask_v[...]
        scores = dot_nt(kv_v[mine, 0:HD], q_v[p, 0 : GROUP * HALF])
        scores = scores + jnp.concatenate([bias] * GROUP, axis=1)
        top = jnp.max(scores, axis=0, keepdims=True)
        expo = jnp.exp2((scores - top) * (SCALE * LOG2E))
        weights = expo * (1.0 / jnp.sum(expo, axis=0, keepdims=True))
        values = turned(1, p) if half else turned_v[...]
        mixed = dot(values, weights.astype(BF16))
        for head in range(GROUP):
            one = mixed[:, head * HALF : (head + 1) * HALF].T.astype(BF16)
            pa_v[half, rows(p * HALF, HALF), head * HD : (head + 1) * HD] = one

    def arrival(slot, i):
        return {
            0: (i + 2) // 3,
            1: 2 + (i + 1) // 2,
            2: 5 + i // 3,
            5: 7 + i // 3,
            3: 9,
            4: 10,
        }[slot]

    def arrived(slot, first, last):
        landed(part_r.at[slot, first:last], part_rs.at[arrival(slot, first)])

    def part(slot, i):
        to = right if slot in (0, 2, 3) else left
        return remote(
            part_s.at[slot, i],
            part_r.at[slot, i],
            part_ss.at[0],
            part_rs.at[arrival(slot, i)],
            head=to,
        )

    def project(half, k, p, jj):
        mine = pa_v[half, rows(p * HALF, HALF), :]
        return jnp.concatenate([dot(mine, wo_v[k, 2 * jj + b]) for b in range(2)], axis=1)

    def send(half, targets, p, jj, far=None):
        i = p * 2 + jj
        values = [project(half, k, p, jj) for k, slot in targets]
        for (k, slot), value in zip(targets, values):
            if far is not None:
                value = value + part_r[far, i].astype(F32)
            part_s[slot, i] = value.astype(BF16)
            part(slot, i).start()

    def first_half(p, carry):
        @pl.when(p == 1)
        def _():
            landed(x_v.at[HALF:LP], x_sem.at[1])

        multiply_first(p)
        attend(0, p)

        def tile(jj, carry):
            @pl.when(p == 0)
            def _():
                landed(wo_v.at[2:4, pl.ds(2 * jj, 2)], wo_sem.at[jj])

                @pl.when(jj == 0)
                def _():
                    pl.semaphore_wait(barrier, NH - 1 + NX - 1 + PER_X - 1)

            send(0, ((2, 0), (3, 4)), p, jj)
            return carry

        lax.fori_loop(0, 2, tile, 0)

        @pl.when(p == 0)
        def _():
            signal_x(row_sem)
            load_dec.start()
            load_x(1, 0).start()
            load_x(1, 1).start()
            for k in (1, 0):
                for j in range(NT):
                    load_o(k, j).start()
            load_cache.start()

        return carry

    def second_half(p):
        attend(1, p)

        def tile(jj, carry):
            send(1, ((1, 3), (2, 1)), p, jj)
            return carry

        lax.fori_loop(0, 2, tile, 0)

    landed(x_v.at[0:HALF], x_sem.at[0])
    lax.fori_loop(0, 2, first_half, 0)

    admitted = [adm[r] for r in range(SLOTS)]
    handed_len = [plen[jnp.maximum(admitted[r], 0)] for r in range(SLOTS)]
    is_new = [admitted[r] >= 0 for r in range(SLOTS)]
    eff_len = [jnp.where(is_new[r], handed_len[r], clen[r]) for r in range(SLOTS)]

    def per_slot(slot, values):
        picked = jnp.full(slot.shape, values[0], jnp.int32)
        for r in range(1, SLOTS):
            picked = jnp.where(slot == r, values[r], picked)
        return picked

    token = iota((ROWS, HD), 0)
    places = per_slot(token & (SLOTS - 1), eff_len) + (token >> 2)
    first, second = rotation(places, freq)
    dq_first, dq_second = gained(first, second, q_gain)
    dk_first, dk_second = gained(first, second, k_gain)

    landed(x_v.at[LP : 2 * LP], x_sem.at[2])
    load_dec.wait()
    x_v[2 * LP : 2 * LP + ROWS, :] = jnp.concatenate(
        [dec_v[t].astype(F32) for t in range(STEPS)], axis=0
    ).astype(BF16)
    def hand(i, way):
        other = lax.rem(me + i, NS)
        return remote(
            give_v.at[rows(other * 16, 16)],
            hand_v.at[rows(way * 16, 16)],
            seq_ss.at[0],
            seq_rs.at[0],
            seq=other,
        )

    def hand_over():
        for p in range(2):
            keys_values(1, p, p * HALF)
        new = f_v[0, LP : LP + ROWS, :]
        dkv_v[...] = jnp.zeros_like(dkv_v)
        dkv_v[0:ROWS, 0:HD] = normrot(new[:, 0:HD], dk_first, dk_second).astype(BF16)
        dkv_v[0:ROWS, HD : 2 * HD] = new[:, HD : 2 * HD].astype(BF16)
        place = iota((2 * LP, 2 * LP), 0)
        source = (((place >> 3) & 1) << 8) + ((place & 7) << 5) + (place >> 4)
        pick = jnp.where(source == iota((2 * LP, 2 * LP), 1), 1.0, 0.0).astype(BF16)
        give_v[...] = dot(pick, kv_v[...]).astype(BF16)
        hand_v[rows(me * 16, 16), :] = give_v[rows(me * 16, 16), :]

        def hand_start(i, carry):
            hand(i, me).start()
            return carry

        pl.semaphore_wait(row_sem, NX - 1)
        lax.fori_loop(1, NS, hand_start, 0)

    multiply_second(hand_over)
    landed(wo_v.at[1], wo_sem.at[3])
    def mixed_right(i):
        send(0, ((1, 2),), i // 2, lax.rem(i, 2), 0)

    def mixed_left(i):
        send(1, ((3, 5),), i // 2, lax.rem(i, 2), 1)

    def mixed_rows(half, k, slot, far, start):
        some = pl.ds(start, HALF // 2)
        mine = pa_v[half, some, :]
        value = jnp.concatenate([dot(mine, wo_v[k, b]) for b in range(2)], axis=1)
        value = value + part_r[far, 0, some, :].astype(F32)
        part_s[slot, 0, some, :] = value.astype(BF16)
        remote(
            part_s.at[slot, 0, some],
            part_r.at[slot, 0, some],
            part_ss.at[0],
            part_rs.at[arrival(slot, 0)],
            head=right if slot == 2 else left,
        ).start()

    second_half(0)
    arrived(0, 0, 1)
    mixed_rows(0, 1, 2, 0, 0)
    load_cache.wait()

    landed(hand_v.at[0 : (NS - 1) * 16], seq_rs.at[0])
    save_hand = pltpu.make_async_copy(hand_v, handed, out_sem.at[0])
    save_hand.start()

    heads = GROUP * ROWS
    queries = dq_v[0:heads]

    def pieces():
        for r in range(SLOTS):
            slot = iota((heads, CACHE), 0) & (SLOTS - 1)
            at = (iota((heads, CACHE), 1) << 5) + me
            limit = jnp.where(is_new[r], 0, clen[r])
            yield (
                dot_nt(queries, cache_v[r * CACHE : (r + 1) * CACHE, 0:HD]),
                (slot == r) & (at < limit),
                cache_v[r * CACHE : (r + 1) * CACHE, HD : 2 * HD],
            )
        slot = iota((heads, 2 * LP), 0) & (SLOTS - 1)
        column = iota((heads, 2 * LP), 1)
        prompt = column >> 3
        at = ((column & 7) << 5) + me
        yield (
            dot_nt(queries, hand_v[:, 0:HD]),
            (prompt == per_slot(slot, admitted)) & (at < per_slot(slot, handed_len)),
            hand_v[:, HD : 2 * HD],
        )
        row = iota((heads, HD), 0)
        column = iota((heads, HD), 1) + jnp.where(me == 0, 0, ROWS)
        yield (
            dot_nt(queries, dkv_v[:, 0:HD]),
            ((row & 3) == (column & 3)) & ((column >> 2) <= ((row >> 2) & 3)) & (column < ROWS),
            dkv_v[:, HD : 2 * HD],
        )

    parts = [(jnp.where(mask, s, NEG), mask, v) for s, mask, v in pieces()]
    top = functools.reduce(jnp.maximum, [jnp.max(s, axis=-1, keepdims=True) for s, _, _ in parts])
    total = jnp.zeros((heads, 1), F32)
    acc = jnp.zeros((heads, HD), F32)
    for s, mask, v in parts:
        expo = jnp.where(mask, jnp.exp2((s - top) * (SCALE * LOG2E)), 0.0)
        total = total + jnp.sum(expo, axis=-1, keepdims=True)
        acc = acc + dot(expo.astype(BF16), v)
    state = jnp.where(iota((heads, HD), 1) < HD // 2, top, total)
    for head in range(GROUP):
        at = pl.ds(8 * (head // 4) + head % 4, ROWS, stride=16)
        soft_s[at, :] = acc[head * ROWS : (head + 1) * ROWS, :]
        also = pl.ds(8 * (head // 4) + head % 4 + 4, ROWS, stride=16)
        soft_s[also, :] = state[head * ROWS : (head + 1) * ROWS, :]
    soft_r[rows(me * 8, 8), :] = soft_s[rows(me * 8, 8), :]

    def soft(i, way):
        other = lax.rem(me + i, NS)
        return remote(
            soft_s.at[rows(other * 8, 8)],
            soft_r.at[rows(way * 8, 8)],
            seq_ss.at[1],
            seq_rs.at[1],
            seq=other,
        )

    def soft_start(i, carry):
        soft(i, me).start()
        return carry

    lax.fori_loop(1, NS, soft_start, 0)
    second_half(1)

    landed(wo_v.at[0], wo_sem.at[2])

    def own(i, carry):
        for half in range(2):
            own_v[half, i] = project(half, 0, i // 2, lax.rem(i, 2))
        return carry

    lax.fori_loop(0, 4, own, 0)

    arrived(1, 0, 1)
    mixed_rows(1, 3, 5, 1, 0)

    landed(soft_r.at[0 : (NS - 1) * 8], seq_rs.at[1])
    joined = []
    for q in range(heads // NS):
        sums = soft_r[pl.ds(q, NS, stride=8), :]
        both = soft_r[pl.ds(q + 4, NS, stride=8), :]
        tops = both[:, 0:1]
        weight = jnp.exp2((tops - jnp.max(tops, axis=0, keepdims=True)) * (SCALE * LOG2E))
        whole = jnp.sum(weight * both[:, HD // 2 : HD // 2 + 1], axis=0, keepdims=True)
        joined.append((jnp.sum(weight * sums, axis=0, keepdims=True) / whole).astype(BF16))
    token_row = jnp.broadcast_to(jnp.concatenate(joined, axis=1).astype(F32), (16, WIDTH // 2))
    token_row = token_row.astype(BF16)

    core = lax.rem(me, 2)

    def dpart(k, e):
        return remote(
            dpart_s.at[2 * k + e],
            dpart_r.at[2 * k + e],
            dpart_ss.at[0],
            dpart_rs.at[0],
            head=lax.rem(y + k, NH),
            seq=me + e * (1 - 2 * core),
        )

    for k in (2, 1, 3, 0):
        for e in range(2):
            side = core + e * (1 - 2 * core)
            for b in range(2):
                tile = wo_v[k, 2 * side + b, rows(core * (WIDTH // 2), WIDTH // 2), :]
                value = dot(token_row, tile)[0:1]
                for lanes in range(2):
                    one = value[:, lanes * HD : (lanes + 1) * HD]
                    row = 2 * b + lanes
                    dpart_s[2 * k + e, row : row + 1, :] = one
                    dpart_s[2 * k + e, row + 4 : row + 5, :] = one
            if (k, e) != (0, 0):
                dpart(k, e).start()

    def right_tile(i, carry):
        mixed_right(i)
        return carry

    mixed_rows(0, 1, 2, 0, HALF // 2)
    mixed_rows(1, 3, 5, 1, HALF // 2)
    arrived(0, 1, 4)
    lax.fori_loop(1, 4, right_tile, 0)
    arrived(1, 1, 3)
    for i in (1, 2):
        mixed_left(i)
    arrived(1, 3, 4)
    mixed_left(3)

    landed(dpart_r.at[1 : 2 * NH], dpart_rs.at[0])
    total = dpart_s[0]
    for n in range(1, 2 * NH):
        total = total + dpart_r[n]
    join_s[...] = total
    join_r[rows(me * 8, 8), :] = total

    def join(i, way):
        other = lax.rem(me + i, NS)
        return remote(join_s, join_r.at[rows(way * 8, 8)], seq_ss.at[2], seq_rs.at[2], seq=other)

    def join_start(i, carry):
        join(i, me).start()
        return carry

    lax.fori_loop(1, NS, join_start, 0)

    landed(hand_v.at[0 : (NS - 1) * 16], seq_ss.at[0])
    landed(soft_r.at[0 : (NS - 1) * 8], seq_ss.at[1])
    save_hand.wait()

    arrived(3, 0, 4)
    arrived(4, 0, 4)

    def early(i, carry):
        own_v[0, i] = own_v[0, i] + part_r[4, i].astype(F32)
        own_v[1, i] = own_v[1, i] + part_r[3, i].astype(F32)
        return carry

    lax.fori_loop(0, 4, early, 0)

    def finish(i, carry):
        p, jj = i // 2, lax.rem(i, 2)
        for half in range(2):
            value = own_v[half, i] + part_r[5 if half else 2, i].astype(F32)
            at = pl.ds(half * HALF, HALF)
            out[p, at, rows(jj * WIDE, WIDE)] = value.astype(BF16)
        return carry

    def save_decoded():
        landed(join_r.at[0 : (NS - 1) * 8], seq_rs.at[2])
        for b in range(GROUP):
            mine = join_r[pl.ds(8 * (b // 4) + b % 4, ROWS, stride=16), :]
            for t in range(STEPS):
                one = mine[t * SLOTS : (t + 1) * SLOTS, :]
                dec_out[t, :, b * HD : (b + 1) * HD] = one.astype(BF16)

    arrived(2, 0, 3)
    arrived(5, 0, 3)
    lax.fori_loop(0, 3, finish, 0)
    save_decoded()
    arrived(2, 3, 4)
    arrived(5, 3, 4)
    finish(3, 0)

    landed(dpart_s.at[1 : 2 * NH], dpart_ss.at[0])
    landed(join_r.at[0 : (NS - 1) * 8], seq_ss.at[2])
    landed(part_s, part_ss.at[0])


def store(out_v, hand_v, dec_v, out, handed, dec_out, sem):
    copies = [
        pltpu.make_async_copy(source, target, sem.at[i])
        for i, (source, target) in enumerate([(out_v, out), (hand_v, handed), (dec_v, dec_out)])
    ]
    for copy in copies:
        copy.start()
    for copy in copies:
        copy.wait()


def local(
    prompts,
    prompt_len,
    admitted,
    cache_len,
    cache_kv,
    dec_tokens,
    w_query,
    w_key,
    w_value,
    w_out,
    q_gain,
    k_gain,
):
    half = HD // 2
    one = (THETA ** (-np.arange(half, dtype=np.float64) / half)).astype(np.float32)
    freq = jnp.asarray(np.concatenate([one, one])[None, :])
    hbm = pl.BlockSpec(memory_space=pl.ANY)
    vmem = pl.BlockSpec(memory_space=pltpu.VMEM)
    dma = pltpu.SemaphoreType.DMA
    shapes = [(2, LP, WIDTH), (2 * LP, 2 * HD), (STEPS, SLOTS, WIDTH)]
    results = pl.pallas_call(
        kernel,
        out_shape=[pltpu.VMEM(shape, BF16) for shape in shapes],
        in_specs=[hbm] * 13,
        out_specs=[vmem, hbm, vmem],
        scratch_shapes=[
            pltpu.SMEM((2 * NS,), jnp.int32),
            pltpu.SMEM((SLOTS,), jnp.int32),
            pltpu.SMEM((SLOTS,), jnp.int32),
            pltpu.VMEM((3, 1, HD), F32),
            pltpu.VMEM((2 * LP + ROWS, D), BF16),
            pltpu.VMEM((STEPS, SLOTS, D), BF16),
            pltpu.VMEM((1 + NT, D, TILE), BF16),
            pltpu.VMEM((NH, NT, WIDTH, TILE), BF16),
            pltpu.VMEM((SLOTS * CACHE, 2 * HD), BF16),
            pltpu.VMEM((2, 4, HALF, HD), F32),
            pltpu.VMEM((2 + NT, LP + ROWS, TILE), F32),
            pltpu.VMEM((2 * LP, 2 * HD), BF16),
            pltpu.VMEM((2 * LP, 2 * HD), BF16),
            pltpu.VMEM((2 * LP, 2 * HD), BF16),
            pltpu.VMEM((HALF, HALF), F32),
            pltpu.VMEM((HD, HALF), BF16),
            pltpu.VMEM((2, (GROUP + 4) * HALF, HD), BF16),
            pltpu.VMEM(((GROUP + 4) * ROWS, HD), BF16),
            pltpu.VMEM((HD, 2 * HD), BF16),
            pltpu.VMEM((2, LP, WIDTH), BF16),
            pltpu.VMEM((6, 4, HALF, WIDE), BF16),
            pltpu.VMEM((6, 4, HALF, WIDE), BF16),
            pltpu.VMEM((2, 4, HALF, WIDE), F32),
            pltpu.VMEM((NS * 8, HD), F32),
            pltpu.VMEM((NS * 8, HD), F32),
            pltpu.VMEM((8, HD), F32),
            pltpu.VMEM((NS * 8, HD), F32),
            pltpu.VMEM((2 * NH, 8, HD), F32),
            pltpu.VMEM((2 * NH, 8, HD), F32),
            dma((4,)),
            dma((3,)),
            dma((2,)),
            dma((1 + NT,)),
            dma((4,)),
            dma((1,)),
            dma((1,)),
            dma((11,)),
            dma((3,)),
            dma((3,)),
            dma((1,)),
            dma((1,)),
            pltpu.SemaphoreType.REGULAR,
        ],
        compiler_params=pltpu.CompilerParams(
            collective_id=0, has_side_effects=True, vmem_limit_bytes=56 * 2**20
        ),
        cost_estimate=pl.CostEstimate(
            flops=10_500_000_000, bytes_accessed=25_000_000, transcendentals=2_000_000
        ),
    )(
        prompt_len,
        admitted,
        cache_len,
        freq,
        q_gain[None, :],
        k_gain[None, :],
        prompts.reshape(2 * LP, D),
        dec_tokens,
        w_query,
        w_key,
        w_value,
        w_out,
        cache_kv.reshape(SLOTS * CACHE, 2 * HD),
    )
    out, handed, decoded = pl.pallas_call(
        store,
        out_shape=[jax.ShapeDtypeStruct(shape, BF16) for shape in shapes],
        in_specs=[hbm] * 3,
        out_specs=[hbm] * 3,
        scratch_shapes=[dma((3,))],
        compiler_params=pltpu.CompilerParams(vmem_limit_bytes=2**20),
    )(*results)
    return (
        out,
        handed.reshape(1, 2 * NS, EACH, 2 * HD),
        decoded,
    )


def solution(mesh):
    placed = (
        P("seq", None, None),
        P(),
        P(),
        P(),
        P("head", None, "seq", None),
        P(),
        P(None, "head"),
        P(None, "head"),
        P(None, "head"),
        P("head", None),
        P(),
        P(),
    )
    return jax.shard_map(
        local,
        mesh=mesh,
        in_specs=placed,
        out_specs=(P("seq", None, "head"), P("head", None, "seq", None), P(None, None, "head")),
        check_vma=False,
    )
```
